256 devices in a mesh: gx: 16 (over z_hi, x, core), gy: 16 (over z_lo, y).
Axes of the slice: x: 4, y: 4, z: 8 (z_hi: 2, z_lo: 4; z = z_hi * 4 + z_lo), core: 2. Of those that a mesh axis runs over, the one named last changes fastest.
Arguments:
- node_feats: bfloat16 [262144, 128], P(('gx', 'gy')), may hold values from -6 to 6
- radial: bfloat16 [8, 32, 262144], P(None, None, ('gx', 'gy')), may hold values from -3 to 3
- neighbours: int32 [32, 262144], P(None, ('gx', 'gy')), may hold values from 0 to 8255, as said below
- nbr_count: int32 [262144], P(('gx', 'gy')), may hold values from 8 to 32, as said below
- domain_count: int32 [256], P(('gx', 'gy')), may hold values from 256 to 1024, as said below
- base_cells: int32 [3, 262144], P(None, ('gx', 'gy')), may hold values from 0 to 255, as said below
- spline_weights: float32 [3, 4, 262144], P(None, None, ('gx', 'gy')), as said below
- w_proj: bfloat16 [2, 128, 128], replicated, may hold values from -0.5 to 0.5
- w_radial: bfloat16 [2, 8, 128], replicated, may hold values from -2 to 2
- w_mix: bfloat16 [2, 128, 128], replicated, may hold values from -0.5 to 0.5
- w_charge: bfloat16 [128], replicated, may hold values from -0.5 to 0.5
- green_kernel: float32 [256, 256, 256], P(None, 'gx', 'gy'), may hold values from 1 to 200, as said below
Outputs:
- charges: float32 [262144], P(('gx', 'gy'))
- atom_potential: float32 [262144], P(('gx', 'gy'))
- potential_grid: float32 [256, 256, 256], P('gx', 'gy')
The draws below stay inside these ranges and needn't reach their ends.
Inputs may be any that keep to these rules, and one draw needn't show every extreme that they name: `neighbours`: an entry is r * 1024 + t (see the steps). With r = 4 (the atom's own domain, slot s), t - s lies in -128 .. 127, and t is below that domain's count if s is. Atoms of slot s < 256 may also name other domains, by the band s // 64: band 0 names r with offset -1 along gx (any offset along gy) and t from 64 to 127; band 1 names offset +1 along gx (any along gy) and t below 64; band 2 names offset (0, -1) and t from 192 to 255; band 3 names offset (0, +1) and t from 128 to 191. Other atoms name only their own domain. Slots at or past nbr_count hold entries of the same kind. `nbr_count`: slots k below the count are live. `domain_count`: the present atoms of a domain fill its first slots. `base_cells`: row 0 lies in 1 to 16, row 1 in 1 to 16, row 2 in 0 to 255. `spline_weights`: for each dimension and atom, the four cubic B-spline weights of one fraction u in [0, 1): (1-u)^3/6, (3u^3-6u^2+4)/6, (-3u^3+3u^2+3u+1)/6, u^3/6. `green_kernel`: the value at wave number k equals the value at (-k) mod 256, taken along all three dimensions.
All inputs are finite; a program needn't handle non-finite values.
Results may differ from the reference program's by a relative error of at most 0.0075.
Values may be sent and summed in bfloat16 or wider, within the bound.
A program may use at most 64 MiB of HBM per device.

```python
import math
import jax
import jax.numpy as jnp
from jax import lax

C = 128
NB = 8
K = 32
L = 2
G = 256
ATOMS_DEV = 1024
REACH = 128
SLABS = 16
COLUMNS = 16
ATOMS = 262144
CELL_X = 16
CELL_Y = 16


def domain_sizes(key):
    key = jax.random.fold_in(key, 11)
    drawn_fill = jax.random.randint(key, (SLABS * COLUMNS,), ATOMS_DEV // 4, ATOMS_DEV // 2 + 1)
    domain_ids = jnp.arange(SLABS * COLUMNS, dtype=jnp.int32)
    electrode = domain_ids // COLUMNS % (SLABS // 2) == 0
    drawn_fill = jnp.where(domain_ids == COLUMNS, ATOMS_DEV // 4, drawn_fill)
    return jnp.where(electrode, ATOMS_DEV, drawn_fill).astype(jnp.int32)


def draw_domain_count(key, part):
    return domain_sizes(key)


def draw_neighbours(key, part):
    domain_fill = domain_sizes(key)
    key = jax.random.fold_in(key, 3)
    key_out, key_side, key_far, key_near = jax.random.split(key, 4)
    band_rows = ATOMS_DEV // 16
    atom_ids = jnp.arange(ATOMS, dtype=jnp.int32)
    slot_ids = atom_ids % ATOMS_DEV
    own_count = domain_fill[atom_ids // ATOMS_DEV]
    band_index = slot_ids // band_rows
    outside = jax.random.bernoulli(key_out, 0.5, (K, ATOMS)) & (band_index < 4)[None, :]
    side_step = jax.random.randint(key_side, (K, ATOMS), -1, 2)
    step_x = jnp.where(band_index == 0, -1, jnp.where(band_index == 1, 1, 0))[None, :]
    step_y = jnp.where((band_index < 2)[None, :], side_step, jnp.where(band_index == 2, -1, 1)[None, :])
    far_base = jnp.where(band_index == 0, band_rows, jnp.where(band_index == 1, 0, jnp.where(band_index == 2, 3 * band_rows, 2 * band_rows)))
    far_slot = far_base[None, :] + jax.random.randint(key_far, (K, ATOMS), 0, band_rows)
    near_offset = jax.random.randint(key_near, (K, ATOMS), -REACH, REACH)
    near_raw = jnp.clip(slot_ids[None, :] + near_offset, 0, ATOMS_DEV - 1)
    near_slot = jnp.where((slot_ids < own_count)[None, :], jnp.minimum(near_raw, own_count[None, :] - 1), near_raw)
    direction = jnp.where(outside, (step_x + 1) * 3 + step_y + 1, 4)
    encoded = direction * ATOMS_DEV + jnp.where(outside, far_slot, near_slot)
    first_slot = jnp.arange(K, dtype=jnp.int32)[:, None] == 0
    encoded = jnp.where(first_slot & (slot_ids == 0)[None, :], band_rows, encoded)
    encoded = jnp.where(first_slot & (slot_ids == band_rows)[None, :], 8 * ATOMS_DEV + band_rows - 1, encoded)
    return encoded.astype(jnp.int32)


def draw_nbr_count(key, part):
    key = jax.random.fold_in(key, 5)
    drawn_count = jax.random.randint(key, (ATOMS,), K // 4, K + 1)
    slot_ids = jnp.arange(ATOMS, dtype=jnp.int32) % ATOMS_DEV
    drawn_count = jnp.where(slot_ids == 0, K, jnp.where(slot_ids == 1, K // 4, drawn_count))
    return drawn_count.astype(jnp.int32)


def draw_base_cells(key, part):
    key = jax.random.fold_in(key, 9)
    key_x, key_y, key_z = jax.random.split(key, 3)
    slot_ids = jnp.arange(ATOMS, dtype=jnp.int32) % ATOMS_DEV
    along_x = jax.random.randint(key_x, (ATOMS,), 1, CELL_X + 1)
    along_y = jax.random.randint(key_y, (ATOMS,), 1, CELL_Y + 1)
    along_z = jax.random.randint(key_z, (ATOMS,), 0, G)
    along_x = jnp.where(slot_ids == 0, 1, jnp.where(slot_ids == 1, CELL_X, along_x))
    along_y = jnp.where(slot_ids == 0, 1, jnp.where(slot_ids == 1, CELL_Y, along_y))
    along_z = jnp.where(slot_ids == 0, G - 1, jnp.where(slot_ids == 1, 0, along_z))
    return jnp.stack([along_x, along_y, along_z]).astype(jnp.int32)


def draw_spline_weights(key, part):
    key = jax.random.fold_in(key, 13)
    fraction = jax.random.uniform(key, (3, ATOMS), jnp.float32)
    remainder = 1.0 - fraction
    squared = fraction * fraction
    third_power = squared * fraction
    weight_zero = remainder * remainder * remainder / 6.0
    weight_one = (3.0 * third_power - 6.0 * squared + 4.0) / 6.0
    weight_two = (-3.0 * third_power + 3.0 * squared + 3.0 * fraction + 1.0) / 6.0
    weight_three = third_power / 6.0
    return jnp.stack([weight_zero, weight_one, weight_two, weight_three], axis=1).astype(jnp.float32)


def draw_green_kernel(key, part):
    key = jax.random.fold_in(key, 17)
    levels = jax.random.uniform(key, (G, G, G), jnp.float32)
    mirrored = jnp.roll(jnp.flip(levels, (0, 1, 2)), 1, axis=(0, 1, 2))
    blended = (levels + mirrored) * 0.5
    return jnp.exp(blended * math.log(200.0)).astype(jnp.float32)


def block_scale(key, dims, cuts, least, high):
    def one(axis_at, shards_of):
        steps = jax.random.uniform(jax.random.fold_in(jax.random.fold_in(key, 6), axis_at), (shards_of,), jnp.float32, least / len(cuts), high / len(cuts))
        return jnp.repeat(jnp.exp(steps), dims[axis_at] // shards_of).reshape((-1,) + (1,) * (len(dims) - axis_at - 1))

    factor_of = one(*cuts[0])
    for cut in cuts[1:]:
        factor_of = factor_of * one(*cut)
    return factor_of


def bell_draw(key, shape, width, bound, pieces=(), kind=jnp.bfloat16):
    drawn = jax.random.normal(key, shape, jnp.float32) * width
    if len(pieces) > 0:
        drawn = block_scale(key, shape, pieces, -0.22, 0.18) * drawn
    return jnp.clip(drawn, min=-bound, max=bound).astype(kind)


def setup_inputs(seed: int = 0) -> dict:
    seeds = jax.random.split(jax.random.key(seed), 13)
    node_feats = bell_draw(seeds[0], (ATOMS, C), 1.0, 6.0, ((0, 256),))
    radial = bell_draw(seeds[1], (NB, K, ATOMS), 0.5, 3.0, ((2, 256),))
    neighbours = draw_neighbours(jax.random.fold_in(seeds[12], 71), 0)
    nbr_count = draw_nbr_count(jax.random.fold_in(seeds[12], 71), 0)
    domain_count = draw_domain_count(jax.random.fold_in(seeds[12], 71), 0)
    base_cells = draw_base_cells(jax.random.fold_in(seeds[12], 71), 0)
    spline_weights = draw_spline_weights(jax.random.fold_in(seeds[12], 71), 0)
    w_proj = bell_draw(seeds[7], (L, C, C), C ** -0.5, 0.5)
    w_radial = bell_draw(seeds[8], (L, NB, C), NB ** -0.5, 2.0)
    w_mix = bell_draw(seeds[9], (L, C, C), C ** -0.5, 0.5)
    w_charge = bell_draw(seeds[10], (C,), C ** -0.5, 0.5)
    green_kernel = draw_green_kernel(jax.random.fold_in(seeds[12], 71), 0)
    return {"node_feats": node_feats, "radial": radial, "neighbours": neighbours, "nbr_count": nbr_count, "domain_count": domain_count, "base_cells": base_cells, "spline_weights": spline_weights, "w_proj": w_proj, "w_radial": w_radial, "w_mix": w_mix, "w_charge": w_charge, "green_kernel": green_kernel}


def neighbour_rows(neighbours, domain):
    direction = neighbours // ATOMS_DEV
    picked = neighbours % ATOMS_DEV
    row_x = domain // COLUMNS
    col_y = domain % COLUMNS
    target_domain = (row_x + direction // 3 - 1) % SLABS * COLUMNS + (col_y + direction % 3 - 1) % COLUMNS
    return target_domain * ATOMS_DEV + picked

def reference(node_feats, radial, neighbours, nbr_count, domain_count, base_cells, spline_weights, w_proj, w_radial, w_mix, w_charge, green_kernel):
    slot_ids = jnp.arange(ATOMS, dtype=jnp.int32)
    owner_ids = slot_ids // ATOMS_DEV
    present = slot_ids % ATOMS_DEV < domain_count[owner_ids]
    features = node_feats
    for layer_index in range(L):
        projected = jnp.dot(features, w_proj[layer_index], preferred_element_type=jnp.float32).astype(jnp.bfloat16)
        filter_weights = w_radial[layer_index].astype(jnp.float32)

        def domain_messages(domain):
            begin_row = domain * ATOMS_DEV
            part_radial = lax.dynamic_slice_in_dim(radial, begin_row, ATOMS_DEV, 2).astype(jnp.float32)
            part_nbrs = lax.dynamic_slice_in_dim(neighbours, begin_row, ATOMS_DEV, 1)
            part_count = lax.dynamic_slice_in_dim(nbr_count, begin_row, ATOMS_DEV, 0)
            gathered = projected[neighbour_rows(part_nbrs, domain)].astype(jnp.float32)
            filters = jnp.einsum('bka,bc->kac', part_radial, filter_weights)
            live_slots = jnp.arange(K, dtype=jnp.int32)[:, None] < part_count[None, :]
            summed = lax.optimization_barrier(jnp.sum(jnp.where(live_slots[:, :, None], filters * gathered, 0.0), axis=0))
            return summed * (1.0 / math.sqrt(K))
        messages = lax.map(domain_messages, jnp.arange(SLABS * COLUMNS, dtype=jnp.int32)).reshape(ATOMS, C)
        mixed_rows = jnp.dot(messages.astype(jnp.bfloat16), w_mix[layer_index], preferred_element_type=jnp.float32)
        features = (features.astype(jnp.float32) + jax.nn.silu(mixed_rows)).astype(jnp.bfloat16)
    charges = jnp.where(present, jnp.dot(features, w_charge, preferred_element_type=jnp.float32), 0.0)
    offsets = jnp.arange(4, dtype=jnp.int32)[:, None]
    row_x = owner_ids // COLUMNS
    col_y = owner_ids % COLUMNS
    cell_ix = (row_x[None, :] * CELL_X + base_cells[0][None, :] - 2 + offsets) % G
    cell_iy = (col_y[None, :] * CELL_Y + base_cells[1][None, :] - 2 + offsets) % G
    cell_iz = (base_cells[2][None, :] + offsets) % G
    spread_w = spline_weights[0][:, None, None, :] * spline_weights[1][None, :, None, :] * spline_weights[2][None, None, :, :]
    index_x = cell_ix[:, None, None, :]
    index_y = cell_iy[None, :, None, :]
    index_z = cell_iz[None, None, :, :]
    density = jnp.zeros((G, G, G), jnp.float32).at[index_x, index_y, index_z].add(spread_w * charges[None, None, None, :])
    spectrum = jnp.fft.fftn(density)
    potential = jnp.real(jnp.fft.ifftn(spectrum * green_kernel)).astype(jnp.float32)
    sampled = potential[index_x, index_y, index_z]
    atom_potential = jnp.where(present, lax.optimization_barrier(jnp.sum(spread_w * sampled, axis=(0, 1, 2))), 0.0)
    return (charges, atom_potential, potential)
```

```python
import functools
import math

import jax
import jax.numpy as jnp
from jax import lax
from jax.experimental import pallas as pl
from jax.experimental.pallas import tpu as pltpu
from jax.sharding import PartitionSpec as P

K = 32
L = 2


highest = lax.Precision.HIGHEST
MESH = pl.DeviceIdType.MESH
TN = (((0,), (0,)), ((), ()))
NT = (((1,), (1,)), ((), ()))
NN = (((1,), (0,)), ((), ()))


def dot(a, b, dims=NN):
    return lax.dot_general(a, b, dims, preferred_element_type=jnp.float32)


def ring(index, step, count):
    return lax.rem(index + step + count, count)


def message_kernel(
    num_x,
    num_y,
    feats_ref,
    radial_ref,
    nbr_ref,
    count_ref,
    fill_ref,
    proj_ref,
    filt_ref,
    mix_ref,
    charge_w_ref,
    charges_ref,
    state,
    table,
    rows_out,
    rows_in,
    head_a,
    head_b,
    pick,
    filt_k,
    total,
    send_sem,
    recv_sem,
):
    px, py = lax.axis_index("gx"), lax.axis_index("gy")
    barrier = pltpu.get_barrier_semaphore()
    peers = [(dx, dy) for dx in (-1, 0, 1) for dy in (-1, 0, 1) if (dx, dy) != (0, 0)]
    for dx, dy in peers:
        pl.semaphore_signal(
            barrier,
            inc=1,
            device_id=(ring(px, dx, num_x), ring(py, dy, num_y)),
            device_id_type=MESH,
        )
    code = nbr_ref[...]
    direction, slot = code // 1024, code % 1024
    lane = lax.broadcasted_iota(jnp.int32, (K, 1024), 1)
    live = lax.broadcasted_iota(jnp.int32, (K, 1024), 0) < count_ref[...]
    block = lane // 128
    near = slot - jnp.maximum(block - 1, 0) * 128
    far = jnp.where(
        direction < 3,
        192 + direction * 64 + slot,
        jnp.where(
            direction > 5,
            64 + direction * 64 + slot,
            jnp.where(direction == 3, 192 + slot, 320 + slot),
        ),
    )
    named = jnp.where(live, jnp.where(direction == 4, near, far), -8192).astype(jnp.float32)
    for b in range(8):
        pick[:, b, :] = named[:, b * 128 : (b + 1) * 128]

    state[...] = jnp.transpose(feats_ref[...].astype(jnp.float32))
    row_id = lax.broadcasted_iota(jnp.int32, (128, 128), 0).astype(jnp.bfloat16)
    one, zero = jnp.ones((128, 128), jnp.bfloat16), jnp.zeros((128, 128), jnp.bfloat16)
    basis_k = lax.broadcasted_iota(jnp.int32, (128, 8 * K), 1) % K

    def onehot(k, begin, groups):
        row = pick[k, begin // 128 : begin // 128 + 1, :]
        parts = [
            jnp.where(row_id == jnp.broadcast_to((row - 128.0 * g).astype(jnp.bfloat16), (128, 128)), one, zero)
            for g in range(groups)
        ]
        return jnp.concatenate(parts, axis=0)

    def messages(group, tables):
        begin = group * 256
        radial = radial_ref[:, begin : begin + 256]
        total[...] = jnp.zeros_like(total)

        def step(pair, carry):
            k = 2 * pair
            filters = dot(filt_k[pl.ds(pl.multiple_of(k * 128, 256), 256), :], radial)
            for half, (source, groups) in enumerate(tables):
                at = begin + 128 * half
                hot = jnp.concatenate([onehot(k, at, groups), onehot(k + 1, at, groups)], axis=1)
                got = dot(source(), hot)
                lanes = slice(128 * half, 128 * half + 128)
                total[:, lanes] += (
                    got[:, :128] * filters[:128, lanes] + got[:, 128:] * filters[128:, lanes]
                )
            return carry

        lax.fori_loop(0, K // 2, step, 0, unroll=2)
        return (total[...] * (1.0 / math.sqrt(K))).astype(jnp.bfloat16)

    for layer in range(L):
        spread = jnp.concatenate(
            [jnp.broadcast_to(filt_ref[layer, b], (K, 128)) for b in range(8)], axis=0
        )
        spread = jnp.transpose(spread.astype(jnp.float32))
        for k in range(K):
            filt_k[k * 128 : (k + 1) * 128, :] = jnp.where(basis_k == k, spread, 0.0).astype(jnp.bfloat16)
        proj = proj_ref[layer]
        first = dot(proj, state[:, :256].astype(jnp.bfloat16), TN).astype(jnp.bfloat16)
        rows_out[layer] = jnp.transpose(first.astype(jnp.float32)).astype(jnp.bfloat16)
        if layer == 0:
            pl.semaphore_wait(barrier, 8)
        copies = []
        for dx, dy in peers:
            if dx == 1:
                band, land = 1, 1 - dy
            elif dx == -1:
                band, land = 0, 4 - dy
            elif dy == 1:
                band, land = 3, 6
            else:
                band, land = 2, 7
            copies.append(
                pltpu.make_async_remote_copy(
                    src_ref=rows_out.at[layer, pl.ds(band * 64, 64)],
                    dst_ref=rows_in.at[layer, pl.ds(land * 64, 64)],
                    send_sem=send_sem.at[layer, land],
                    recv_sem=recv_sem.at[layer, land],
                    device_id=(ring(px, dx, num_x), ring(py, dy, num_y)),
                    device_id_type=MESH,
                )
            )
            copies[-1].start()
        table[:, :256] = first
        table[:, 256:] = dot(proj, state[:, 256:].astype(jnp.bfloat16), TN).astype(jnp.bfloat16)

        def update(group, tables):
            begin = group * 256
            u = messages(group, tables)
            mixed = dot(mix_ref[layer], u, TN)
            lanes = slice(begin, begin + 256)
            state[:, lanes] = (
                (state[:, lanes] + mixed / (1.0 + jnp.exp(-mixed))).astype(jnp.bfloat16).astype(jnp.float32)
            )

        def window(block):
            low = max(block - 1, 0) * 128
            high = min(block + 2, 8) * 128
            return (lambda: table[:, low:high]), (high - low) // 128

        for group in (1, 2, 3):
            update(group, [window(2 * group), window(2 * group + 1)])
        for copy in copies:
            copy.wait()
        far_rows = jnp.transpose(rows_in[layer].astype(jnp.float32)).astype(jnp.bfloat16)
        head_a[:, :256] = table[:, :256]
        head_a[:, 256:] = far_rows[:, :384]
        head_b[:, :384] = table[:, :384]
        head_b[:, 384:] = far_rows[:, 384:]
        update(0, [((lambda: head_a[...]), 5), ((lambda: head_b[...]), 4)])
    charge = dot(charge_w_ref[...], state[...].astype(jnp.bfloat16))[0:1]
    inside = lax.broadcasted_iota(jnp.int32, (1, 1024), 1) < fill_ref[...]
    charges_ref[...] = jnp.where(inside, charge, 0.0)


def message_passing(feats, radial, neighbours, nbr_count, fill, w_proj, w_radial, w_mix, w_charge):
    num_x, num_y = lax.axis_size("gx"), lax.axis_size("gy")
    vmem = pl.BlockSpec(memory_space=pltpu.VMEM)
    bf16 = jnp.bfloat16
    return pl.pallas_call(
        functools.partial(message_kernel, num_x, num_y),
        out_shape=jax.ShapeDtypeStruct((1, 1024), jnp.float32),
        in_specs=[vmem] * 9,
        out_specs=vmem,
        scratch_shapes=[
            pltpu.VMEM((128, 1024), jnp.float32),
            pltpu.VMEM((128, 1024), bf16),
            pltpu.VMEM((L, 256, 128), bf16),
            pltpu.VMEM((L, 512, 128), bf16),
            pltpu.VMEM((128, 640), bf16),
            pltpu.VMEM((128, 512), bf16),
            pltpu.VMEM((K, 8, 128), jnp.float32),
            pltpu.VMEM((K * 128, 8 * K), bf16),
            pltpu.VMEM((128, 256), jnp.float32),
            pltpu.SemaphoreType.DMA((L, 8)),
            pltpu.SemaphoreType.DMA((L, 8)),
        ],
        compiler_params=pltpu.CompilerParams(
            collective_id=0, has_side_effects=True, vmem_limit_bytes=48 * 1024 * 1024
        ),
        name="message_passing",
    )(
        feats,
        radial.reshape(8 * K, 1024),
        neighbours,
        nbr_count.reshape(1, 1024),
        jnp.broadcast_to(fill.reshape(1, 1), (1, 1024)),
        w_proj,
        w_radial.reshape(L, 8, 1, 128),
        w_mix,
        jnp.broadcast_to(w_charge.reshape(1, 128), (8, 128)),
    )


def extended(block, sides, width):
    for axis, dim in sides:
        count = lax.axis_size(axis)
        forward = [(i, i + 1) for i in range(count - 1)]
        forward.append((count - 1, 0))
        backward = [(target, source) for source, target in forward]
        low = lax.ppermute(
            lax.slice_in_dim(block, block.shape[dim] - width, None, axis=dim), axis, forward
        )
        high = lax.ppermute(lax.slice_in_dim(block, 0, width, axis=dim), axis, backward)
        block = jnp.concatenate([low, block, high], axis=dim)
    return block


def spline_profile(base_row, weights, length, cyclic):
    cell_ids = jnp.arange(length, dtype=jnp.int32)[:, None]
    profile = jnp.zeros((length, base_row.shape[0]), jnp.float32)
    for offset in range(4):
        target = base_row[None, :] + offset
        if cyclic:
            target = target % length
        profile = profile + jnp.where(cell_ids == target, weights[offset][None, :], 0.0)
    return profile


def widen(values):
    return extended(values, (("gx", 0), ("gy", 1)), 2)


def fold_axis(padded, axis_index, inner_len):
    middle = lax.slice_in_dim(padded, 4, inner_len + 4, axis=axis_index)
    low_rows = lax.slice_in_dim(padded, 0, 2, axis=axis_index)
    high_rows = lax.slice_in_dim(padded, inner_len + 6, inner_len + 8, axis=axis_index)
    low_pad = [(0, 0)] * padded.ndim
    low_pad[axis_index] = (0, inner_len - 2)
    high_pad = [(0, 0)] * padded.ndim
    high_pad[axis_index] = (inner_len - 2, 0)
    return middle + jnp.pad(low_rows, low_pad) + jnp.pad(high_rows, high_pad)


def dft_tables(points, sign_value):
    index_n = jnp.arange(points, dtype=jnp.int32)
    phase_ids = index_n[:, None] * index_n[None, :] % points
    angles = phase_ids.astype(jnp.float32) * (2.0 * math.pi / points)
    return (jnp.cos(angles), sign_value * jnp.sin(angles))


def complex_contract(formula, pair_in, kernel):
    real_part = jnp.einsum(formula, pair_in[0], kernel[0], precision=highest) - jnp.einsum(
        formula, pair_in[1], kernel[1], precision=highest
    )
    imag_part = jnp.einsum(formula, pair_in[0], kernel[1], precision=highest) + jnp.einsum(
        formula, pair_in[1], kernel[0], precision=highest
    )
    return jnp.stack([real_part, imag_part])


def swap_columns(stacked):
    return lax.all_to_all(stacked, "gy", split_axis=2, concat_axis=2, tiled=True)


def swap_rows(stacked):
    return lax.all_to_all(stacked, "gx", split_axis=1, concat_axis=1, tiled=True)


def shards(
    node_feats,
    radial,
    neighbours,
    nbr_count,
    domain_count,
    base_cells,
    spline_weights,
    w_proj,
    w_radial,
    w_mix,
    w_charge,
    green_kernel,
):
    capacity = node_feats.shape[0]
    present = jnp.arange(capacity, dtype=jnp.int32) < domain_count[0]
    charges = message_passing(
        node_feats, radial, neighbours, nbr_count, domain_count, w_proj, w_radial, w_mix, w_charge
    ).reshape(capacity)
    points = green_kernel.shape[0]
    num_x = lax.axis_size("gx")
    num_y = lax.axis_size("gy")
    cell_x = points // num_x
    cell_y = points // num_y
    block_y = points // num_x
    block_z = points // num_y
    prof_x = spline_profile(base_cells[0], spline_weights[0], cell_x + 4, False)
    prof_y = spline_profile(base_cells[1], spline_weights[1], cell_y + 4, False)
    prof_z = spline_profile(base_cells[2], spline_weights[2], points, True)
    plane_weights = (prof_x[:, None, :] * prof_y[None, :, :]).reshape(
        (cell_x + 4) * (cell_y + 4), capacity
    )
    spread = jnp.einsum("pa,za->pz", plane_weights * charges[None, :], prof_z, precision=highest)
    padded = widen(spread.reshape(cell_x + 4, cell_y + 4, points))
    density = fold_axis(fold_axis(padded, 0, cell_x), 1, cell_y)
    freq_slots = jnp.arange(block_z, dtype=jnp.int32)
    slot_weight = jnp.ones((block_z,), jnp.float32)
    frequencies = jnp.arange(num_y, dtype=jnp.int32)[:, None] * block_z + freq_slots[None, :]
    grid_ids = jnp.arange(points, dtype=jnp.int32)
    z_angles = (grid_ids[:, None, None] * frequencies[None, :, :] % points).astype(jnp.float32) * (
        2.0 * math.pi / points
    )
    z_cos = jnp.cos(z_angles)
    z_sin = jnp.sin(z_angles)
    cos_fwd, sin_fwd = dft_tables(points, -1.0)
    cos_inv, sin_inv = dft_tables(points, 1.0)
    zpart_re = jnp.einsum("xyz,zjl->xjyl", density, z_cos, precision=highest)
    zpart_im = jnp.einsum("xyz,zjl->xjyl", density, -z_sin, precision=highest)
    sectioned = jnp.stack([zpart_re, zpart_im]).reshape(2, cell_x, num_y, cell_y * block_z)
    swapped = swap_columns(sectioned).reshape(2, cell_x, points, block_z)
    kernel_y = (cos_fwd.reshape(points, num_x, block_y), sin_fwd.reshape(points, num_x, block_y))
    forward_y = complex_contract("xyl,yiq->ixql", (swapped[0], swapped[1]), kernel_y)
    swapped = swap_rows(forward_y.reshape(2, num_x, cell_x * block_y * block_z)).reshape(
        2, points, block_y, block_z
    )
    forward_x = complex_contract("xql,xk->kql", (swapped[0], swapped[1]), (cos_fwd, sin_fwd))
    filtered = forward_x * green_kernel[None, :, :, :block_z]
    kernel_x = (cos_inv.reshape(points, num_x, cell_x), sin_inv.reshape(points, num_x, cell_x))
    inverse_x = complex_contract("kql,ksx->sxql", (filtered[0], filtered[1]), kernel_x)
    swapped = swap_rows(inverse_x.reshape(2, num_x, cell_x * block_y * block_z)).reshape(
        2, num_x, cell_x, block_y, block_z
    )
    kernel_back = (
        cos_inv.reshape(num_x, block_y, num_y, cell_y),
        sin_inv.reshape(num_x, block_y, num_y, cell_y),
    )
    inverse_y = complex_contract("qxvl,qvjy->xjyl", (swapped[0], swapped[1]), kernel_back)
    swapped = swap_columns(inverse_y.reshape(2, cell_x, num_y, cell_y * block_z)).reshape(
        2, cell_x, num_y, cell_y, block_z
    )
    back_cos = jnp.transpose(z_cos * slot_weight[None, None, :], (1, 2, 0))
    back_sin = jnp.transpose(z_sin * slot_weight[None, None, :], (1, 2, 0))
    real_sum = jnp.einsum("xsyl,slz->xyz", swapped[0], back_cos, precision=highest)
    imag_sum = jnp.einsum("xsyl,slz->xyz", swapped[1], back_sin, precision=highest)
    potential = (real_sum - imag_sum) * (1.0 / float(points**3))
    widened = widen(potential)
    sampled = jnp.einsum(
        "pz,za->pa", widened.reshape((cell_x + 4) * (cell_y + 4), points), prof_z, precision=highest
    )
    atom_potential = jnp.where(present, jnp.sum(plane_weights * sampled, axis=0), 0.0)
    return (charges, atom_potential, potential)


def solution(mesh):
    return jax.shard_map(
        shards,
        mesh=mesh,
        in_specs=(
            P(("gx", "gy"), None),
            P(None, None, ("gx", "gy")),
            P(None, ("gx", "gy")),
            P(("gx", "gy")),
            P(("gx", "gy")),
            P(None, ("gx", "gy")),
            P(None, None, ("gx", "gy")),
            P(),
            P(),
            P(),
            P(),
            P(None, "gx", "gy"),
        ),
        out_specs=(P(("gx", "gy")), P(("gx", "gy")), P("gx", "gy", None)),
        check_vma=False,
    )
```

```python
import functools
import math

import jax
import jax.numpy as jnp
import ml_dtypes
import numpy as np
from jax import lax
from jax.experimental import pallas as pl
from jax.experimental.pallas import tpu as pltpu
from jax.sharding import PartitionSpec as P

K = 32
L = 2


MESH = pl.DeviceIdType.MESH
TN = (((0,), (0,)), ((), ()))
NT = (((1,), (1,)), ((), ()))
NN = (((1,), (0,)), ((), ()))


def dot(a, b, dims=NN):
    return lax.dot_general(a, b, dims, preferred_element_type=jnp.float32)


def ring(index, step, count):
    return lax.rem(index + step + count, count)


def message_kernel(
    num_x,
    num_y,
    feats_ref,
    radial_ref,
    nbr_ref,
    count_ref,
    fill_ref,
    proj_ref,
    filt_ref,
    mix_ref,
    charge_w_ref,
    charges_ref,
    state,
    table,
    rows_out,
    rows_in,
    head_a,
    head_b,
    pick,
    filt_k,
    total,
    send_sem,
    recv_sem,
):
    px, py = lax.axis_index("gx"), lax.axis_index("gy")
    barrier = pltpu.get_barrier_semaphore()
    peers = [(dx, dy) for dx in (-1, 0, 1) for dy in (-1, 0, 1) if (dx, dy) != (0, 0)]
    for dx, dy in peers:
        pl.semaphore_signal(
            barrier,
            inc=1,
            device_id=(ring(px, dx, num_x), ring(py, dy, num_y)),
            device_id_type=MESH,
        )
    code = nbr_ref[...]
    direction, slot = code // 1024, code % 1024
    lane = lax.broadcasted_iota(jnp.int32, (K, 1024), 1)
    live = lax.broadcasted_iota(jnp.int32, (K, 1024), 0) < count_ref[...]
    block = lane // 128
    near = slot - jnp.maximum(block - 1, 0) * 128
    far = jnp.where(
        direction < 3,
        192 + direction * 64 + slot,
        jnp.where(
            direction > 5,
            64 + direction * 64 + slot,
            jnp.where(direction == 3, 192 + slot, 320 + slot),
        ),
    )
    named = jnp.where(live, jnp.where(direction == 4, near, far), -8192).astype(jnp.float32)
    for b in range(8):
        pick[:, b, :] = named[:, b * 128 : (b + 1) * 128]

    state[...] = jnp.transpose(feats_ref[...].astype(jnp.float32))
    row_id = lax.broadcasted_iota(jnp.int32, (128, 128), 0).astype(jnp.bfloat16)
    one, zero = jnp.ones((128, 128), jnp.bfloat16), jnp.zeros((128, 128), jnp.bfloat16)
    basis_k = lax.broadcasted_iota(jnp.int32, (128, 8 * K), 1) % K

    def onehot(k, begin, groups):
        row = pick[k, begin // 128 : begin // 128 + 1, :]
        parts = [
            jnp.where(row_id == jnp.broadcast_to((row - 128.0 * g).astype(jnp.bfloat16), (128, 128)), one, zero)
            for g in range(groups)
        ]
        return jnp.concatenate(parts, axis=0)

    def messages(group, tables):
        begin = group * 256
        radial = radial_ref[:, begin : begin + 256]
        total[...] = jnp.zeros_like(total)

        def step(pair, carry):
            k = 2 * pair
            filters = dot(filt_k[pl.ds(pl.multiple_of(k * 128, 256), 256), :], radial)
            for half, (source, groups) in enumerate(tables):
                at = begin + 128 * half
                hot = jnp.concatenate([onehot(k, at, groups), onehot(k + 1, at, groups)], axis=1)
                got = dot(source(), hot)
                lanes = slice(128 * half, 128 * half + 128)
                total[:, lanes] += (
                    got[:, :128] * filters[:128, lanes] + got[:, 128:] * filters[128:, lanes]
                )
            return carry

        lax.fori_loop(0, K // 2, step, 0, unroll=2)
        return (total[...] * (1.0 / math.sqrt(K))).astype(jnp.bfloat16)

    for layer in range(L):
        spread = jnp.concatenate(
            [jnp.broadcast_to(filt_ref[layer, b], (K, 128)) for b in range(8)], axis=0
        )
        spread = jnp.transpose(spread.astype(jnp.float32))
        for k in range(K):
            filt_k[k * 128 : (k + 1) * 128, :] = jnp.where(basis_k == k, spread, 0.0).astype(jnp.bfloat16)
        proj = proj_ref[layer]
        first = dot(proj, state[:, :256].astype(jnp.bfloat16), TN).astype(jnp.bfloat16)
        rows_out[layer] = jnp.transpose(first.astype(jnp.float32)).astype(jnp.bfloat16)
        if layer == 0:
            pl.semaphore_wait(barrier, 8)
        copies = []
        for dx, dy in peers:
            if dx == 1:
                band, land = 1, 1 - dy
            elif dx == -1:
                band, land = 0, 4 - dy
            elif dy == 1:
                band, land = 3, 6
            else:
                band, land = 2, 7
            copies.append(
                pltpu.make_async_remote_copy(
                    src_ref=rows_out.at[layer, pl.ds(band * 64, 64)],
                    dst_ref=rows_in.at[layer, pl.ds(land * 64, 64)],
                    send_sem=send_sem.at[layer, land],
                    recv_sem=recv_sem.at[layer, land],
                    device_id=(ring(px, dx, num_x), ring(py, dy, num_y)),
                    device_id_type=MESH,
                )
            )
            copies[-1].start()
        table[:, :256] = first
        table[:, 256:] = dot(proj, state[:, 256:].astype(jnp.bfloat16), TN).astype(jnp.bfloat16)

        def update(group, tables):
            begin = group * 256
            u = messages(group, tables)
            mixed = dot(mix_ref[layer], u, TN)
            lanes = slice(begin, begin + 256)
            state[:, lanes] = (
                (state[:, lanes] + mixed / (1.0 + jnp.exp(-mixed))).astype(jnp.bfloat16).astype(jnp.float32)
            )

        def window(block):
            low = max(block - 1, 0) * 128
            high = min(block + 2, 8) * 128
            return (lambda: table[:, low:high]), (high - low) // 128

        for group in (1, 2, 3):
            update(group, [window(2 * group), window(2 * group + 1)])
        for copy in copies:
            copy.wait()
        far_rows = jnp.transpose(rows_in[layer].astype(jnp.float32)).astype(jnp.bfloat16)
        head_a[:, :256] = table[:, :256]
        head_a[:, 256:] = far_rows[:, :384]
        head_b[:, :384] = table[:, :384]
        head_b[:, 384:] = far_rows[:, 384:]
        update(0, [((lambda: head_a[...]), 5), ((lambda: head_b[...]), 4)])
    charge = dot(charge_w_ref[...], state[...].astype(jnp.bfloat16))[0:1]
    inside = lax.broadcasted_iota(jnp.int32, (1, 1024), 1) < fill_ref[...]
    charges_ref[...] = jnp.where(inside, charge, 0.0)


def message_passing(feats, radial, neighbours, nbr_count, fill, w_proj, w_radial, w_mix, w_charge):
    num_x, num_y = lax.axis_size("gx"), lax.axis_size("gy")
    vmem = pl.BlockSpec(memory_space=pltpu.VMEM)
    bf16 = jnp.bfloat16
    return pl.pallas_call(
        functools.partial(message_kernel, num_x, num_y),
        out_shape=jax.ShapeDtypeStruct((1, 1024), jnp.float32),
        in_specs=[vmem] * 9,
        out_specs=vmem,
        scratch_shapes=[
            pltpu.VMEM((128, 1024), jnp.float32),
            pltpu.VMEM((128, 1024), bf16),
            pltpu.VMEM((L, 256, 128), bf16),
            pltpu.VMEM((L, 512, 128), bf16),
            pltpu.VMEM((128, 640), bf16),
            pltpu.VMEM((128, 512), bf16),
            pltpu.VMEM((K, 8, 128), jnp.float32),
            pltpu.VMEM((K * 128, 8 * K), bf16),
            pltpu.VMEM((128, 256), jnp.float32),
            pltpu.SemaphoreType.DMA((L, 8)),
            pltpu.SemaphoreType.DMA((L, 8)),
        ],
        compiler_params=pltpu.CompilerParams(
            collective_id=0, has_side_effects=True, vmem_limit_bytes=48 * 1024 * 1024
        ),
        name="message_passing",
    )(
        feats,
        radial.reshape(8 * K, 1024),
        neighbours,
        nbr_count.reshape(1, 1024),
        fill,
        w_proj,
        w_radial.reshape(L, 8, 1, 128),
        w_mix,
        jnp.broadcast_to(w_charge.reshape(1, 128), (8, 128)),
    )

SIDES = ((-1, 0), (1, 0), (0, -1), (0, 1), (-1, -1), (-1, 1), (1, -1), (1, 1))
SIDE_ROWS = (32, 32, 32, 32, 16, 16, 16, 16)
SIDE_AT = (0, 32, 64, 96, 128, 144, 160, 176)
OPPOSITE = (1, 0, 3, 2, 7, 6, 5, 4)


def split(values):
    high = values.astype(jnp.bfloat16)
    return high, (values - high.astype(jnp.float32)).astype(jnp.bfloat16)


def np_split(values):
    high = values.astype(ml_dtypes.bfloat16)
    return high, (values - high.astype(np.float64)).astype(ml_dtypes.bfloat16)


def mesh_tables():
    ids = np.arange(256)
    angles = 2.0 * np.pi * (ids[:, None] * ids[None, :] % 256) / 256
    waves = np.concatenate([np.cos(angles), np.sin(angles)], axis=0)
    column, slot = np.arange(16)[:, None], np.arange(8)[None, :]
    kz = (16 * column + slot + (column >= 8)).reshape(128)
    turn = 2.0 * np.pi * (kz[:, None] * ids[None, :] % 256) / 256
    ahead = np.stack([np.cos(turn), -np.sin(turn)])
    back = 2.0 * ahead
    ahead[0, 0], ahead[1, 0] = 1.0, 1.0 - 2.0 * (ids % 2)
    back[0, 0], back[1, 0] = ahead[0, 0], ahead[1, 0]
    back = back / 256.0**3
    fold = np.zeros((16, 16, 192))
    for at, (dx, dy) in zip(SIDE_AT, SIDES, strict=True):
        first_x, first_y = (14 if dx > 0 else 0), (14 if dy > 0 else 0)
        for i in range(2):
            if dy == 0:
                for y in range(16):
                    fold[y, first_x + i, at + 16 * i + y] = 1
            elif dx == 0:
                for x in range(16):
                    fold[first_y + i, x, at + 16 * i + x] = 1
            else:
                for j in range(2):
                    fold[first_y + j, first_x + i, at + 2 * i + j] = 1
    return (
        *np_split(waves),
        *np_split(ahead.reshape(256, 256)),
        *np_split(back.reshape(256, 256)),
        fold.reshape(256, 192).astype(ml_dtypes.bfloat16),
    )


def regroup(parts):
    group = lax.broadcasted_iota(jnp.int32, (16, 128), 1) // 16
    parts = list(parts)
    for step in (1, 2, 4):
        low = (group & step) == 0
        for i in range(8):
            if i & step == 0:
                a, b = parts[i], parts[i | step]
                parts[i] = jnp.where(low, a, pltpu.roll(b, 16 * step, 1))
                parts[i | step] = jnp.where(low, pltpu.roll(a, 128 - 16 * step, 1), b)
    return parts


def swap_groups(values):
    row = lax.broadcasted_iota(jnp.int32, values.shape, 1)
    group = lax.broadcasted_iota(jnp.int32, values.shape, 2) // 16
    for step in (1, 2, 4):
        row_high, group_high = (row & step) != 0, (group & step) != 0
        if step == 4:
            moved = pltpu.roll(pltpu.roll(values, 4, 1), 64, 2)
        else:
            up = pltpu.roll(pltpu.roll(values, 8 - step, 1), 16 * step, 2)
            down = pltpu.roll(pltpu.roll(values, step, 1), 128 - 16 * step, 2)
            moved = jnp.where(row_high, down, up)
        values = jnp.where(row_high == group_high, values, moved)
    return values


def profile(cells, base, weights):
    total = jnp.zeros(cells.shape, jnp.float32)
    for offset in range(4):
        total = total + jnp.where(cells == base[offset], weights[offset], 0.0)
    return total


def mesh_kernel(
    charges_ref,
    fill_ref,
    base_ref,
    spline_ref,
    green_ref,
    green_last_ref,
    wave_h,
    wave_l,
    ahead_h,
    ahead_l,
    back_h,
    back_l,
    fold_ref,
    atom_ref,
    grid_ref,
    plane,
    prof_h,
    prof_l,
    halo_out,
    halo_in,
    z_out,
    z_in,
    y_out,
    y_in,
    x_out,
    x_in,
    v_out,
    v_in,
    shared,
    green_in,
    send_sem,
    recv_sem,
):
    count = 16
    px, py = lax.axis_index("gx"), lax.axis_index("gy")
    barrier = pltpu.get_barrier_semaphore()

    def greet(d, carry):
        for where in ((ring(px, d, count), py), (px, ring(py, d, count))):
            pl.semaphore_signal(barrier, inc=1, device_id=where, device_id_type=MESH)
        return carry

    lax.fori_loop(1, count, greet, 0)
    for dx, dy in SIDES[4:]:
        pl.semaphore_signal(
            barrier,
            inc=1,
            device_id=(ring(px, dx, count), ring(py, dy, count)),
            device_id_type=MESH,
        )

    def remote(source, target, stage, index, where):
        return pltpu.make_async_remote_copy(
            src_ref=source,
            dst_ref=target,
            send_sem=send_sem.at[stage, index],
            recv_sem=recv_sem.at[stage, index],
            device_id=where,
            device_id_type=MESH,
        )

    def exchange(make):
        def start(d, carry):
            make(d).start()
            return carry

        lax.fori_loop(1, count, start, 0)

    def arrive(make):
        def wait(d, carry):
            make(d).wait()
            return carry

        lax.fori_loop(1, count, wait, 0)

    def side_copies(half):
        return [
            remote(
                halo_out.at[half, pl.ds(SIDE_AT[e], SIDE_ROWS[e])],
                halo_in.at[half, pl.ds(SIDE_AT[OPPOSITE[e]], SIDE_ROWS[e])],
                half,
                e,
                (ring(px, SIDES[e][0], count), ring(py, SIDES[e][1], count)),
            )
            for e in range(8)
        ]

    def column_copy(out, into, stage):
        def make(d):
            to = ring(py, d, count)
            return remote(out.at[:, to], into.at[:, py], stage, d, (px, to))

        return make

    def row_copy(out, into, stage, layers):
        def make(d):
            to = ring(px, d, count)
            return remote(out.at[layers, to], into.at[layers, px], stage, d, (to, py))

        return make

    main, extra = pl.ds(0, 2), pl.ds(2, 1)

    def green_copy():
        return remote(green_last_ref, green_in, 8, 0, (px, 0))

    def rows(dim):
        base = base_ref[dim : dim + 1, :]
        cells = [base + offset for offset in range(4)]
        if dim == 2:
            cells = [jnp.where(c >= 256, c - 256, c) for c in cells]
        return cells, [spline_ref[4 * dim + o : 4 * dim + o + 1, :] for o in range(4)]

    z_cells = lax.broadcasted_iota(jnp.int32, (256, 1024), 0)
    high, low = split(profile(z_cells, *rows(2)))
    prof_h[...] = high
    prof_l[...] = low
    sixteen = lax.broadcasted_iota(jnp.int32, (16, 1024), 0)
    eight = lax.broadcasted_iota(jnp.int32, (8, 1024), 0)
    edge = jnp.where(eight < 2, eight, eight + 16)
    in_x, in_y = (profile(sixteen + 2, *rows(dim)) for dim in (0, 1))
    edge_x, edge_y = (profile(edge, *rows(dim)) for dim in (0, 1))
    for y in range(16):
        plane[16 * y : 16 * y + 16, :] = in_y[y : y + 1, :] * in_x
    for i in range(4):
        at = 256 + 32 * (i // 2) + 16 * (i % 2)
        plane[at : at + 16, :] = edge_x[i : i + 1, :] * in_y
        plane[at + 64 : at + 80, :] = edge_y[i : i + 1, :] * in_x
    corner = sixteen < 4
    corner_x = [
        profile(jnp.where(corner, sixteen // 2 + begin, 99), *rows(0)) for begin in (0, 18)
    ]
    corner_y = [
        profile(jnp.where(corner, sixteen % 2 + begin, 99), *rows(1)) for begin in (0, 18)
    ]
    for e in range(4):
        at = 256 + SIDE_AT[4 + e]
        plane[at : at + 16, :] = corner_x[e // 2] * corner_y[e % 2]

    high, low = split(plane[...] * charges_ref[...])
    spread = dot(high, prof_h[...], NT) + dot(low, prof_h[...], NT) + dot(high, prof_l[...], NT)
    halo_out[0] = spread[256:].astype(jnp.bfloat16)
    pl.semaphore_wait(barrier, 34)
    copies = side_copies(0)
    for copy in copies:
        copy.start()

    @pl.when(py == 8)
    def _():
        green_copy().start()

    for copy in copies:
        copy.wait()
    high, low = split(spread[:256] + dot(fold_ref[...], halo_in[0]))

    lines = dot(ahead_h[...], high, NT) + dot(ahead_l[...], high, NT) + dot(ahead_h[...], low, NT)
    halves = [
        swap_groups(lines[:, 128 * half : 128 * half + 128].reshape(32, 8, 128)) for half in (0, 1)
    ]
    z_out[...] = jnp.concatenate(halves, axis=1).astype(jnp.bfloat16).reshape(2, 16, 16, 128)
    make = column_copy(z_out, z_in, 2)
    exchange(make)
    z_in[:, pl.ds(py, 1)] = z_out[:, pl.ds(py, 1)]
    arrive(make)

    cos_h, sin_h = wave_h[:256], wave_h[256:]
    cos_l, sin_l = wave_l[:256], wave_l[256:]
    both = jnp.concatenate([z_in[0].reshape(256, 128), z_in[1].reshape(256, 128)], axis=1)
    both = jnp.transpose(both.astype(jnp.float32)).astype(jnp.bfloat16)
    c = dot(both, cos_h) + dot(both, cos_l)
    s = dot(both, sin_h) + dot(both, sin_l)
    apart = (lax.broadcasted_iota(jnp.int32, (128, 256), 0) < 16) & (py == 0)
    real = c[:128] + jnp.where(apart, 0.0, s[128:])
    imag = jnp.where(apart, 0.0, c[128:]) - s[:128]

    def to_slots(values, layer):
        for half in (0, 1):
            lanes = slice(128 * half, 128 * half + 128)
            done = regroup([values[16 * i : 16 * i + 16, lanes] for i in range(8)])
            for i in range(8):
                y_out[layer, 8 * half + i] = done[i].astype(jnp.bfloat16)

    to_slots(real, 0)
    to_slots(imag, 1)
    make = row_copy(y_out, y_in, 3, main)
    exchange(make)
    y_in[0:2, pl.ds(px, 1)] = y_out[0:2, pl.ds(px, 1)]

    @pl.when(py == 0)
    def _():
        blank = jnp.zeros((96, 256), jnp.float32)
        to_slots(jnp.concatenate([c[128:144], -s[128:144], blank], axis=0), 2)
        exchange(row_copy(y_out, y_in, 4, extra))
        y_in[2:3, pl.ds(px, 1)] = y_out[2:3, pl.ds(px, 1)]

    arrive(make)

    def forward_x(values):
        return dot(cos_h, values) + dot(cos_l, values), dot(sin_h, values) + dot(sin_l, values)

    def inverse_x(values):
        high, low = split(values)
        return (
            dot(cos_h, high) + dot(cos_l, high) + dot(cos_h, low),
            dot(sin_h, high) + dot(sin_l, high) + dot(sin_h, low),
        )

    c, s = forward_x(
        jnp.concatenate([y_in[0].reshape(256, 128), y_in[1].reshape(256, 128)], axis=1)
    )
    real = (c[:, :128] + s[:, 128:]) * green_ref[...]
    imag = (c[:, 128:] - s[:, :128]) * green_ref[...]
    c, s = inverse_x(jnp.concatenate([real, imag], axis=1))
    x_out[0] = (c[:, :128] - s[:, 128:]).astype(jnp.bfloat16).reshape(16, 16, 128)
    x_out[1] = (c[:, 128:] + s[:, :128]).astype(jnp.bfloat16).reshape(16, 16, 128)
    make = row_copy(x_out, x_in, 5, main)
    exchange(make)
    x_in[0:2, pl.ds(px, 1)] = x_out[0:2, pl.ds(px, 1)]

    @pl.when(py == 0)
    def _():
        arrive(row_copy(y_out, y_in, 4, extra))
        green_copy().wait_recv()
        first = lax.broadcasted_iota(jnp.int32, (256, 128), 1) < 16
        c, s = forward_x(y_in[2].reshape(256, 128))
        real = (c + pltpu.roll(s, 112, 1)) * green_in[...]
        imag = (pltpu.roll(c, 112, 1) - s) * green_in[...]
        c, s = inverse_x(real + pltpu.roll(imag, 16, 1))
        real = jnp.where(first, c - pltpu.roll(s, 112, 1), 0.0)
        imag = jnp.where(first, pltpu.roll(c, 112, 1) + s, 0.0)
        x_out[2] = (real + pltpu.roll(imag, 16, 1)).astype(jnp.bfloat16).reshape(16, 16, 128)
        back_copy = row_copy(x_out, x_in, 6, extra)
        exchange(back_copy)
        x_in[2:3, pl.ds(px, 1)] = x_out[2:3, pl.ds(px, 1)]

    @pl.when(py == 8)
    def _():
        green_copy().wait_send()

    arrive(make)

    def to_rows(layer):
        halves = [
            regroup([x_in[layer, 8 * half + i].astype(jnp.float32) for i in range(8)])
            for half in (0, 1)
        ]
        return [jnp.concatenate([halves[0][i], halves[1][i]], axis=1) for i in range(8)]

    real, imag = to_rows(0), to_rows(1)
    shared[0] = real[0]
    shared[1] = imag[0]

    @pl.when(py == 0)
    def _():
        arrive(row_copy(x_out, x_in, 6, extra))
        last = to_rows(2)
        shared[0] = -last[1]
        shared[1] = last[0]

    a = jnp.concatenate(real, axis=0).astype(jnp.bfloat16)
    b = jnp.concatenate(imag, axis=0).astype(jnp.bfloat16)
    a_too = jnp.concatenate([shared[0], *real[1:]], axis=0).astype(jnp.bfloat16)
    b_too = jnp.concatenate([shared[1], *imag[1:]], axis=0).astype(jnp.bfloat16)
    real = dot(cos_h, a, NT) + dot(cos_l, a, NT) - dot(sin_h, b, NT) - dot(sin_l, b, NT)
    imag = dot(cos_h, b_too, NT) + dot(cos_l, b_too, NT) + dot(sin_h, a_too, NT) + dot(sin_l, a_too, NT)
    v_out[0] = real.astype(jnp.bfloat16).reshape(16, 16, 128)
    v_out[1] = imag.astype(jnp.bfloat16).reshape(16, 16, 128)
    make = column_copy(v_out, v_in, 7)
    exchange(make)
    v_in[:, pl.ds(py, 1)] = v_out[:, pl.ds(py, 1)]
    arrive(make)

    got = v_in[...].reshape(32, 16, 128).astype(jnp.float32)
    halves = [swap_groups(got[:, 8 * half : 8 * half + 8]).reshape(256, 128) for half in (0, 1)]
    lines = jnp.concatenate(halves, axis=1).astype(jnp.bfloat16)
    grid = dot(lines, back_h[...], TN) + dot(lines, back_l[...], TN)
    grid_ref[...] = grid
    high, low = split(grid)
    halo_out[1] = dot(fold_ref[...], high, TN).astype(jnp.bfloat16)
    copies = side_copies(1)
    for copy in copies:
        copy.start()

    sampled = dot(high, prof_h[...]) + dot(low, prof_h[...]) + dot(high, prof_l[...])
    total = jnp.sum(sampled * plane[:256], axis=0, keepdims=True)
    for copy in copies:
        copy.wait()
    sampled = dot(halo_in[1], prof_h[...]) + dot(halo_in[1], prof_l[...])
    total = total + jnp.sum(sampled * plane[256:], axis=0, keepdims=True)
    inside = lax.broadcasted_iota(jnp.int32, (1, 1024), 1) < fill_ref[...]
    atom_ref[...] = jnp.where(inside, total, 0.0)


def mesh_potential(charges, fill, base_cells, spline_weights, green):
    vmem = pl.BlockSpec(memory_space=pltpu.VMEM)
    bf16, f32 = jnp.bfloat16, jnp.float32
    picked = jnp.where(lax.axis_index("gy") < 8, green[:, :, 0:8], green[:, :, 1:9])
    picked = jnp.transpose(picked, (0, 2, 1)).reshape(256, 128)
    last = jnp.pad(green[:, :, 0], ((0, 0), (0, 112)))
    blocks = (16, 16, 128)
    atom, grid = pl.pallas_call(
        mesh_kernel,
        out_shape=(
            jax.ShapeDtypeStruct((1, 1024), f32),
            jax.ShapeDtypeStruct((256, 256), f32),
        ),
        in_specs=[vmem] * 13,
        out_specs=(vmem, vmem),
        scratch_shapes=[
            pltpu.VMEM((448, 1024), f32),
            pltpu.VMEM((256, 1024), bf16),
            pltpu.VMEM((256, 1024), bf16),
            pltpu.VMEM((2, 192, 256), bf16),
            pltpu.VMEM((2, 192, 256), bf16),
            pltpu.VMEM((2, *blocks), bf16),
            pltpu.VMEM((2, *blocks), bf16),
            pltpu.VMEM((3, *blocks), bf16),
            pltpu.VMEM((3, *blocks), bf16),
            pltpu.VMEM((3, *blocks), bf16),
            pltpu.VMEM((3, *blocks), bf16),
            pltpu.VMEM((2, *blocks), bf16),
            pltpu.VMEM((2, *blocks), bf16),
            pltpu.VMEM((2, 16, 256), f32),
            pltpu.VMEM((256, 128), f32),
            pltpu.SemaphoreType.DMA((9, 16)),
            pltpu.SemaphoreType.DMA((9, 16)),
        ],
        compiler_params=pltpu.CompilerParams(
            collective_id=1, has_side_effects=True, vmem_limit_bytes=48 * 1024 * 1024
        ),
        name="mesh_potential",
    )(
        charges,
        fill,
        base_cells,
        spline_weights.reshape(12, 1024),
        picked,
        last,
        *(jnp.asarray(table) for table in mesh_tables()),
    )
    return atom, jnp.transpose(grid.reshape(16, 16, 256), (1, 0, 2))


def shards(
    node_feats,
    radial,
    neighbours,
    nbr_count,
    domain_count,
    base_cells,
    spline_weights,
    w_proj,
    w_radial,
    w_mix,
    w_charge,
    green_kernel,
):
    fill = jnp.broadcast_to(domain_count.reshape(1, 1), (1, 1024))
    charges = message_passing(
        node_feats, radial, neighbours, nbr_count, fill, w_proj, w_radial, w_mix, w_charge
    )
    atom_potential, potential = mesh_potential(
        charges, fill, base_cells, spline_weights, green_kernel
    )
    return (charges.reshape(1024), atom_potential.reshape(1024), potential)


def solution(mesh):
    return jax.shard_map(
        shards,
        mesh=mesh,
        in_specs=(
            P(("gx", "gy"), None),
            P(None, None, ("gx", "gy")),
            P(None, ("gx", "gy")),
            P(("gx", "gy")),
            P(("gx", "gy")),
            P(None, ("gx", "gy")),
            P(None, None, ("gx", "gy")),
            P(),
            P(),
            P(),
            P(),
            P(None, "gx", "gy"),
        ),
        out_specs=(P(("gx", "gy")), P(("gx", "gy")), P("gx", "gy", None)),
        check_vma=False,
    )
```

```python
import functools
import math

import jax
import jax.numpy as jnp
import ml_dtypes
import numpy as np
from jax import lax
from jax.experimental import pallas as pl
from jax.experimental.pallas import tpu as pltpu
from jax.sharding import PartitionSpec as P

K = 32
L = 2


MESH = pl.DeviceIdType.MESH
TN = (((0,), (0,)), ((), ()))
NT = (((1,), (1,)), ((), ()))
NN = (((1,), (0,)), ((), ()))


def dot(a, b, dims=NN):
    return lax.dot_general(a, b, dims, preferred_element_type=jnp.float32)


def ring(index, step, count):
    return lax.rem(index + step + count, count)


def message_kernel(
    num_x,
    num_y,
    feats_ref,
    radial_ref,
    nbr_ref,
    count_ref,
    fill_ref,
    proj_ref,
    filt_ref,
    mix_ref,
    charge_w_ref,
    charges_ref,
    state,
    table,
    rows_out,
    rows_in,
    head_a,
    head_b,
    pick,
    filt_k,
    total,
    send_sem,
    recv_sem,
):
    px, py = lax.axis_index("gx"), lax.axis_index("gy")
    barrier = pltpu.get_barrier_semaphore()
    peers = [(dx, dy) for dx in (-1, 0, 1) for dy in (-1, 0, 1) if (dx, dy) != (0, 0)]
    for dx, dy in peers:
        pl.semaphore_signal(
            barrier,
            inc=1,
            device_id=(ring(px, dx, num_x), ring(py, dy, num_y)),
            device_id_type=MESH,
        )
    code = nbr_ref[...]
    direction, slot = code // 1024, code % 1024
    lane = lax.broadcasted_iota(jnp.int32, (K, 1024), 1)
    live = lax.broadcasted_iota(jnp.int32, (K, 1024), 0) < count_ref[...]
    block = lane // 128
    near = slot - jnp.maximum(block - 1, 0) * 128
    far = jnp.where(
        direction < 3,
        192 + direction * 64 + slot,
        jnp.where(
            direction > 5,
            64 + direction * 64 + slot,
            jnp.where(direction == 3, 192 + slot, 320 + slot),
        ),
    )
    named = jnp.where(live, jnp.where(direction == 4, near, far), -8192).astype(jnp.float32)
    for b in range(8):
        pick[:, b, :] = named[:, b * 128 : (b + 1) * 128]

    state[...] = jnp.transpose(feats_ref[...].astype(jnp.float32))
    row_id = lax.broadcasted_iota(jnp.int32, (128, 128), 0).astype(jnp.bfloat16)
    one, zero = jnp.ones((128, 128), jnp.bfloat16), jnp.zeros((128, 128), jnp.bfloat16)
    basis_k = lax.broadcasted_iota(jnp.int32, (128, 8 * K), 1) % K

    def onehot(k, begin, groups):
        row = pick[k, begin // 128 : begin // 128 + 1, :]
        parts = [
            jnp.where(row_id == jnp.broadcast_to((row - 128.0 * g).astype(jnp.bfloat16), (128, 128)), one, zero)
            for g in range(groups)
        ]
        return jnp.concatenate(parts, axis=0)

    def messages(group, tables):
        begin = group * 256
        radial = radial_ref[:, begin : begin + 256]
        total[...] = jnp.zeros_like(total)

        for k in range(0, K, 2):
            filters = dot(filt_k[k * 128 : k * 128 + 256, :], radial)
            for half, (source, groups) in enumerate(tables):
                at = begin + 128 * half
                hot = jnp.concatenate([onehot(k, at, groups), onehot(k + 1, at, groups)], axis=1)
                got = dot(source(), hot)
                lanes = slice(128 * half, 128 * half + 128)
                total[:, lanes] += (
                    got[:, :128] * filters[:128, lanes] + got[:, 128:] * filters[128:, lanes]
                )
        return (total[...] * (1.0 / math.sqrt(K))).astype(jnp.bfloat16)

    for layer in range(L):
        spread = jnp.concatenate(
            [jnp.broadcast_to(filt_ref[layer, b], (K, 128)) for b in range(8)], axis=0
        )
        spread = jnp.transpose(spread.astype(jnp.float32))
        for k in range(K):
            filt_k[k * 128 : (k + 1) * 128, :] = jnp.where(basis_k == k, spread, 0.0).astype(jnp.bfloat16)
        proj = proj_ref[layer]
        first = dot(proj, state[:, :256].astype(jnp.bfloat16), TN).astype(jnp.bfloat16)
        rows_out[layer] = jnp.transpose(first.astype(jnp.float32)).astype(jnp.bfloat16)
        if layer == 0:
            pl.semaphore_wait(barrier, 8)
        copies = []
        for dx, dy in peers:
            if dx == 1:
                band, land = 1, 1 - dy
            elif dx == -1:
                band, land = 0, 4 - dy
            elif dy == 1:
                band, land = 3, 6
            else:
                band, land = 2, 7
            copies.append(
                pltpu.make_async_remote_copy(
                    src_ref=rows_out.at[layer, pl.ds(band * 64, 64)],
                    dst_ref=rows_in.at[layer, pl.ds(land * 64, 64)],
                    send_sem=send_sem.at[layer, land],
                    recv_sem=recv_sem.at[layer, land],
                    device_id=(ring(px, dx, num_x), ring(py, dy, num_y)),
                    device_id_type=MESH,
                )
            )
            copies[-1].start()
        table[:, :256] = first
        table[:, 256:] = dot(proj, state[:, 256:].astype(jnp.bfloat16), TN).astype(jnp.bfloat16)

        def update(group, tables):
            begin = group * 256
            u = messages(group, tables)
            mixed = dot(mix_ref[layer], u, TN)
            lanes = slice(begin, begin + 256)
            state[:, lanes] = (
                (state[:, lanes] + mixed / (1.0 + jnp.exp(-mixed))).astype(jnp.bfloat16).astype(jnp.float32)
            )

        def window(block):
            low = max(block - 1, 0) * 128
            high = min(block + 2, 8) * 128
            return (lambda: table[:, low:high]), (high - low) // 128

        for group in (1, 2, 3):
            update(group, [window(2 * group), window(2 * group + 1)])
        for copy in copies:
            copy.wait()
        far_rows = jnp.transpose(rows_in[layer].astype(jnp.float32)).astype(jnp.bfloat16)
        head_a[:, :256] = table[:, :256]
        head_a[:, 256:] = far_rows[:, :384]
        head_b[:, :384] = table[:, :384]
        head_b[:, 384:] = far_rows[:, 384:]
        update(0, [((lambda: head_a[...]), 5), ((lambda: head_b[...]), 4)])
    charge = dot(charge_w_ref[...], state[...].astype(jnp.bfloat16))[0:1]
    inside = lax.broadcasted_iota(jnp.int32, (1, 1024), 1) < fill_ref[...]
    charges_ref[...] = jnp.where(inside, charge, 0.0)


def message_passing(feats, radial, neighbours, nbr_count, fill, w_proj, w_radial, w_mix, w_charge):
    num_x, num_y = lax.axis_size("gx"), lax.axis_size("gy")
    vmem = pl.BlockSpec(memory_space=pltpu.VMEM)
    bf16 = jnp.bfloat16
    return pl.pallas_call(
        functools.partial(message_kernel, num_x, num_y),
        out_shape=jax.ShapeDtypeStruct((1, 1024), jnp.float32),
        in_specs=[vmem] * 9,
        out_specs=vmem,
        scratch_shapes=[
            pltpu.VMEM((128, 1024), jnp.float32),
            pltpu.VMEM((128, 1024), bf16),
            pltpu.VMEM((L, 256, 128), bf16),
            pltpu.VMEM((L, 512, 128), bf16),
            pltpu.VMEM((128, 640), bf16),
            pltpu.VMEM((128, 512), bf16),
            pltpu.VMEM((K, 8, 128), jnp.float32),
            pltpu.VMEM((K * 128, 8 * K), bf16),
            pltpu.VMEM((128, 256), jnp.float32),
            pltpu.SemaphoreType.DMA((L, 8)),
            pltpu.SemaphoreType.DMA((L, 8)),
        ],
        compiler_params=pltpu.CompilerParams(
            collective_id=0, has_side_effects=True, vmem_limit_bytes=48 * 1024 * 1024
        ),
        name="message_passing",
    )(
        feats,
        radial.reshape(8 * K, 1024),
        neighbours,
        nbr_count.reshape(1, 1024),
        fill,
        w_proj,
        w_radial.reshape(L, 8, 1, 128),
        w_mix,
        jnp.broadcast_to(w_charge.reshape(1, 128), (8, 128)),
    )

SIDES = ((-1, 0), (1, 0), (0, -1), (0, 1), (-1, -1), (-1, 1), (1, -1), (1, 1))
SIDE_ROWS = (32, 32, 32, 32, 16, 16, 16, 16)
SIDE_AT = (0, 32, 64, 96, 128, 144, 160, 176)
OPPOSITE = (1, 0, 3, 2, 7, 6, 5, 4)


def split(values):
    high = values.astype(jnp.bfloat16)
    return high, (values - high.astype(jnp.float32)).astype(jnp.bfloat16)


def np_split(values):
    high = values.astype(ml_dtypes.bfloat16)
    return high, (values - high.astype(np.float64)).astype(ml_dtypes.bfloat16)


def mesh_tables():
    ids = np.arange(256)
    angles = 2.0 * np.pi * (ids[:, None] * ids[None, :] % 256) / 256
    waves = np.concatenate([np.cos(angles), np.sin(angles)], axis=0)
    column, slot = np.arange(16)[:, None], np.arange(8)[None, :]
    kz = (16 * column + slot + (column >= 8)).reshape(128)
    turn = 2.0 * np.pi * (kz[:, None] * ids[None, :] % 256) / 256
    ahead = np.stack([np.cos(turn), -np.sin(turn)])
    back = 2.0 * ahead
    ahead[0, 0], ahead[1, 0] = 1.0, 1.0 - 2.0 * (ids % 2)
    back[0, 0], back[1, 0] = ahead[0, 0], ahead[1, 0]
    back = back / 256.0**3
    fold = np.zeros((16, 16, 192))
    for at, (dx, dy) in zip(SIDE_AT, SIDES, strict=True):
        first_x, first_y = (14 if dx > 0 else 0), (14 if dy > 0 else 0)
        for i in range(2):
            if dy == 0:
                for y in range(16):
                    fold[y, first_x + i, at + 16 * i + y] = 1
            elif dx == 0:
                for x in range(16):
                    fold[first_y + i, x, at + 16 * i + x] = 1
            else:
                for j in range(2):
                    fold[first_y + j, first_x + i, at + 2 * i + j] = 1
    return (
        *np_split(waves),
        *np_split(ahead.reshape(256, 256)),
        *np_split(back.reshape(256, 256)),
        fold.reshape(256, 192).astype(ml_dtypes.bfloat16),
    )


def regroup(parts):
    group = lax.broadcasted_iota(jnp.int32, (16, 128), 1) // 16
    parts = list(parts)
    for step in (1, 2, 4):
        low = (group & step) == 0
        for i in range(8):
            if i & step == 0:
                a, b = parts[i], parts[i | step]
                parts[i] = jnp.where(low, a, pltpu.roll(b, 16 * step, 1))
                parts[i | step] = jnp.where(low, pltpu.roll(a, 128 - 16 * step, 1), b)
    return parts


def swap_groups(values):
    row = lax.broadcasted_iota(jnp.int32, values.shape, 1)
    group = lax.broadcasted_iota(jnp.int32, values.shape, 2) // 16
    for step in (1, 2, 4):
        row_high, group_high = (row & step) != 0, (group & step) != 0
        if step == 4:
            moved = pltpu.roll(pltpu.roll(values, 4, 1), 64, 2)
        else:
            up = pltpu.roll(pltpu.roll(values, 8 - step, 1), 16 * step, 2)
            down = pltpu.roll(pltpu.roll(values, step, 1), 128 - 16 * step, 2)
            moved = jnp.where(row_high, down, up)
        values = jnp.where(row_high == group_high, values, moved)
    return values


def profile(cells, base, weights):
    total = jnp.zeros(cells.shape, jnp.float32)
    for offset in range(4):
        total = total + jnp.where(cells == base[offset], weights[offset], 0.0)
    return total


def mesh_kernel(
    charges_ref,
    fill_ref,
    base_ref,
    spline_ref,
    green_ref,
    green_last_ref,
    wave_h,
    wave_l,
    ahead_h,
    ahead_l,
    back_h,
    back_l,
    fold_ref,
    atom_ref,
    grid_ref,
    plane,
    prof_h,
    prof_l,
    halo_out,
    halo_in,
    z_out,
    z_in,
    y_out,
    y_in,
    x_out,
    x_in,
    v_out,
    v_in,
    shared,
    green_in,
    send_sem,
    recv_sem,
):
    count = 16
    px, py = lax.axis_index("gx"), lax.axis_index("gy")
    barrier = pltpu.get_barrier_semaphore()

    def greet(d, carry):
        for where in ((ring(px, d, count), py), (px, ring(py, d, count))):
            pl.semaphore_signal(barrier, inc=1, device_id=where, device_id_type=MESH)
        return carry

    lax.fori_loop(1, count, greet, 0)
    for dx, dy in SIDES[4:]:
        pl.semaphore_signal(
            barrier,
            inc=1,
            device_id=(ring(px, dx, count), ring(py, dy, count)),
            device_id_type=MESH,
        )

    def remote(source, target, stage, index, where):
        return pltpu.make_async_remote_copy(
            src_ref=source,
            dst_ref=target,
            send_sem=send_sem.at[stage, index],
            recv_sem=recv_sem.at[stage, index],
            device_id=where,
            device_id_type=MESH,
        )

    def exchange(make):
        def start(d, carry):
            make(d).start()
            return carry

        lax.fori_loop(1, count, start, 0)

    def arrive(make):
        def wait(d, carry):
            make(d).wait()
            return carry

        lax.fori_loop(1, count, wait, 0)

    def side_copies(half):
        return [
            remote(
                halo_out.at[half, pl.ds(SIDE_AT[e], SIDE_ROWS[e])],
                halo_in.at[half, pl.ds(SIDE_AT[OPPOSITE[e]], SIDE_ROWS[e])],
                half,
                e,
                (ring(px, SIDES[e][0], count), ring(py, SIDES[e][1], count)),
            )
            for e in range(8)
        ]

    def column_copy(out, into, stage):
        def make(d):
            to = ring(py, d, count)
            return remote(out.at[:, to], into.at[:, py], stage, d, (px, to))

        return make

    def row_copy(out, into, stage, layers):
        def make(d):
            to = ring(px, d, count)
            return remote(out.at[layers, to], into.at[layers, px], stage, d, (to, py))

        return make

    main, extra = pl.ds(0, 2), pl.ds(2, 1)

    def green_copy():
        return remote(green_last_ref, green_in, 8, 0, (px, 0))

    def rows(dim):
        base = base_ref[dim : dim + 1, :]
        cells = [base + offset for offset in range(4)]
        if dim == 2:
            cells = [jnp.where(c >= 256, c - 256, c) for c in cells]
        return cells, [spline_ref[4 * dim + o : 4 * dim + o + 1, :] for o in range(4)]

    z_cells = lax.broadcasted_iota(jnp.int32, (256, 1024), 0)
    high, low = split(profile(z_cells, *rows(2)))
    prof_h[...] = high
    prof_l[...] = low
    sixteen = lax.broadcasted_iota(jnp.int32, (16, 1024), 0)
    eight = lax.broadcasted_iota(jnp.int32, (8, 1024), 0)
    edge = jnp.where(eight < 2, eight, eight + 16)
    in_x, in_y = (profile(sixteen + 2, *rows(dim)) for dim in (0, 1))
    edge_x, edge_y = (profile(edge, *rows(dim)) for dim in (0, 1))
    for y in range(16):
        plane[16 * y : 16 * y + 16, :] = in_y[y : y + 1, :] * in_x
    for i in range(4):
        at = 256 + 32 * (i // 2) + 16 * (i % 2)
        plane[at : at + 16, :] = edge_x[i : i + 1, :] * in_y
        plane[at + 64 : at + 80, :] = edge_y[i : i + 1, :] * in_x
    corner = sixteen < 4
    corner_x = [
        profile(jnp.where(corner, sixteen // 2 + begin, 99), *rows(0)) for begin in (0, 18)
    ]
    corner_y = [
        profile(jnp.where(corner, sixteen % 2 + begin, 99), *rows(1)) for begin in (0, 18)
    ]
    for e in range(4):
        at = 256 + SIDE_AT[4 + e]
        plane[at : at + 16, :] = corner_x[e // 2] * corner_y[e % 2]

    high, low = split(plane[...] * charges_ref[...])
    spread = dot(high, prof_h[...], NT) + dot(low, prof_h[...], NT) + dot(high, prof_l[...], NT)
    halo_out[0] = spread[256:].astype(jnp.bfloat16)
    pl.semaphore_wait(barrier, 34)
    copies = side_copies(0)
    for copy in copies:
        copy.start()

    @pl.when(py == 8)
    def _():
        green_copy().start()

    for copy in copies:
        copy.wait()
    high, low = split(spread[:256] + dot(fold_ref[...], halo_in[0]))

    lines = dot(ahead_h[...], high, NT) + dot(ahead_l[...], high, NT) + dot(ahead_h[...], low, NT)
    halves = [
        swap_groups(lines[:, 128 * half : 128 * half + 128].reshape(32, 8, 128)) for half in (0, 1)
    ]
    z_out[...] = jnp.concatenate(halves, axis=1).astype(jnp.bfloat16).reshape(2, 16, 16, 128)
    make = column_copy(z_out, z_in, 2)
    exchange(make)
    z_in[:, pl.ds(py, 1)] = z_out[:, pl.ds(py, 1)]
    arrive(make)

    cos_h, sin_h = wave_h[:256], wave_h[256:]
    cos_l, sin_l = wave_l[:256], wave_l[256:]
    both = jnp.concatenate([z_in[0].reshape(256, 128), z_in[1].reshape(256, 128)], axis=1)
    both = jnp.transpose(both.astype(jnp.float32)).astype(jnp.bfloat16)
    c = dot(both, cos_h) + dot(both, cos_l)
    s = dot(both, sin_h) + dot(both, sin_l)
    apart = (lax.broadcasted_iota(jnp.int32, (128, 256), 0) < 16) & (py == 0)
    real = c[:128] + jnp.where(apart, 0.0, s[128:])
    imag = jnp.where(apart, 0.0, c[128:]) - s[:128]

    def to_slots(values, layer):
        for half in (0, 1):
            lanes = slice(128 * half, 128 * half + 128)
            done = regroup([values[16 * i : 16 * i + 16, lanes] for i in range(8)])
            for i in range(8):
                y_out[layer, 8 * half + i] = done[i].astype(jnp.bfloat16)

    to_slots(real, 0)
    to_slots(imag, 1)
    make = row_copy(y_out, y_in, 3, main)
    exchange(make)
    y_in[0:2, pl.ds(px, 1)] = y_out[0:2, pl.ds(px, 1)]

    @pl.when(py == 0)
    def _():
        blank = jnp.zeros((96, 256), jnp.float32)
        to_slots(jnp.concatenate([c[128:144], -s[128:144], blank], axis=0), 2)
        exchange(row_copy(y_out, y_in, 4, extra))
        y_in[2:3, pl.ds(px, 1)] = y_out[2:3, pl.ds(px, 1)]

    arrive(make)

    def forward_x(values):
        return dot(cos_h, values) + dot(cos_l, values), dot(sin_h, values) + dot(sin_l, values)

    def inverse_x(values):
        high, low = split(values)
        return (
            dot(cos_h, high) + dot(cos_l, high) + dot(cos_h, low),
            dot(sin_h, high) + dot(sin_l, high) + dot(sin_h, low),
        )

    c, s = forward_x(
        jnp.concatenate([y_in[0].reshape(256, 128), y_in[1].reshape(256, 128)], axis=1)
    )
    real = (c[:, :128] + s[:, 128:]) * green_ref[...]
    imag = (c[:, 128:] - s[:, :128]) * green_ref[...]
    c, s = inverse_x(jnp.concatenate([real, imag], axis=1))
    x_out[0] = (c[:, :128] - s[:, 128:]).astype(jnp.bfloat16).reshape(16, 16, 128)
    x_out[1] = (c[:, 128:] + s[:, :128]).astype(jnp.bfloat16).reshape(16, 16, 128)
    make = row_copy(x_out, x_in, 5, main)
    exchange(make)
    x_in[0:2, pl.ds(px, 1)] = x_out[0:2, pl.ds(px, 1)]

    @pl.when(py == 0)
    def _():
        arrive(row_copy(y_out, y_in, 4, extra))
        green_copy().wait_recv()
        first = lax.broadcasted_iota(jnp.int32, (256, 128), 1) < 16
        c, s = forward_x(y_in[2].reshape(256, 128))
        real = (c + pltpu.roll(s, 112, 1)) * green_in[...]
        imag = (pltpu.roll(c, 112, 1) - s) * green_in[...]
        c, s = inverse_x(real + pltpu.roll(imag, 16, 1))
        real = jnp.where(first, c - pltpu.roll(s, 112, 1), 0.0)
        imag = jnp.where(first, pltpu.roll(c, 112, 1) + s, 0.0)
        x_out[2] = (real + pltpu.roll(imag, 16, 1)).astype(jnp.bfloat16).reshape(16, 16, 128)
        back_copy = row_copy(x_out, x_in, 6, extra)
        exchange(back_copy)
        x_in[2:3, pl.ds(px, 1)] = x_out[2:3, pl.ds(px, 1)]

    @pl.when(py == 8)
    def _():
        green_copy().wait_send()

    arrive(make)

    def to_rows(layer):
        halves = [
            regroup([x_in[layer, 8 * half + i].astype(jnp.float32) for i in range(8)])
            for half in (0, 1)
        ]
        return [jnp.concatenate([halves[0][i], halves[1][i]], axis=1) for i in range(8)]

    real, imag = to_rows(0), to_rows(1)
    shared[0] = real[0]
    shared[1] = imag[0]

    @pl.when(py == 0)
    def _():
        arrive(row_copy(x_out, x_in, 6, extra))
        last = to_rows(2)
        shared[0] = -last[1]
        shared[1] = last[0]

    a = jnp.concatenate(real, axis=0).astype(jnp.bfloat16)
    b = jnp.concatenate(imag, axis=0).astype(jnp.bfloat16)
    a_too = jnp.concatenate([shared[0], *real[1:]], axis=0).astype(jnp.bfloat16)
    b_too = jnp.concatenate([shared[1], *imag[1:]], axis=0).astype(jnp.bfloat16)
    real = dot(cos_h, a, NT) + dot(cos_l, a, NT) - dot(sin_h, b, NT) - dot(sin_l, b, NT)
    imag = dot(cos_h, b_too, NT) + dot(cos_l, b_too, NT) + dot(sin_h, a_too, NT) + dot(sin_l, a_too, NT)
    v_out[0] = real.astype(jnp.bfloat16).reshape(16, 16, 128)
    v_out[1] = imag.astype(jnp.bfloat16).reshape(16, 16, 128)
    make = column_copy(v_out, v_in, 7)
    exchange(make)
    v_in[:, pl.ds(py, 1)] = v_out[:, pl.ds(py, 1)]
    arrive(make)

    got = v_in[...].reshape(32, 16, 128).astype(jnp.float32)
    halves = [swap_groups(got[:, 8 * half : 8 * half + 8]).reshape(256, 128) for half in (0, 1)]
    lines = jnp.concatenate(halves, axis=1).astype(jnp.bfloat16)
    grid = dot(lines, back_h[...], TN) + dot(lines, back_l[...], TN)
    grid_ref[...] = grid
    high, low = split(grid)
    halo_out[1] = dot(fold_ref[...], high, TN).astype(jnp.bfloat16)
    copies = side_copies(1)
    for copy in copies:
        copy.start()

    sampled = dot(high, prof_h[...]) + dot(low, prof_h[...]) + dot(high, prof_l[...])
    total = jnp.sum(sampled * plane[:256], axis=0, keepdims=True)
    for copy in copies:
        copy.wait()
    sampled = dot(halo_in[1], prof_h[...]) + dot(halo_in[1], prof_l[...])
    total = total + jnp.sum(sampled * plane[256:], axis=0, keepdims=True)
    inside = lax.broadcasted_iota(jnp.int32, (1, 1024), 1) < fill_ref[...]
    atom_ref[...] = jnp.where(inside, total, 0.0)


def mesh_potential(charges, fill, base_cells, spline_weights, green):
    vmem = pl.BlockSpec(memory_space=pltpu.VMEM)
    bf16, f32 = jnp.bfloat16, jnp.float32
    picked = jnp.where(lax.axis_index("gy") < 8, green[:, :, 0:8], green[:, :, 1:9])
    picked = jnp.transpose(picked, (0, 2, 1)).reshape(256, 128)
    last = jnp.pad(green[:, :, 0], ((0, 0), (0, 112)))
    blocks = (16, 16, 128)
    atom, grid = pl.pallas_call(
        mesh_kernel,
        out_shape=(
            jax.ShapeDtypeStruct((1, 1024), f32),
            jax.ShapeDtypeStruct((256, 256), f32),
        ),
        in_specs=[vmem] * 13,
        out_specs=(vmem, vmem),
        scratch_shapes=[
            pltpu.VMEM((448, 1024), f32),
            pltpu.VMEM((256, 1024), bf16),
            pltpu.VMEM((256, 1024), bf16),
            pltpu.VMEM((2, 192, 256), bf16),
            pltpu.VMEM((2, 192, 256), bf16),
            pltpu.VMEM((2, *blocks), bf16),
            pltpu.VMEM((2, *blocks), bf16),
            pltpu.VMEM((3, *blocks), bf16),
            pltpu.VMEM((3, *blocks), bf16),
            pltpu.VMEM((3, *blocks), bf16),
            pltpu.VMEM((3, *blocks), bf16),
            pltpu.VMEM((2, *blocks), bf16),
            pltpu.VMEM((2, *blocks), bf16),
            pltpu.VMEM((2, 16, 256), f32),
            pltpu.VMEM((256, 128), f32),
            pltpu.SemaphoreType.DMA((9, 16)),
            pltpu.SemaphoreType.DMA((9, 16)),
        ],
        compiler_params=pltpu.CompilerParams(
            collective_id=1, has_side_effects=True, vmem_limit_bytes=48 * 1024 * 1024
        ),
        name="mesh_potential",
    )(
        charges,
        fill,
        base_cells,
        spline_weights.reshape(12, 1024),
        picked,
        last,
        *(jnp.asarray(table) for table in mesh_tables()),
    )
    return atom, jnp.transpose(grid.reshape(16, 16, 256), (1, 0, 2))


def shards(
    node_feats,
    radial,
    neighbours,
    nbr_count,
    domain_count,
    base_cells,
    spline_weights,
    w_proj,
    w_radial,
    w_mix,
    w_charge,
    green_kernel,
):
    fill = jnp.broadcast_to(domain_count.reshape(1, 1), (1, 1024))
    charges = message_passing(
        node_feats, radial, neighbours, nbr_count, fill, w_proj, w_radial, w_mix, w_charge
    )
    atom_potential, potential = mesh_potential(
        charges, fill, base_cells, spline_weights, green_kernel
    )
    return (charges.reshape(1024), atom_potential.reshape(1024), potential)


def solution(mesh):
    return jax.shard_map(
        shards,
        mesh=mesh,
        in_specs=(
            P(("gx", "gy"), None),
            P(None, None, ("gx", "gy")),
            P(None, ("gx", "gy")),
            P(("gx", "gy")),
            P(("gx", "gy")),
            P(None, ("gx", "gy")),
            P(None, None, ("gx", "gy")),
            P(),
            P(),
            P(),
            P(),
            P(None, "gx", "gy"),
        ),
        out_specs=(P(("gx", "gy")), P(("gx", "gy")), P("gx", "gy", None)),
        check_vma=False,
    )
```

```python
import functools
import math

import jax
import jax.numpy as jnp
import ml_dtypes
import numpy as np
from jax import lax
from jax.experimental import pallas as pl
from jax.experimental.pallas import tpu as pltpu
from jax.sharding import PartitionSpec as P

K = 32
L = 2


MESH = pl.DeviceIdType.MESH
TN = (((0,), (0,)), ((), ()))
NT = (((1,), (1,)), ((), ()))
NN = (((1,), (0,)), ((), ()))


def dot(a, b, dims=NN):
    return lax.dot_general(a, b, dims, preferred_element_type=jnp.float32)


def ring(index, step, count):
    return lax.rem(index + step + count, count)


def message_kernel(
    num_x,
    num_y,
    feats_ref,
    radial_ref,
    nbr_ref,
    count_ref,
    fill_ref,
    proj_ref,
    filt_ref,
    mix_ref,
    charge_w_ref,
    charges_ref,
    state,
    table,
    rows_out,
    rows_in,
    head_a,
    head_b,
    pick,
    filt_k,
    total,
    send_sem,
    recv_sem,
):
    px, py = lax.axis_index("gx"), lax.axis_index("gy")
    barrier = pltpu.get_barrier_semaphore()
    peers = [(dx, dy) for dx in (-1, 0, 1) for dy in (-1, 0, 1) if (dx, dy) != (0, 0)]
    for dx, dy in peers:
        pl.semaphore_signal(
            barrier,
            inc=1,
            device_id=(ring(px, dx, num_x), ring(py, dy, num_y)),
            device_id_type=MESH,
        )
    code = nbr_ref[...]
    direction, slot = code // 1024, code % 1024
    lane = lax.broadcasted_iota(jnp.int32, (K, 1024), 1)
    live = lax.broadcasted_iota(jnp.int32, (K, 1024), 0) < count_ref[...]
    block = lane // 128
    near = slot - jnp.maximum(block - 1, 0) * 128
    far = jnp.where(
        direction < 3,
        192 + direction * 64 + slot,
        jnp.where(
            direction > 5,
            64 + direction * 64 + slot,
            jnp.where(direction == 3, 192 + slot, 320 + slot),
        ),
    )
    named = jnp.where(live, jnp.where(direction == 4, near, far), -8192).astype(jnp.float32)
    for b in range(8):
        pick[:, b, :] = named[:, b * 128 : (b + 1) * 128]

    state[...] = jnp.transpose(feats_ref[...].astype(jnp.float32))
    row_id = lax.broadcasted_iota(jnp.int32, (128, 128), 0).astype(jnp.bfloat16)
    one, zero = jnp.ones((128, 128), jnp.bfloat16), jnp.zeros((128, 128), jnp.bfloat16)
    basis_k = lax.broadcasted_iota(jnp.int32, (128, 8 * K), 1) % K

    def onehot(k, begin, groups):
        row = pick[k, begin // 128 : begin // 128 + 1, :]
        parts = [
            jnp.where(row_id == jnp.broadcast_to((row - 128.0 * g).astype(jnp.bfloat16), (128, 128)), one, zero)
            for g in range(groups)
        ]
        return jnp.concatenate(parts, axis=0)

    def messages(group, tables):
        begin = group * 256
        radial = radial_ref[:, begin : begin + 256]
        total[...] = jnp.zeros_like(total)

        for k in range(0, K, 2):
            filters = dot(filt_k[k * 128 : k * 128 + 256, :], radial)
            for half, (source, groups) in enumerate(tables):
                at = begin + 128 * half
                hot = jnp.concatenate([onehot(k, at, groups), onehot(k + 1, at, groups)], axis=1)
                got = dot(source(), hot)
                lanes = slice(128 * half, 128 * half + 128)
                total[:, lanes] += (
                    got[:, :128] * filters[:128, lanes] + got[:, 128:] * filters[128:, lanes]
                )
        return (total[...] * (1.0 / math.sqrt(K))).astype(jnp.bfloat16)

    for layer in range(L):
        spread = jnp.concatenate(
            [jnp.broadcast_to(filt_ref[layer, b], (K, 128)) for b in range(8)], axis=0
        )
        spread = jnp.transpose(spread.astype(jnp.float32))
        for k in range(K):
            filt_k[k * 128 : (k + 1) * 128, :] = jnp.where(basis_k == k, spread, 0.0).astype(jnp.bfloat16)
        proj = proj_ref[layer]
        first = dot(proj, state[:, :256].astype(jnp.bfloat16), TN).astype(jnp.bfloat16)
        rows_out[layer] = jnp.transpose(first.astype(jnp.float32)).astype(jnp.bfloat16)
        if layer == 0:
            pl.semaphore_wait(barrier, 8)
        copies = []
        for dx, dy in peers:
            if dx == 1:
                band, land = 1, 1 - dy
            elif dx == -1:
                band, land = 0, 4 - dy
            elif dy == 1:
                band, land = 3, 6
            else:
                band, land = 2, 7
            copies.append(
                pltpu.make_async_remote_copy(
                    src_ref=rows_out.at[layer, pl.ds(band * 64, 64)],
                    dst_ref=rows_in.at[layer, pl.ds(land * 64, 64)],
                    send_sem=send_sem.at[layer, land],
                    recv_sem=recv_sem.at[layer, land],
                    device_id=(ring(px, dx, num_x), ring(py, dy, num_y)),
                    device_id_type=MESH,
                )
            )
            copies[-1].start()
        table[:, :256] = first
        table[:, 256:] = dot(proj, state[:, 256:].astype(jnp.bfloat16), TN).astype(jnp.bfloat16)

        def update(group, tables):
            begin = group * 256
            u = messages(group, tables)
            mixed = dot(mix_ref[layer], u, TN)
            lanes = slice(begin, begin + 256)
            state[:, lanes] = (
                (state[:, lanes] + mixed / (1.0 + jnp.exp(-mixed))).astype(jnp.bfloat16).astype(jnp.float32)
            )

        def window(block):
            low = max(block - 1, 0) * 128
            high = min(block + 2, 8) * 128
            return (lambda: table[:, low:high]), (high - low) // 128

        for group in (1, 2, 3):
            update(group, [window(2 * group), window(2 * group + 1)])
        for copy in copies:
            copy.wait()
        far_rows = jnp.transpose(rows_in[layer].astype(jnp.float32)).astype(jnp.bfloat16)
        head_a[:, :256] = table[:, :256]
        head_a[:, 256:] = far_rows[:, :384]
        head_b[:, :384] = table[:, :384]
        head_b[:, 384:] = far_rows[:, 384:]
        update(0, [((lambda: head_a[...]), 5), ((lambda: head_b[...]), 4)])
    charge = dot(charge_w_ref[...], state[...].astype(jnp.bfloat16))[0:1]
    inside = lax.broadcasted_iota(jnp.int32, (1, 1024), 1) < fill_ref[...]
    charges_ref[...] = jnp.where(inside, charge, 0.0)


def message_passing(feats, radial, neighbours, nbr_count, fill, w_proj, w_radial, w_mix, w_charge):
    num_x, num_y = lax.axis_size("gx"), lax.axis_size("gy")
    vmem = pl.BlockSpec(memory_space=pltpu.VMEM)
    bf16 = jnp.bfloat16
    return pl.pallas_call(
        functools.partial(message_kernel, num_x, num_y),
        out_shape=jax.ShapeDtypeStruct((1, 1024), jnp.float32),
        in_specs=[vmem] * 9,
        out_specs=vmem,
        scratch_shapes=[
            pltpu.VMEM((128, 1024), jnp.float32),
            pltpu.VMEM((128, 1024), bf16),
            pltpu.VMEM((L, 256, 128), bf16),
            pltpu.VMEM((L, 512, 128), bf16),
            pltpu.VMEM((128, 640), bf16),
            pltpu.VMEM((128, 512), bf16),
            pltpu.VMEM((K, 8, 128), jnp.float32),
            pltpu.VMEM((K * 128, 8 * K), bf16),
            pltpu.VMEM((128, 256), jnp.float32),
            pltpu.SemaphoreType.DMA((L, 8)),
            pltpu.SemaphoreType.DMA((L, 8)),
        ],
        compiler_params=pltpu.CompilerParams(
            collective_id=0, has_side_effects=True, vmem_limit_bytes=48 * 1024 * 1024
        ),
        name="message_passing",
    )(
        feats,
        radial.reshape(8 * K, 1024),
        neighbours,
        nbr_count.reshape(1, 1024),
        fill,
        w_proj,
        w_radial.reshape(L, 8, 1, 128),
        w_mix,
        jnp.broadcast_to(w_charge.reshape(1, 128), (8, 128)),
    )

def split(values):
    high = values.astype(jnp.bfloat16)
    return high, (values - high.astype(jnp.float32)).astype(jnp.bfloat16)


def np_split(values):
    high = values.astype(ml_dtypes.bfloat16)
    return high, (values - high.astype(np.float64)).astype(ml_dtypes.bfloat16)


def mesh_tables():
    ids = np.arange(256)
    angles = 2.0 * np.pi * (ids[:, None] * ids[None, :] % 256) / 256
    waves = np.concatenate([np.cos(angles), np.sin(angles)], axis=0)
    column, slot = np.arange(16)[:, None], np.arange(8)[None, :]
    kz = (16 * column + slot + (column >= 8)).reshape(128)
    turn = 2.0 * np.pi * (kz[:, None] * ids[None, :] % 256) / 256
    ahead = np.stack([np.cos(turn), -np.sin(turn)])
    back = 2.0 * ahead
    ahead[0, 0], ahead[1, 0] = 1.0, 1.0 - 2.0 * (ids % 2)
    back[0, 0], back[1, 0] = ahead[0, 0], ahead[1, 0]
    back = back / 256.0**3
    return (
        *np_split(waves),
        *np_split(ahead.reshape(256, 256)),
        *np_split(back.reshape(256, 256)),
    )


def regroup(parts):
    group = lax.broadcasted_iota(jnp.int32, parts[0].shape, 1) // 16
    parts = list(parts)
    for step in (1, 2, 4):
        low = (group & step) == 0
        for i in range(8):
            if i & step == 0:
                a, b = parts[i], parts[i | step]
                parts[i] = jnp.where(low, a, pltpu.roll(b, 16 * step, 1))
                parts[i | step] = jnp.where(low, pltpu.roll(a, 128 - 16 * step, 1), b)
    return parts


def swap_groups(values):
    row = lax.broadcasted_iota(jnp.int32, values.shape, 1)
    group = lax.broadcasted_iota(jnp.int32, values.shape, 2) // 16
    for step in (1, 2, 4):
        row_high, group_high = (row & step) != 0, (group & step) != 0
        if step == 4:
            moved = pltpu.roll(pltpu.roll(values, 4, 1), 64, 2)
        else:
            up = pltpu.roll(pltpu.roll(values, 8 - step, 1), 16 * step, 2)
            down = pltpu.roll(pltpu.roll(values, step, 1), 128 - 16 * step, 2)
            moved = jnp.where(row_high, down, up)
        values = jnp.where(row_high == group_high, values, moved)
    return values


def turned(values, step):
    return jnp.concatenate([values[step:], values[:step]], axis=0)


def fold_edges(edge):
    before, after = turned(edge, -1), turned(edge, 1)
    row = lax.broadcasted_iota(jnp.int32, edge.shape, 1)
    return [
        jnp.concatenate(
            [
                jnp.where(row < 2, pltpu.roll(before, step, 1), 0.0),
                jnp.where(row >= 6, pltpu.roll(after, step, 1), 0.0),
            ],
            axis=1,
        )
        for step in (6, 2)
    ]


def edges_of(real, imag):
    row = lax.broadcasted_iota(jnp.int32, (16, 8, 128), 1)
    ends = [
        pltpu.roll(part, step, 1)
        for values, step in ((real, 2), (imag, 6))
        for part in (turned(values, -1)[:, 8:], turned(values, 1)[:, :8])
    ]
    return jnp.where(
        row < 2, ends[0], jnp.where(row < 4, ends[1], jnp.where(row < 6, ends[2], ends[3]))
    )


def tile(low, high=None):
    high = jnp.zeros_like(low) if high is None else high
    return jnp.concatenate([low, high], axis=low.ndim - 2).astype(jnp.bfloat16)


def profile(cells, base, weights):
    total = jnp.zeros(cells.shape, jnp.float32)
    for offset in range(4):
        total = total + jnp.where(cells == base[offset], weights[offset], 0.0)
    return total


def mesh_kernel(
    charges_ref,
    fill_ref,
    base_ref,
    spline_ref,
    green_ref,
    green_last_ref,
    wave_h,
    wave_l,
    ahead_h,
    ahead_l,
    back_h,
    back_l,
    atom_ref,
    grid_ref,
    plane,
    prof_h,
    prof_l,
    z_out,
    z_in,
    y_out,
    y_in,
    x_out,
    x_in,
    v_out,
    v_in,
    shared,
    shared_edge,
    green_in,
    send_sem,
    recv_sem,
):
    count = 16
    px, py = lax.axis_index("gx"), lax.axis_index("gy")
    barrier = pltpu.get_barrier_semaphore()

    def greet(d, carry):
        for where in ((ring(px, d, count), py), (px, ring(py, d, count))):
            pl.semaphore_signal(barrier, inc=1, device_id=where, device_id_type=MESH)
        return carry

    lax.fori_loop(1, count, greet, 0)
    def remote(source, target, stage, index, where):
        return pltpu.make_async_remote_copy(
            src_ref=source,
            dst_ref=target,
            send_sem=send_sem.at[stage, index],
            recv_sem=recv_sem.at[stage, index],
            device_id=where,
            device_id_type=MESH,
        )

    def exchange(make):
        def start(d, carry):
            make(d).start()
            return carry

        lax.fori_loop(1, count, start, 0)

    def arrive(make):
        def wait(d, carry):
            make(d).wait()
            return carry

        lax.fori_loop(1, count, wait, 0)

    def column_copy(out, into, stage):
        def make(d):
            to = ring(py, d, count)
            return remote(out.at[:, to], into.at[:, py], stage, d, (px, to))

        return make

    def row_copy(out, into, stage, layers):
        def make(d):
            to = ring(px, d, count)
            return remote(out.at[layers, to], into.at[layers, px], stage, d, (to, py))

        return make

    main, extra = pl.ds(0, 3), pl.ds(3, 2)

    def green_copy():
        return remote(green_last_ref, green_in, 8, 0, (px, 0))

    def rows(dim):
        base = base_ref[dim : dim + 1, :]
        cells = [base + offset for offset in range(4)]
        if dim == 2:
            cells = [jnp.where(c >= 256, c - 256, c) for c in cells]
        return cells, [spline_ref[4 * dim + o : 4 * dim + o + 1, :] for o in range(4)]

    z_cells = lax.broadcasted_iota(jnp.int32, (256, 1024), 0)
    high, low = split(profile(z_cells, *rows(2)))
    prof_h[...] = high
    prof_l[...] = low
    sixteen = lax.broadcasted_iota(jnp.int32, (16, 1024), 0)
    eight = lax.broadcasted_iota(jnp.int32, (8, 1024), 0)
    edge = jnp.where(eight < 2, eight, eight + 16)
    in_x, in_y = (profile(sixteen + 2, *rows(dim)) for dim in (0, 1))
    edge_x, edge_y = (profile(edge, *rows(dim)) for dim in (0, 1))
    for y in range(16):
        plane[16 * y : 16 * y + 16, :] = in_y[y : y + 1, :] * in_x
    for y in range(16):
        plane[256 + 8 * y : 264 + 8 * y, :] = in_y[y : y + 1, :] * edge_x
    for i in range(4):
        plane[384 + 16 * i : 400 + 16 * i, :] = edge_y[i : i + 1, :] * in_x
        plane[448 + 8 * i : 456 + 8 * i, :] = edge_y[i : i + 1, :] * edge_x

    high, low = split(plane[...] * charges_ref[...])
    spread = dot(high, prof_h[...], NT) + dot(low, prof_h[...], NT) + dot(high, prof_l[...], NT)
    edges = spread[256:]
    edges = [
        tile(edges[:128].reshape(16, 8, 256)).reshape(256, 256),
        tile(edges[128:192]),
        tile(tile(edges[192:].reshape(4, 8, 256)).reshape(64, 256)),
    ]
    edges = jnp.concatenate(edges, axis=0)
    high, low = split(spread[:256])

    lines = dot(ahead_h[...], high, NT) + dot(ahead_l[...], high, NT) + dot(ahead_h[...], low, NT)
    halves = [
        swap_groups(lines[:, 128 * half : 128 * half + 128].reshape(32, 8, 128)) for half in (0, 1)
    ]
    z_out[0:2] = jnp.concatenate(halves, axis=1).astype(jnp.bfloat16).reshape(2, 16, 16, 128)
    lines = dot(ahead_h[...], edges, NT) + dot(ahead_l[...], edges, NT)
    real, imag = lines[:128], lines[128:]
    sides = real[:, :256] + pltpu.roll(imag[:, :256], 4, 1)
    ends = real[:, 256:384] + pltpu.roll(imag[:, 256:384], 64, 1)
    corners = real[:, 384:] + pltpu.roll(imag[:, 384:], 4, 1)
    pieces = [
        swap_groups(part.reshape(16, 8, 128))
        for part in (sides[:, :128], sides[:, 128:], ends, corners)
    ]
    z_out[2] = tile(pieces[0], pieces[1])
    z_out[3] = tile(pieces[2], pieces[3])
    pl.semaphore_wait(barrier, 30)
    make = column_copy(z_out, z_in, 2)
    exchange(make)

    @pl.when(py == 8)
    def _():
        green_copy().start()

    z_in[:, pl.ds(py, 1)] = z_out[:, pl.ds(py, 1)]
    arrive(make)

    cos_h, sin_h = wave_h[:256], wave_h[256:]
    cos_l, sin_l = wave_l[:256], wave_l[256:]
    ends = z_in[3].astype(jnp.float32)
    adds = [*fold_edges(ends[:, :8]), fold_edges(ends[:, 8:])[0]]
    both = jnp.concatenate(
        [(z_in[i].astype(jnp.float32) + adds[i]).reshape(256, 128) for i in range(3)], axis=1
    )
    both = jnp.transpose(both).astype(jnp.bfloat16)
    c = dot(both, cos_h) + dot(both, cos_l)
    s = dot(both, sin_h) + dot(both, sin_l)
    apart = (lax.broadcasted_iota(jnp.int32, (128, 256), 0) < 16) & (py == 0)
    real = c[:128] + jnp.where(apart, 0.0, s[128:256])
    imag = jnp.where(apart, 0.0, c[128:256]) - s[:128]

    c_edge, s_edge = (v[256:].reshape(8, 16, 256)[:, :8] for v in (c, s))
    c_swap, s_swap = pltpu.roll(c_edge, 4, 1), pltpu.roll(s_edge, 4, 1)
    top = lax.broadcasted_iota(jnp.int32, (8, 8, 256), 1) < 4
    apart = (lax.broadcasted_iota(jnp.int32, (8, 8, 256), 0) == 0) & (py == 0)
    edge = jnp.where(
        top,
        c_edge + jnp.where(apart, 0.0, s_swap),
        jnp.where(apart, 0.0, c_edge) - s_swap,
    )

    def to_slots(values, layer):
        for half in (0, 1):
            lanes = slice(128 * half, 128 * half + 128)
            done = regroup([v[:, lanes] for v in values])
            for i in range(8):
                whole = done[i].shape[0] == 16
                y_out[layer, 8 * half + i] = done[i].astype(jnp.bfloat16) if whole else tile(done[i])

    to_slots([real[16 * i : 16 * i + 16] for i in range(8)], 0)
    to_slots([imag[16 * i : 16 * i + 16] for i in range(8)], 1)
    to_slots([edge[i] for i in range(8)], 2)
    make = row_copy(y_out, y_in, 3, main)
    exchange(make)
    y_in[0:3, pl.ds(px, 1)] = y_out[0:3, pl.ds(px, 1)]

    @pl.when(py == 0)
    def _():
        blank = jnp.zeros((16, 256), jnp.float32)
        to_slots([c[128:144], -s[128:144]] + [blank] * 6, 3)
        to_slots([jnp.where(top[0], c_swap[0], -s_edge[0])] + [blank[:8]] * 7, 4)
        exchange(row_copy(y_out, y_in, 4, extra))
        y_in[3:5, pl.ds(px, 1)] = y_out[3:5, pl.ds(px, 1)]

    arrive(make)

    def forward_x(values):
        return dot(cos_h, values) + dot(cos_l, values), dot(sin_h, values) + dot(sin_l, values)

    def inverse_x(values):
        high, low = split(values)
        return (
            dot(cos_h, high) + dot(cos_l, high) + dot(cos_h, low),
            dot(sin_h, high) + dot(sin_l, high) + dot(sin_h, low),
        )

    adds = fold_edges(y_in[2].astype(jnp.float32)[:, :8])
    c, s = forward_x(
        jnp.concatenate(
            [(y_in[i].astype(jnp.float32) + adds[i]).reshape(256, 128) for i in range(2)], axis=1
        ).astype(jnp.bfloat16)
    )
    real = (c[:, :128] + s[:, 128:]) * green_ref[...]
    imag = (c[:, 128:] - s[:, :128]) * green_ref[...]
    c, s = inverse_x(jnp.concatenate([real, imag], axis=1))
    real = (c[:, :128] - s[:, 128:]).reshape(16, 16, 128)
    imag = (c[:, 128:] + s[:, :128]).reshape(16, 16, 128)
    x_out[0] = real.astype(jnp.bfloat16)
    x_out[1] = imag.astype(jnp.bfloat16)
    x_out[2] = tile(edges_of(real, imag))
    make = row_copy(x_out, x_in, 5, main)
    exchange(make)
    x_in[0:3, pl.ds(px, 1)] = x_out[0:3, pl.ds(px, 1)]

    @pl.when(py == 0)
    def _():
        arrive(row_copy(y_out, y_in, 4, extra))
        green_copy().wait_recv()
        first = lax.broadcasted_iota(jnp.int32, (256, 128), 1) < 16
        adds = fold_edges(y_in[4].astype(jnp.float32)[:, :8])
        last = y_in[3].astype(jnp.float32) + adds[0] + pltpu.roll(adds[1], 16, 2)
        c, s = forward_x(last.reshape(256, 128).astype(jnp.bfloat16))
        real = (c + pltpu.roll(s, 112, 1)) * green_in[...]
        imag = (pltpu.roll(c, 112, 1) - s) * green_in[...]
        c, s = inverse_x(real + pltpu.roll(imag, 16, 1))
        real = jnp.where(first, c - pltpu.roll(s, 112, 1), 0.0)
        imag = jnp.where(first, pltpu.roll(c, 112, 1) + s, 0.0)
        x_out[3] = (real + pltpu.roll(imag, 16, 1)).astype(jnp.bfloat16).reshape(16, 16, 128)
        x_out[4] = tile(edges_of(real.reshape(16, 16, 128), imag.reshape(16, 16, 128)))
        back_copy = row_copy(x_out, x_in, 6, extra)
        exchange(back_copy)
        x_in[3:5, pl.ds(px, 1)] = x_out[3:5, pl.ds(px, 1)]

    @pl.when(py == 8)
    def _():
        green_copy().wait_send()

    arrive(make)

    def to_rows(layer, count=16):
        halves = [
            regroup([x_in[layer, 8 * half + i].astype(jnp.float32)[:count] for i in range(8)])
            for half in (0, 1)
        ]
        return [jnp.concatenate([halves[0][i], halves[1][i]], axis=1) for i in range(8)]

    real, imag, edge = to_rows(0), to_rows(1), to_rows(2, 8)
    shared[0] = real[0]
    shared[1] = imag[0]
    shared_edge[...] = edge[0]

    @pl.when(py == 0)
    def _():
        arrive(row_copy(x_out, x_in, 6, extra))
        last = to_rows(3)
        shared[0] = -last[1]
        shared[1] = last[0]
        last = pltpu.roll(to_rows(4, 8)[0], 4, 0)
        shared_edge[...] = jnp.where(top[0], -last, last)

    a = jnp.concatenate(real, axis=0).astype(jnp.bfloat16)
    b = jnp.concatenate(imag, axis=0).astype(jnp.bfloat16)
    a_too = jnp.concatenate([shared[0], *real[1:]], axis=0).astype(jnp.bfloat16)
    b_too = jnp.concatenate([shared[1], *imag[1:]], axis=0).astype(jnp.bfloat16)
    real = dot(cos_h, a, NT) + dot(cos_l, a, NT) - dot(sin_h, b, NT) - dot(sin_l, b, NT)
    imag = dot(cos_h, b_too, NT) + dot(cos_l, b_too, NT) + dot(sin_h, a_too, NT) + dot(sin_l, a_too, NT)
    sides = []
    for first in (edge[0], shared_edge[...]):
        rows = jnp.concatenate([tile(v) for v in [first, *edge[1:]]], axis=0)
        sides.append(
            (
                dot(cos_h, rows, NT) + dot(cos_l, rows, NT),
                dot(sin_h, rows, NT) + dot(sin_l, rows, NT),
            )
        )
    within = lax.broadcasted_iota(jnp.int32, (256, 128), 1) % 16
    sides = jnp.where(
        within < 4,
        sides[0][0] - pltpu.roll(sides[0][1], 124, 1),
        sides[1][0] + pltpu.roll(sides[1][1], 4, 1),
    )
    sides = jnp.where(within < 8, sides, 0.0).reshape(16, 16, 128)
    real, imag = real.reshape(16, 16, 128), imag.reshape(16, 16, 128)
    v_out[0] = real.astype(jnp.bfloat16)
    v_out[1] = imag.astype(jnp.bfloat16)
    v_out[2] = sides.astype(jnp.bfloat16)
    v_out[3] = tile(edges_of(real, imag), edges_of(sides, sides))
    make = column_copy(v_out, v_in, 7)
    exchange(make)
    v_in[:, pl.ds(py, 1)] = v_out[:, pl.ds(py, 1)]
    arrive(make)

    def to_lines(values):
        return swap_groups(values).reshape(-1, 128)

    got = v_in[0:2].reshape(32, 16, 128).astype(jnp.float32)
    lines = jnp.concatenate([to_lines(got[:, :8]), to_lines(got[:, 8:])], axis=1).astype(jnp.bfloat16)
    grid = dot(lines, back_h[...], TN) + dot(lines, back_l[...], TN)
    grid_ref[...] = grid
    got = v_in[2:4].reshape(32, 16, 128).astype(jnp.float32)
    sides = jnp.concatenate([to_lines(got[:16, :8]), to_lines(got[:16, 8:])], axis=1)
    ends, corners = to_lines(got[16:, :8]), to_lines(got[16:, 8:])
    lines = jnp.concatenate(
        [
            jnp.concatenate([sides, ends, corners], axis=1),
            jnp.concatenate(
                [pltpu.roll(sides, 252, 1), pltpu.roll(ends, 64, 1), pltpu.roll(corners, 124, 1)],
                axis=1,
            ),
        ],
        axis=0,
    ).astype(jnp.bfloat16)
    edges = dot(lines, back_h[...], TN) + dot(lines, back_l[...], TN)

    values = jnp.concatenate(
        [
            grid,
            edges[:256].reshape(16, 16, 256)[:, :8].reshape(128, 256),
            edges[256:320],
            edges[384:448].reshape(4, 16, 256)[:, :8].reshape(32, 256),
        ],
        axis=0,
    )
    high, low = split(values)
    sampled = dot(high, prof_h[...]) + dot(low, prof_h[...]) + dot(high, prof_l[...])
    total = jnp.sum(sampled * plane[...], axis=0, keepdims=True)
    inside = lax.broadcasted_iota(jnp.int32, (1, 1024), 1) < fill_ref[...]
    atom_ref[...] = jnp.where(inside, total, 0.0)


def mesh_potential(charges, fill, base_cells, spline_weights, green):
    vmem = pl.BlockSpec(memory_space=pltpu.VMEM)
    bf16, f32 = jnp.bfloat16, jnp.float32
    picked = jnp.where(lax.axis_index("gy") < 8, green[:, :, 0:8], green[:, :, 1:9])
    picked = jnp.transpose(picked, (0, 2, 1)).reshape(256, 128)
    last = jnp.pad(green[:, :, 0], ((0, 0), (0, 112)))
    blocks = (16, 16, 128)
    atom, grid = pl.pallas_call(
        mesh_kernel,
        out_shape=(
            jax.ShapeDtypeStruct((1, 1024), f32),
            jax.ShapeDtypeStruct((256, 256), f32),
        ),
        in_specs=[vmem] * 12,
        out_specs=(vmem, vmem),
        scratch_shapes=[
            pltpu.VMEM((480, 1024), f32),
            pltpu.VMEM((256, 1024), bf16),
            pltpu.VMEM((256, 1024), bf16),
            pltpu.VMEM((4, *blocks), bf16),
            pltpu.VMEM((4, *blocks), bf16),
            pltpu.VMEM((5, *blocks), bf16),
            pltpu.VMEM((5, *blocks), bf16),
            pltpu.VMEM((5, *blocks), bf16),
            pltpu.VMEM((5, *blocks), bf16),
            pltpu.VMEM((4, *blocks), bf16),
            pltpu.VMEM((4, *blocks), bf16),
            pltpu.VMEM((2, 16, 256), f32),
            pltpu.VMEM((8, 256), f32),
            pltpu.VMEM((256, 128), f32),
            pltpu.SemaphoreType.DMA((9, 16)),
            pltpu.SemaphoreType.DMA((9, 16)),
        ],
        compiler_params=pltpu.CompilerParams(
            collective_id=1, has_side_effects=True, vmem_limit_bytes=48 * 1024 * 1024
        ),
        name="mesh_potential",
    )(
        charges,
        fill,
        base_cells,
        spline_weights.reshape(12, 1024),
        picked,
        last,
        *(jnp.asarray(table) for table in mesh_tables()),
    )
    return atom, jnp.transpose(grid.reshape(16, 16, 256), (1, 0, 2))


def shards(
    node_feats,
    radial,
    neighbours,
    nbr_count,
    domain_count,
    base_cells,
    spline_weights,
    w_proj,
    w_radial,
    w_mix,
    w_charge,
    green_kernel,
):
    fill = jnp.broadcast_to(domain_count.reshape(1, 1), (1, 1024))
    charges = message_passing(
        node_feats, radial, neighbours, nbr_count, fill, w_proj, w_radial, w_mix, w_charge
    )
    atom_potential, potential = mesh_potential(
        charges, fill, base_cells, spline_weights, green_kernel
    )
    return (charges.reshape(1024), atom_potential.reshape(1024), potential)


def solution(mesh):
    return jax.shard_map(
        shards,
        mesh=mesh,
        in_specs=(
            P(("gx", "gy"), None),
            P(None, None, ("gx", "gy")),
            P(None, ("gx", "gy")),
            P(("gx", "gy")),
            P(("gx", "gy")),
            P(None, ("gx", "gy")),
            P(None, None, ("gx", "gy")),
            P(),
            P(),
            P(),
            P(),
            P(None, "gx", "gy"),
        ),
        out_specs=(P(("gx", "gy")), P(("gx", "gy")), P("gx", "gy", None)),
        check_vma=False,
    )
```

```python
import math

import jax
import jax.numpy as jnp
import ml_dtypes
import numpy as np
from jax import lax
from jax.experimental import pallas as pl
from jax.experimental.pallas import tpu as pltpu
from jax.sharding import PartitionSpec as P

K = 32
L = 2


MESH = pl.DeviceIdType.MESH
TN = (((0,), (0,)), ((), ()))
NT = (((1,), (1,)), ((), ()))
NN = (((1,), (0,)), ((), ()))


def dot(a, b, dims=NN):
    return lax.dot_general(a, b, dims, preferred_element_type=jnp.float32)


def ring(index, step, count):
    return lax.rem(index + step + count, count)


def message_stage(
    enter,
    idle,
    feats_ref,
    radial_ref,
    nbr_ref,
    count_ref,
    fill_ref,
    proj_ref,
    filt_ref,
    mix_ref,
    charge_w_ref,
    charges_ref,
    state,
    table,
    rows_out,
    rows_in,
    head_a,
    head_b,
    pick,
    filt_k,
    total,
    send_sem,
    recv_sem,
):
    px, py = lax.axis_index("gx"), lax.axis_index("gy")
    num_x = num_y = 16
    peers = [(dx, dy) for dx in (-1, 0, 1) for dy in (-1, 0, 1) if (dx, dy) != (0, 0)]
    code = nbr_ref[...]
    direction, slot = code // 1024, code % 1024
    lane = lax.broadcasted_iota(jnp.int32, (K, 1024), 1)
    live = lax.broadcasted_iota(jnp.int32, (K, 1024), 0) < count_ref[...]
    block = lane // 128
    near = slot - jnp.maximum(block - 1, 0) * 128
    far = jnp.where(
        direction < 3,
        192 + direction * 64 + slot,
        jnp.where(
            direction > 5,
            64 + direction * 64 + slot,
            jnp.where(direction == 3, 192 + slot, 320 + slot),
        ),
    )
    named = jnp.where(live, jnp.where(direction == 4, near, far), -8192).astype(jnp.float32)
    for b in range(8):
        pick[:, b, :] = named[:, b * 128 : (b + 1) * 128]

    state[...] = jnp.transpose(feats_ref[...].astype(jnp.float32))
    row_id = lax.broadcasted_iota(jnp.int32, (128, 128), 0).astype(jnp.bfloat16)
    one, zero = jnp.ones((128, 128), jnp.bfloat16), jnp.zeros((128, 128), jnp.bfloat16)
    basis_k = lax.broadcasted_iota(jnp.int32, (128, 8 * K), 1) % K

    def onehot(k, begin, groups):
        row = pick[k, begin // 128 : begin // 128 + 1, :]
        parts = [
            jnp.where(row_id == jnp.broadcast_to((row - 128.0 * g).astype(jnp.bfloat16), (128, 128)), one, zero)
            for g in range(groups)
        ]
        return jnp.concatenate(parts, axis=0)

    def messages(group, tables):
        begin = group * 256
        radial = radial_ref[:, begin : begin + 256]
        total[...] = jnp.zeros_like(total)

        for k in range(0, K, 2):
            filters = dot(filt_k[k * 128 : k * 128 + 256, :], radial)
            for half, (source, groups) in enumerate(tables):
                at = begin + 128 * half
                hot = jnp.concatenate([onehot(k, at, groups), onehot(k + 1, at, groups)], axis=1)
                got = dot(source(), hot)
                lanes = slice(128 * half, 128 * half + 128)
                total[:, lanes] += (
                    got[:, :128] * filters[:128, lanes] + got[:, 128:] * filters[128:, lanes]
                )
        return (total[...] * (1.0 / math.sqrt(K))).astype(jnp.bfloat16)

    for layer in range(L):
        spread = jnp.concatenate(
            [jnp.broadcast_to(filt_ref[layer, b : b + 1], (K, 128)) for b in range(8)], axis=0
        )
        spread = jnp.transpose(spread.astype(jnp.float32))
        for k in range(K):
            filt_k[k * 128 : (k + 1) * 128, :] = jnp.where(basis_k == k, spread, 0.0).astype(jnp.bfloat16)
        proj = proj_ref[layer]
        first = dot(proj, state[:, :256].astype(jnp.bfloat16), TN).astype(jnp.bfloat16)
        rows_out[layer] = jnp.transpose(first.astype(jnp.float32)).astype(jnp.bfloat16)
        if layer == 0:
            enter()
        copies = []
        for dx, dy in peers:
            if dx == 1:
                band, land = 1, 1 - dy
            elif dx == -1:
                band, land = 0, 4 - dy
            elif dy == 1:
                band, land = 3, 6
            else:
                band, land = 2, 7
            copies.append(
                pltpu.make_async_remote_copy(
                    src_ref=rows_out.at[layer, pl.ds(band * 64, 64)],
                    dst_ref=rows_in.at[layer, pl.ds(land * 64, 64)],
                    send_sem=send_sem.at[layer, land],
                    recv_sem=recv_sem.at[layer, land],
                    device_id=(ring(px, dx, num_x), ring(py, dy, num_y)),
                    device_id_type=MESH,
                )
            )
            copies[-1].start()
        table[:, :256] = first
        table[:, 256:] = dot(proj, state[:, 256:].astype(jnp.bfloat16), TN).astype(jnp.bfloat16)

        def update(group, tables):
            begin = group * 256
            u = messages(group, tables)
            mixed = dot(mix_ref[layer], u, TN)
            lanes = slice(begin, begin + 256)
            state[:, lanes] = (
                (state[:, lanes] + mixed / (1.0 + jnp.exp(-mixed))).astype(jnp.bfloat16).astype(jnp.float32)
            )

        def window(block):
            low = max(block - 1, 0) * 128
            high = min(block + 2, 8) * 128
            return (lambda: table[:, low:high]), (high - low) // 128

        for group in (1, 2, 3):
            update(group, [window(2 * group), window(2 * group + 1)])
        idle[layer]()
        for copy in copies:
            copy.wait()
        far_rows = jnp.transpose(rows_in[layer].astype(jnp.float32)).astype(jnp.bfloat16)
        head_a[:, :256] = table[:, :256]
        head_a[:, 256:] = far_rows[:, :384]
        head_b[:, :384] = table[:, :384]
        head_b[:, 384:] = far_rows[:, 384:]
        update(0, [((lambda: head_a[...]), 5), ((lambda: head_b[...]), 4)])
    charge = dot(jnp.broadcast_to(charge_w_ref[...], (8, 128)), state[...].astype(jnp.bfloat16))[0:1]
    inside = lax.broadcasted_iota(jnp.int32, (1, 1024), 1) < fill_ref[0]
    charges_ref[...] = jnp.where(inside, charge, 0.0)


def split(values):
    high = values.astype(jnp.bfloat16)
    return high, (values - high.astype(jnp.float32)).astype(jnp.bfloat16)


def np_split(values):
    high = values.astype(ml_dtypes.bfloat16)
    return high, (values - high.astype(np.float64)).astype(ml_dtypes.bfloat16)


def mesh_tables():
    ids = np.arange(256)
    angles = 2.0 * np.pi * (ids[:, None] * ids[None, :] % 256) / 256
    waves = np.concatenate([np.cos(angles), np.sin(angles)], axis=0)
    column, slot = np.arange(16)[:, None], np.arange(8)[None, :]
    kz = (16 * column + slot + (column >= 8)).reshape(128)
    turn = 2.0 * np.pi * (kz[:, None] * ids[None, :] % 256) / 256
    ahead = np.stack([np.cos(turn), -np.sin(turn)])
    back = 2.0 * ahead
    ahead[0, 0], ahead[1, 0] = 1.0, 1.0 - 2.0 * (ids % 2)
    back[0, 0], back[1, 0] = ahead[0, 0], ahead[1, 0]
    back = back / 256.0**3
    return (
        *np_split(waves),
        *np_split(ahead.reshape(256, 256)),
        *np_split(back.reshape(256, 256)),
    )


def regroup(parts):
    group = lax.broadcasted_iota(jnp.int32, parts[0].shape, 1) // 16
    parts = list(parts)
    for step in (1, 2, 4):
        low = (group & step) == 0
        for i in range(8):
            if i & step == 0:
                a, b = parts[i], parts[i | step]
                parts[i] = jnp.where(low, a, pltpu.roll(b, 16 * step, 1))
                parts[i | step] = jnp.where(low, pltpu.roll(a, 128 - 16 * step, 1), b)
    return parts


def swap_groups(values):
    row = lax.broadcasted_iota(jnp.int32, values.shape, 1)
    group = lax.broadcasted_iota(jnp.int32, values.shape, 2) // 16
    for step in (1, 2, 4):
        row_high, group_high = (row & step) != 0, (group & step) != 0
        if step == 4:
            moved = pltpu.roll(pltpu.roll(values, 4, 1), 64, 2)
        else:
            up = pltpu.roll(pltpu.roll(values, 8 - step, 1), 16 * step, 2)
            down = pltpu.roll(pltpu.roll(values, step, 1), 128 - 16 * step, 2)
            moved = jnp.where(row_high, down, up)
        values = jnp.where(row_high == group_high, values, moved)
    return values


def turned(values, step):
    return jnp.concatenate([values[step:], values[:step]], axis=0)


def fold_edges(edge):
    before, after = turned(edge, -1), turned(edge, 1)
    row = lax.broadcasted_iota(jnp.int32, edge.shape, 1)
    return [
        jnp.concatenate(
            [
                jnp.where(row < 2, pltpu.roll(before, step, 1), 0.0),
                jnp.where(row >= 6, pltpu.roll(after, step, 1), 0.0),
            ],
            axis=1,
        )
        for step in (6, 2)
    ]


def edges_of(real, imag):
    row = lax.broadcasted_iota(jnp.int32, (16, 8, 128), 1)
    ends = [
        pltpu.roll(part, step, 1)
        for values, step in ((real, 2), (imag, 6))
        for part in (turned(values, -1)[:, 8:], turned(values, 1)[:, :8])
    ]
    return jnp.where(
        row < 2, ends[0], jnp.where(row < 4, ends[1], jnp.where(row < 6, ends[2], ends[3]))
    )


def tile(low, high=None):
    high = jnp.zeros_like(low) if high is None else high
    return jnp.concatenate([low, high], axis=low.ndim - 2).astype(jnp.bfloat16)


def profile(cells, base, weights):
    total = jnp.zeros(cells.shape, jnp.float32)
    for offset in range(4):
        total = total + jnp.where(cells == base[offset], weights[offset], 0.0)
    return total


def mesh_stage(
    charges_ref,
    fill_ref,
    base_ref,
    spline_ref,
    green_ref,
    wave_h,
    wave_l,
    ahead_h,
    ahead_l,
    back_h,
    back_l,
    atom_ref,
    grid_ref,
    plane,
    prof_h,
    prof_l,
    z_out,
    z_in,
    y_out,
    y_in,
    x_out,
    x_in,
    v_out,
    v_in,
    shared,
    shared_edge,
    green,
    green_out,
    green_in,
    send_sem,
    recv_sem,
):
    count = 16
    px, py = lax.axis_index("gx"), lax.axis_index("gy")
    def remote(source, target, stage, index, where):
        return pltpu.make_async_remote_copy(
            src_ref=source,
            dst_ref=target,
            send_sem=send_sem.at[stage, index],
            recv_sem=recv_sem.at[stage, index],
            device_id=where,
            device_id_type=MESH,
        )

    def exchange(make):
        def start(d, carry):
            make(d).start()
            return carry

        lax.fori_loop(1, count, start, 0)

    def arrive(make):
        def wait(d, carry):
            make(d).wait()
            return carry

        lax.fori_loop(1, count, wait, 0)

    def column_copy(out, into, stage):
        def make(d):
            to = ring(py, d, count)
            return remote(out.at[to], into.at[py], stage, d, (px, to))

        return make

    def row_copy(out, into, stage, layers):
        def make(d):
            to = ring(px, d, count)
            return remote(out.at[to, layers], into.at[px, layers], stage, d, (to, py))

        return make

    main, extra = pl.ds(0, 3), pl.ds(3, 2)

    def green_copy():
        return remote(green_out, green_in, 8, 0, (px, 0))

    def rows(dim):
        base = base_ref[dim : dim + 1, :]
        cells = [base + offset for offset in range(4)]
        if dim == 2:
            cells = [jnp.where(c >= 256, c - 256, c) for c in cells]
        return cells, [spline_ref[dim, o : o + 1, :] for o in range(4)]

    def lines_of_atoms():
        z_cells = lax.broadcasted_iota(jnp.int32, (256, 1024), 0)
        high, low = split(profile(z_cells, *rows(2)))
        prof_h[...] = high
        prof_l[...] = low
        slots = [green_ref[:, i, :] for i in range(9)]
        green_out[...] = slots[0]
        picked = [jnp.where(py < 8, slots[i], slots[i + 1]) for i in range(8)]
        green[...] = jnp.transpose(jnp.concatenate(picked, axis=0))

    def planes_of_atoms():
        sixteen = lax.broadcasted_iota(jnp.int32, (16, 1024), 0)
        eight = lax.broadcasted_iota(jnp.int32, (8, 1024), 0)
        edge = jnp.where(eight < 2, eight, eight + 16)
        in_x, in_y = (profile(sixteen + 2, *rows(dim)) for dim in (0, 1))
        edge_x, edge_y = (profile(edge, *rows(dim)) for dim in (0, 1))
        for y in range(16):
            plane[16 * y : 16 * y + 16, :] = in_y[y : y + 1, :] * in_x
        for y in range(16):
            plane[256 + 8 * y : 264 + 8 * y, :] = in_y[y : y + 1, :] * edge_x
        for i in range(4):
            plane[384 + 16 * i : 400 + 16 * i, :] = edge_y[i : i + 1, :] * in_x
            plane[448 + 8 * i : 456 + 8 * i, :] = edge_y[i : i + 1, :] * edge_x

    def run():
        high, low = split(plane[...] * charges_ref[...])
        spread = dot(high, prof_h[...], NT) + dot(low, prof_h[...], NT) + dot(high, prof_l[...], NT)
        edges = spread[256:]
        edges = [
            tile(edges[:128].reshape(16, 8, 256)).reshape(256, 256),
            tile(edges[128:192]),
            tile(tile(edges[192:].reshape(4, 8, 256)).reshape(64, 256)),
        ]
        edges = jnp.concatenate(edges, axis=0)
        high, low = split(spread[:256])

        lines = dot(ahead_h[...], high, NT) + dot(ahead_l[...], high, NT) + dot(ahead_h[...], low, NT)
        halves = [
            swap_groups(lines[:, 128 * half : 128 * half + 128].reshape(32, 8, 128)) for half in (0, 1)
        ]
        halves = jnp.concatenate(halves, axis=1).astype(jnp.bfloat16)
        z_out[:, 0] = halves[:16]
        z_out[:, 1] = halves[16:]
        lines = dot(ahead_h[...], edges, NT) + dot(ahead_l[...], edges, NT)
        real, imag = lines[:128], lines[128:]
        sides = real[:, :256] + pltpu.roll(imag[:, :256], 4, 1)
        ends = real[:, 256:384] + pltpu.roll(imag[:, 256:384], 64, 1)
        corners = real[:, 384:] + pltpu.roll(imag[:, 384:], 4, 1)
        pieces = [
            swap_groups(part.reshape(16, 8, 128))
            for part in (sides[:, :128], sides[:, 128:], ends, corners)
        ]
        z_out[:, 2] = tile(pieces[0], pieces[1])
        z_out[:, 3] = tile(pieces[2], pieces[3])
        make = column_copy(z_out, z_in, 2)
        exchange(make)

        @pl.when(py == 8)
        def _():
            green_copy().start()

        z_in[pl.ds(py, 1)] = z_out[pl.ds(py, 1)]
        arrive(make)

        cos_h, sin_h = wave_h[:256], wave_h[256:]
        cos_l, sin_l = wave_l[:256], wave_l[256:]
        ends = z_in[:, 3].astype(jnp.float32)
        adds = [*fold_edges(ends[:, :8]), fold_edges(ends[:, 8:])[0]]
        both = jnp.concatenate(
            [(z_in[:, i].astype(jnp.float32) + adds[i]).reshape(256, 128) for i in range(3)], axis=1
        )
        both = jnp.transpose(both).astype(jnp.bfloat16)
        c = dot(both, cos_h) + dot(both, cos_l)
        s = dot(both, sin_h) + dot(both, sin_l)
        apart = (lax.broadcasted_iota(jnp.int32, (128, 256), 0) < 16) & (py == 0)
        real = c[:128] + jnp.where(apart, 0.0, s[128:256])
        imag = jnp.where(apart, 0.0, c[128:256]) - s[:128]

        c_edge, s_edge = (v[256:].reshape(8, 16, 256)[:, :8] for v in (c, s))
        c_swap, s_swap = pltpu.roll(c_edge, 4, 1), pltpu.roll(s_edge, 4, 1)
        top = lax.broadcasted_iota(jnp.int32, (8, 8, 256), 1) < 4
        apart = (lax.broadcasted_iota(jnp.int32, (8, 8, 256), 0) == 0) & (py == 0)
        edge = jnp.where(
            top,
            c_edge + jnp.where(apart, 0.0, s_swap),
            jnp.where(apart, 0.0, c_edge) - s_swap,
        )

        def to_slots(values, layer):
            for half in (0, 1):
                lanes = slice(128 * half, 128 * half + 128)
                done = regroup([v[:, lanes] for v in values])
                for i in range(8):
                    whole = done[i].shape[0] == 16
                    y_out[8 * half + i, layer] = done[i].astype(jnp.bfloat16) if whole else tile(done[i])

        to_slots([real[16 * i : 16 * i + 16] for i in range(8)], 0)
        to_slots([imag[16 * i : 16 * i + 16] for i in range(8)], 1)
        to_slots([edge[i] for i in range(8)], 2)
        make = row_copy(y_out, y_in, 3, main)
        exchange(make)
        y_in[pl.ds(px, 1), 0:3] = y_out[pl.ds(px, 1), 0:3]

        @pl.when(py == 0)
        def _():
            blank = jnp.zeros((16, 256), jnp.float32)
            to_slots([c[128:144], -s[128:144]] + [blank] * 6, 3)
            to_slots([jnp.where(top[0], c_swap[0], -s_edge[0])] + [blank[:8]] * 7, 4)
            exchange(row_copy(y_out, y_in, 4, extra))
            y_in[pl.ds(px, 1), 3:5] = y_out[pl.ds(px, 1), 3:5]

        arrive(make)

        def forward_x(values):
            return dot(cos_h, values) + dot(cos_l, values), dot(sin_h, values) + dot(sin_l, values)

        def inverse_x(values):
            high, low = split(values)
            return (
                dot(cos_h, high) + dot(cos_l, high) + dot(cos_h, low),
                dot(sin_h, high) + dot(sin_l, high) + dot(sin_h, low),
            )

        adds = fold_edges(y_in[:, 2].astype(jnp.float32)[:, :8])
        c, s = forward_x(
            jnp.concatenate(
                [(y_in[:, i].astype(jnp.float32) + adds[i]).reshape(256, 128) for i in range(2)], axis=1
            ).astype(jnp.bfloat16)
        )
        real = (c[:, :128] + s[:, 128:]) * green[...]
        imag = (c[:, 128:] - s[:, :128]) * green[...]
        c, s = inverse_x(jnp.concatenate([real, imag], axis=1))
        real = (c[:, :128] - s[:, 128:]).reshape(16, 16, 128)
        imag = (c[:, 128:] + s[:, :128]).reshape(16, 16, 128)
        x_out[:, 0] = real.astype(jnp.bfloat16)
        x_out[:, 1] = imag.astype(jnp.bfloat16)
        x_out[:, 2] = tile(edges_of(real, imag))
        make = row_copy(x_out, x_in, 5, main)
        exchange(make)
        x_in[pl.ds(px, 1), 0:3] = x_out[pl.ds(px, 1), 0:3]

        @pl.when(py == 0)
        def _():
            arrive(row_copy(y_out, y_in, 4, extra))
            green_copy().wait_recv()
            first = lax.broadcasted_iota(jnp.int32, (256, 128), 1) < 16
            adds = fold_edges(y_in[:, 4].astype(jnp.float32)[:, :8])
            last = y_in[:, 3].astype(jnp.float32) + adds[0] + pltpu.roll(adds[1], 16, 2)
            c, s = forward_x(last.reshape(256, 128).astype(jnp.bfloat16))
            kernel = jnp.transpose(
                jnp.concatenate([green_in[...], jnp.zeros((112, 256), jnp.float32)], axis=0)
            )
            real = (c + pltpu.roll(s, 112, 1)) * kernel
            imag = (pltpu.roll(c, 112, 1) - s) * kernel
            c, s = inverse_x(real + pltpu.roll(imag, 16, 1))
            real = jnp.where(first, c - pltpu.roll(s, 112, 1), 0.0)
            imag = jnp.where(first, pltpu.roll(c, 112, 1) + s, 0.0)
            x_out[:, 3] = (real + pltpu.roll(imag, 16, 1)).astype(jnp.bfloat16).reshape(16, 16, 128)
            x_out[:, 4] = tile(edges_of(real.reshape(16, 16, 128), imag.reshape(16, 16, 128)))
            back_copy = row_copy(x_out, x_in, 6, extra)
            exchange(back_copy)
            x_in[pl.ds(px, 1), 3:5] = x_out[pl.ds(px, 1), 3:5]

        @pl.when(py == 8)
        def _():
            green_copy().wait_send()

        arrive(make)

        def to_rows(layer, count=16):
            halves = [
                regroup([x_in[8 * half + i, layer].astype(jnp.float32)[:count] for i in range(8)])
                for half in (0, 1)
            ]
            return [jnp.concatenate([halves[0][i], halves[1][i]], axis=1) for i in range(8)]

        real, imag, edge = to_rows(0), to_rows(1), to_rows(2, 8)
        shared[0] = real[0]
        shared[1] = imag[0]
        shared_edge[...] = edge[0]

        @pl.when(py == 0)
        def _():
            arrive(row_copy(x_out, x_in, 6, extra))
            last = to_rows(3)
            shared[0] = -last[1]
            shared[1] = last[0]
            last = pltpu.roll(to_rows(4, 8)[0], 4, 0)
            shared_edge[...] = jnp.where(top[0], -last, last)

        a = jnp.concatenate(real, axis=0).astype(jnp.bfloat16)
        b = jnp.concatenate(imag, axis=0).astype(jnp.bfloat16)
        a_too = jnp.concatenate([shared[0], *real[1:]], axis=0).astype(jnp.bfloat16)
        b_too = jnp.concatenate([shared[1], *imag[1:]], axis=0).astype(jnp.bfloat16)
        real = dot(cos_h, a, NT) + dot(cos_l, a, NT) - dot(sin_h, b, NT) - dot(sin_l, b, NT)
        imag = dot(cos_h, b_too, NT) + dot(cos_l, b_too, NT) + dot(sin_h, a_too, NT) + dot(sin_l, a_too, NT)
        sides = []
        for first in (edge[0], shared_edge[...]):
            rows = jnp.concatenate([tile(v) for v in [first, *edge[1:]]], axis=0)
            sides.append(
                (
                    dot(cos_h, rows, NT) + dot(cos_l, rows, NT),
                    dot(sin_h, rows, NT) + dot(sin_l, rows, NT),
                )
            )
        within = lax.broadcasted_iota(jnp.int32, (256, 128), 1) % 16
        sides = jnp.where(
            within < 4,
            sides[0][0] - pltpu.roll(sides[0][1], 124, 1),
            sides[1][0] + pltpu.roll(sides[1][1], 4, 1),
        )
        sides = jnp.where(within < 8, sides, 0.0).reshape(16, 16, 128)
        real, imag = real.reshape(16, 16, 128), imag.reshape(16, 16, 128)
        v_out[:, 0] = real.astype(jnp.bfloat16)
        v_out[:, 1] = imag.astype(jnp.bfloat16)
        v_out[:, 2] = sides.astype(jnp.bfloat16)
        v_out[:, 3] = tile(edges_of(real, imag), edges_of(sides, sides))
        make = column_copy(v_out, v_in, 7)
        exchange(make)
        v_in[pl.ds(py, 1)] = v_out[pl.ds(py, 1)]
        arrive(make)

        def to_lines(values):
            return swap_groups(values).reshape(-1, 128)

        got = jnp.concatenate([v_in[:, 0], v_in[:, 1]], axis=0).astype(jnp.float32)
        lines = jnp.concatenate([to_lines(got[:, :8]), to_lines(got[:, 8:])], axis=1).astype(jnp.bfloat16)
        grid = dot(lines, back_h[...], TN) + dot(lines, back_l[...], TN)
        for y in range(16):
            grid_ref[:, y, :] = grid[16 * y : 16 * y + 16]
        got = jnp.concatenate([v_in[:, 2], v_in[:, 3]], axis=0).astype(jnp.float32)
        sides = jnp.concatenate([to_lines(got[:16, :8]), to_lines(got[:16, 8:])], axis=1)
        ends, corners = to_lines(got[16:, :8]), to_lines(got[16:, 8:])
        lines = jnp.concatenate(
            [
                jnp.concatenate([sides, ends, corners], axis=1),
                jnp.concatenate(
                    [pltpu.roll(sides, 252, 1), pltpu.roll(ends, 64, 1), pltpu.roll(corners, 124, 1)],
                    axis=1,
                ),
            ],
            axis=0,
        ).astype(jnp.bfloat16)
        edges = dot(lines, back_h[...], TN) + dot(lines, back_l[...], TN)

        values = jnp.concatenate(
            [
                grid,
                edges[:256].reshape(16, 16, 256)[:, :8].reshape(128, 256),
                edges[256:320],
                edges[384:448].reshape(4, 16, 256)[:, :8].reshape(32, 256),
            ],
            axis=0,
        )
        high, low = split(values)
        sampled = dot(high, prof_h[...]) + dot(low, prof_h[...]) + dot(high, prof_l[...])
        total = jnp.sum(sampled * plane[...], axis=0, keepdims=True)
        inside = lax.broadcasted_iota(jnp.int32, (1, 1024), 1) < fill_ref[0]
        atom_ref[...] = jnp.where(inside, total, 0.0)

    return lines_of_atoms, planes_of_atoms, run


def step_kernel(*refs):
    far, fill_ref, outs = refs[:17], refs[17], refs[18:21]
    near, load_sem, refs = refs[21:38], refs[38], refs[39:]
    message_scratch, mesh_scratch = refs[:11], refs[11:]
    loads = [
        pltpu.make_async_copy(source, target, load_sem.at[i])
        for i, (source, target) in enumerate(zip(far, near, strict=True))
    ]
    for load in loads:
        load.start()
    feats_ref, nbr_ref, count_ref, radial_ref, *weights, charge_w_ref = near[:8]
    message_in = (feats_ref, radial_ref, nbr_ref, count_ref, fill_ref, *weights, charge_w_ref)
    count = 16
    px, py = lax.axis_index("gx"), lax.axis_index("gy")
    barrier = pltpu.get_barrier_semaphore()

    def greet(d, carry):
        for where in ((ring(px, d, count), py), (px, ring(py, d, count))):
            pl.semaphore_signal(barrier, inc=1, device_id=where, device_id_type=MESH)
        return carry

    lax.fori_loop(1, count, greet, 0)
    for dx in (-1, 1):
        for dy in (-1, 1):
            pl.semaphore_signal(
                barrier,
                inc=1,
                device_id=(ring(px, dx, count), ring(py, dy, count)),
                device_id_type=MESH,
            )
    lines_of_atoms, planes_of_atoms, run = mesh_stage(
        outs[0], fill_ref, *near[8:], *outs[1:], *mesh_scratch
    )

    def first_idle():
        for load in loads[8:]:
            load.wait()
        lines_of_atoms()

    for load in loads[:8]:
        load.wait()
    message_stage(
        lambda: pl.semaphore_wait(barrier, 34),
        (first_idle, planes_of_atoms),
        *message_in,
        outs[0],
        *message_scratch,
    )
    run()


def hand_on(*refs):
    copies = [pltpu.make_async_copy(refs[i], refs[3 + i], refs[6].at[i]) for i in range(3)]
    for copy in copies:
        copy.start()
    for copy in copies:
        copy.wait()


def shards(
    node_feats,
    radial,
    neighbours,
    nbr_count,
    domain_count,
    base_cells,
    spline_weights,
    w_proj,
    w_radial,
    w_mix,
    w_charge,
    green_kernel,
):
    vmem = pl.BlockSpec(memory_space=pltpu.VMEM)
    bf16, f32 = jnp.bfloat16, jnp.float32
    far = [
        node_feats,
        neighbours,
        nbr_count.reshape(1, 1024),
        radial.reshape(8 * K, 1024),
        w_proj,
        w_radial,
        w_mix,
        w_charge.reshape(1, 128),
        base_cells,
        spline_weights,
        jnp.transpose(green_kernel, (1, 2, 0)),
        *(jnp.asarray(table) for table in mesh_tables()),
    ]
    charges, atom_potential, potential = pl.pallas_call(
        step_kernel,
        out_shape=(
            jax.ShapeDtypeStruct((1, 1024), f32),
            jax.ShapeDtypeStruct((1, 1024), f32),
            jax.ShapeDtypeStruct((16, 16, 256), f32),
        ),
        in_specs=[pl.BlockSpec(memory_space=pltpu.HBM)] * 17
        + [pl.BlockSpec(memory_space=pltpu.SMEM)],
        out_specs=(vmem, vmem, vmem),
        scratch_shapes=[
            *(pltpu.VMEM(array.shape, array.dtype) for array in far),
            pltpu.SemaphoreType.DMA((17,)),
            pltpu.VMEM((128, 1024), f32),
            pltpu.VMEM((128, 1024), bf16),
            pltpu.VMEM((L, 256, 128), bf16),
            pltpu.VMEM((L, 512, 128), bf16),
            pltpu.VMEM((128, 640), bf16),
            pltpu.VMEM((128, 512), bf16),
            pltpu.VMEM((K, 8, 128), f32),
            pltpu.VMEM((K * 128, 8 * K), bf16),
            pltpu.VMEM((128, 256), f32),
            pltpu.SemaphoreType.DMA((L, 8)),
            pltpu.SemaphoreType.DMA((L, 8)),
            pltpu.VMEM((480, 1024), f32),
            pltpu.VMEM((256, 1024), bf16),
            pltpu.VMEM((256, 1024), bf16),
            *[pltpu.VMEM((16, 4, 16, 128), bf16)] * 2,
            *[pltpu.VMEM((16, 5, 16, 128), bf16)] * 4,
            *[pltpu.VMEM((16, 4, 16, 128), bf16)] * 2,
            pltpu.VMEM((2, 16, 256), f32),
            pltpu.VMEM((8, 256), f32),
            pltpu.VMEM((256, 128), f32),
            pltpu.VMEM((16, 256), f32),
            pltpu.VMEM((16, 256), f32),
            pltpu.SemaphoreType.DMA((9, 16)),
            pltpu.SemaphoreType.DMA((9, 16)),
        ],
        compiler_params=pltpu.CompilerParams(
            collective_id=0, has_side_effects=True, vmem_limit_bytes=56 * 1024 * 1024
        ),
        name="potential_step",
    )(
        *far,
        domain_count,
    )
    results = (charges, atom_potential, potential)
    charges, atom_potential, potential = pl.pallas_call(
        hand_on,
        out_shape=tuple(jax.ShapeDtypeStruct(array.shape, f32) for array in results),
        in_specs=[pl.BlockSpec(memory_space=pl.ANY)] * 3,
        out_specs=[pl.BlockSpec(memory_space=pl.ANY)] * 3,
        scratch_shapes=[pltpu.SemaphoreType.DMA((3,))],
        name="hand_on",
    )(*results)
    return (charges.reshape(1024), atom_potential.reshape(1024), potential)


def solution(mesh):
    return jax.shard_map(
        shards,
        mesh=mesh,
        in_specs=(
            P(("gx", "gy"), None),
            P(None, None, ("gx", "gy")),
            P(None, ("gx", "gy")),
            P(("gx", "gy")),
            P(("gx", "gy")),
            P(None, ("gx", "gy")),
            P(None, None, ("gx", "gy")),
            P(),
            P(),
            P(),
            P(),
            P(None, "gx", "gy"),
        ),
        out_specs=(P(("gx", "gy")), P(("gx", "gy")), P("gx", "gy", None)),
        check_vma=False,
    )
```

```python
import math

import jax
import jax.numpy as jnp
import ml_dtypes
import numpy as np
from jax import lax
from jax.experimental import pallas as pl
from jax.experimental.pallas import tpu as pltpu
from jax.sharding import PartitionSpec as P

K = 32
L = 2


MESH = pl.DeviceIdType.MESH
TN = (((0,), (0,)), ((), ()))
NT = (((1,), (1,)), ((), ()))
NN = (((1,), (0,)), ((), ()))


def dot(a, b, dims=NN):
    return lax.dot_general(a, b, dims, preferred_element_type=jnp.float32)


def ring(index, step, count):
    return lax.rem(index + step + count, count)


def message_stage(
    enter,
    idle,
    feats_ref,
    radial_ref,
    nbr_ref,
    count_ref,
    fill_ref,
    proj_ref,
    filt_ref,
    mix_ref,
    charge_w_ref,
    charges_ref,
    state,
    table,
    rows_out,
    rows_in,
    head_a,
    head_b,
    pick,
    filt_k,
    total,
    send_sem,
    recv_sem,
):
    px, py = lax.axis_index("gx"), lax.axis_index("gy")
    num_x = num_y = 16
    peers = [(dx, dy) for dx in (-1, 0, 1) for dy in (-1, 0, 1) if (dx, dy) != (0, 0)]
    code = nbr_ref[...]
    direction, slot = code // 1024, code % 1024
    lane = lax.broadcasted_iota(jnp.int32, (K, 1024), 1)
    live = lax.broadcasted_iota(jnp.int32, (K, 1024), 0) < count_ref[...]
    block = lane // 128
    near = slot - jnp.maximum(block - 1, 0) * 128
    far = jnp.where(
        direction < 3,
        192 + direction * 64 + slot,
        jnp.where(
            direction > 5,
            64 + direction * 64 + slot,
            jnp.where(direction == 3, 192 + slot, 320 + slot),
        ),
    )
    named = jnp.where(live, jnp.where(direction == 4, near, far), -8192).astype(jnp.float32)
    for b in range(8):
        pick[:, b, :] = named[:, b * 128 : (b + 1) * 128]

    state[...] = jnp.transpose(feats_ref[...].astype(jnp.float32))
    row_id = lax.broadcasted_iota(jnp.int32, (128, 128), 0).astype(jnp.bfloat16)
    one, zero = jnp.ones((128, 128), jnp.bfloat16), jnp.zeros((128, 128), jnp.bfloat16)
    basis_k = lax.broadcasted_iota(jnp.int32, (128, 8 * K), 1) % K

    def onehot(k, begin, groups):
        row = pick[k, begin // 128 : begin // 128 + 1, :]
        parts = [
            jnp.where(row_id == jnp.broadcast_to((row - 128.0 * g).astype(jnp.bfloat16), (128, 128)), one, zero)
            for g in range(groups)
        ]
        return jnp.concatenate(parts, axis=0)

    def messages(group, tables):
        begin = group * 256
        radial = radial_ref[:, begin : begin + 256]
        total[...] = jnp.zeros_like(total)

        for k in range(0, K, 2):
            filters = dot(filt_k[k * 128 : k * 128 + 256, :], radial)
            for half, (source, groups) in enumerate(tables):
                at = begin + 128 * half
                hot = jnp.concatenate([onehot(k, at, groups), onehot(k + 1, at, groups)], axis=1)
                got = dot(source(), hot)
                lanes = slice(128 * half, 128 * half + 128)
                total[:, lanes] += (
                    got[:, :128] * filters[:128, lanes] + got[:, 128:] * filters[128:, lanes]
                )
        return (total[...] * (1.0 / math.sqrt(K))).astype(jnp.bfloat16)

    for layer in range(L):
        spread = jnp.concatenate(
            [jnp.broadcast_to(filt_ref[layer, b : b + 1], (K, 128)) for b in range(8)], axis=0
        )
        spread = jnp.transpose(spread.astype(jnp.float32))
        for k in range(K):
            filt_k[k * 128 : (k + 1) * 128, :] = jnp.where(basis_k == k, spread, 0.0).astype(jnp.bfloat16)
        proj = proj_ref[layer]
        first = dot(proj, state[:, :256].astype(jnp.bfloat16), TN).astype(jnp.bfloat16)
        rows_out[layer] = jnp.transpose(first.astype(jnp.float32)).astype(jnp.bfloat16)
        if layer == 0:
            enter()
        copies = []
        for dx, dy in peers:
            if dx == 1:
                band, land = 1, 1 - dy
            elif dx == -1:
                band, land = 0, 4 - dy
            elif dy == 1:
                band, land = 3, 6
            else:
                band, land = 2, 7
            copies.append(
                pltpu.make_async_remote_copy(
                    src_ref=rows_out.at[layer, pl.ds(band * 64, 64)],
                    dst_ref=rows_in.at[layer, pl.ds(land * 64, 64)],
                    send_sem=send_sem.at[layer, land],
                    recv_sem=recv_sem.at[layer, land],
                    device_id=(ring(px, dx, num_x), ring(py, dy, num_y)),
                    device_id_type=MESH,
                )
            )
            copies[-1].start()
        table[:, :256] = first
        table[:, 256:] = dot(proj, state[:, 256:].astype(jnp.bfloat16), TN).astype(jnp.bfloat16)

        def update(group, tables):
            begin = group * 256
            u = messages(group, tables)
            mixed = dot(mix_ref[layer], u, TN)
            lanes = slice(begin, begin + 256)
            state[:, lanes] = (
                (state[:, lanes] + mixed / (1.0 + jnp.exp(-mixed))).astype(jnp.bfloat16).astype(jnp.float32)
            )

        def window(block):
            low = max(block - 1, 0) * 128
            high = min(block + 2, 8) * 128
            return (lambda: table[:, low:high]), (high - low) // 128

        for group in (1, 2, 3):
            update(group, [window(2 * group), window(2 * group + 1)])
        idle[layer]()
        for copy in copies:
            copy.wait()
        far_rows = jnp.transpose(rows_in[layer].astype(jnp.float32)).astype(jnp.bfloat16)
        head_a[:, :256] = table[:, :256]
        head_a[:, 256:] = far_rows[:, :384]
        head_b[:, :384] = table[:, :384]
        head_b[:, 384:] = far_rows[:, 384:]
        update(0, [((lambda: head_a[...]), 5), ((lambda: head_b[...]), 4)])
    charge = dot(jnp.broadcast_to(charge_w_ref[...], (8, 128)), state[...].astype(jnp.bfloat16))[0:1]
    inside = lax.broadcasted_iota(jnp.int32, (1, 1024), 1) < fill_ref[0]
    charges_ref[...] = jnp.where(inside, charge, 0.0)


def split(values):
    high = values.astype(jnp.bfloat16)
    return high, (values - high.astype(jnp.float32)).astype(jnp.bfloat16)


def np_split(values):
    high = values.astype(ml_dtypes.bfloat16)
    return high, (values - high.astype(np.float64)).astype(ml_dtypes.bfloat16)


def mesh_tables():
    ids = np.arange(256)
    angles = 2.0 * np.pi * (ids[:, None] * ids[None, :] % 256) / 256
    waves = np.concatenate([np.cos(angles), np.sin(angles)], axis=0)
    column, slot = np.arange(16)[:, None], np.arange(8)[None, :]
    kz = (16 * column + slot + (column >= 8)).reshape(128)
    turn = 2.0 * np.pi * (kz[:, None] * ids[None, :] % 256) / 256
    ahead = np.stack([np.cos(turn), -np.sin(turn)])
    back = 2.0 * ahead
    ahead[0, 0], ahead[1, 0] = 1.0, 1.0 - 2.0 * (ids % 2)
    back[0, 0], back[1, 0] = ahead[0, 0], ahead[1, 0]
    back = back / 256.0**3
    return (
        *np_split(waves),
        *np_split(ahead.reshape(256, 256)),
        *np_split(back.reshape(256, 256)),
    )


def regroup(parts):
    group = lax.broadcasted_iota(jnp.int32, parts[0].shape, 1) // 16
    parts = list(parts)
    for step in (1, 2, 4):
        low = (group & step) == 0
        for i in range(8):
            if i & step == 0:
                a, b = parts[i], parts[i | step]
                parts[i] = jnp.where(low, a, pltpu.roll(b, 16 * step, 1))
                parts[i | step] = jnp.where(low, pltpu.roll(a, 128 - 16 * step, 1), b)
    return parts


def swap_groups(values):
    row = lax.broadcasted_iota(jnp.int32, values.shape, 1)
    group = lax.broadcasted_iota(jnp.int32, values.shape, 2) // 16
    for step in (1, 2, 4):
        row_high, group_high = (row & step) != 0, (group & step) != 0
        if step == 4:
            moved = pltpu.roll(pltpu.roll(values, 4, 1), 64, 2)
        else:
            up = pltpu.roll(pltpu.roll(values, 8 - step, 1), 16 * step, 2)
            down = pltpu.roll(pltpu.roll(values, step, 1), 128 - 16 * step, 2)
            moved = jnp.where(row_high, down, up)
        values = jnp.where(row_high == group_high, values, moved)
    return values


def turned(values, step):
    return jnp.concatenate([values[step:], values[:step]], axis=0)


def fold_edges(edge):
    before, after = turned(edge, -1), turned(edge, 1)
    row = lax.broadcasted_iota(jnp.int32, edge.shape, 1)
    return [
        jnp.concatenate(
            [
                jnp.where(row < 2, pltpu.roll(before, step, 1), 0.0),
                jnp.where(row >= 6, pltpu.roll(after, step, 1), 0.0),
            ],
            axis=1,
        )
        for step in (6, 2)
    ]


def edges_of(real, imag):
    row = lax.broadcasted_iota(jnp.int32, (16, 8, 128), 1)
    ends = [
        pltpu.roll(part, step, 1)
        for values, step in ((real, 2), (imag, 6))
        for part in (turned(values, -1)[:, 8:], turned(values, 1)[:, :8])
    ]
    return jnp.where(
        row < 2, ends[0], jnp.where(row < 4, ends[1], jnp.where(row < 6, ends[2], ends[3]))
    )


def tile(low, high=None):
    high = jnp.zeros_like(low) if high is None else high
    return jnp.concatenate([low, high], axis=low.ndim - 2).astype(jnp.bfloat16)


def profile(cells, base, weights):
    total = jnp.zeros(cells.shape, jnp.float32)
    for offset in range(4):
        total = total + jnp.where(cells == base[offset], weights[offset], 0.0)
    return total


def mesh_stage(
    charges_ref,
    fill_ref,
    base_ref,
    spline_ref,
    green_ref,
    wave_h,
    wave_l,
    ahead_h,
    ahead_l,
    back_h,
    back_l,
    atom_ref,
    grid_ref,
    plane,
    prof_h,
    prof_l,
    z_out,
    z_in,
    y_out,
    y_in,
    x_out,
    x_in,
    v_out,
    v_in,
    shared,
    shared_edge,
    green,
    green_out,
    green_in,
    send_sem,
    recv_sem,
):
    count = 16
    px, py = lax.axis_index("gx"), lax.axis_index("gy")
    def remote(source, target, stage, index, where):
        return pltpu.make_async_remote_copy(
            src_ref=source,
            dst_ref=target,
            send_sem=send_sem.at[stage, index],
            recv_sem=recv_sem.at[stage, index],
            device_id=where,
            device_id_type=MESH,
        )

    def exchange(make):
        def start(d, carry):
            make(d).start()
            return carry

        lax.fori_loop(1, count, start, 0)

    def arrive(make):
        def wait(d, carry):
            make(d).wait()
            return carry

        lax.fori_loop(1, count, wait, 0)

    def column_copy(out, into, stage):
        def make(d):
            to = ring(py, d, count)
            return remote(out.at[to], into.at[py], stage, d, (px, to))

        return make

    def row_copy(out, into, stage, layers):
        def make(d):
            to = ring(px, d, count)
            return remote(out.at[to, layers], into.at[px, layers], stage, d, (to, py))

        return make

    main, extra = pl.ds(0, 3), pl.ds(3, 2)

    def green_copy():
        return remote(green_out, green_in, 8, 0, (px, 0))

    def rows(dim):
        base = base_ref[dim : dim + 1, :]
        cells = [base + offset for offset in range(4)]
        if dim == 2:
            cells = [jnp.where(c >= 256, c - 256, c) for c in cells]
        return cells, [spline_ref[dim, o : o + 1, :] for o in range(4)]

    def lines_of_atoms():
        z_cells = lax.broadcasted_iota(jnp.int32, (256, 1024), 0)
        high, low = split(profile(z_cells, *rows(2)))
        prof_h[...] = high
        prof_l[...] = low
        slots = [green_ref[:, i, :] for i in range(9)]
        green_out[...] = slots[0]
        picked = [jnp.where(py < 8, slots[i], slots[i + 1]) for i in range(8)]
        green[...] = jnp.transpose(jnp.concatenate(picked, axis=0))

    def planes_of_atoms():
        sixteen = lax.broadcasted_iota(jnp.int32, (16, 1024), 0)
        eight = lax.broadcasted_iota(jnp.int32, (8, 1024), 0)
        edge = jnp.where(eight < 2, eight, eight + 16)
        in_x, in_y = (profile(sixteen + 2, *rows(dim)) for dim in (0, 1))
        edge_x, edge_y = (profile(edge, *rows(dim)) for dim in (0, 1))
        for y in range(16):
            plane[16 * y : 16 * y + 16, :] = in_y[y : y + 1, :] * in_x
        for y in range(16):
            plane[256 + 8 * y : 264 + 8 * y, :] = in_y[y : y + 1, :] * edge_x
        for i in range(4):
            plane[384 + 16 * i : 400 + 16 * i, :] = edge_y[i : i + 1, :] * in_x
            plane[448 + 8 * i : 456 + 8 * i, :] = edge_y[i : i + 1, :] * edge_x

    def run():
        high, low = split(plane[...] * charges_ref[...])
        spread = dot(high, prof_h[...], NT) + dot(low, prof_h[...], NT) + dot(high, prof_l[...], NT)
        edges = spread[256:]
        edges = [
            tile(edges[:128].reshape(16, 8, 256)).reshape(256, 256),
            tile(edges[128:192]),
            tile(tile(edges[192:].reshape(4, 8, 256)).reshape(64, 256)),
        ]
        edges = jnp.concatenate(edges, axis=0)
        high, low = split(spread[:256])

        lines = dot(ahead_h[...], high, NT) + dot(ahead_l[...], high, NT) + dot(ahead_h[...], low, NT)
        halves = [
            swap_groups(lines[:, 128 * half : 128 * half + 128].reshape(32, 8, 128)) for half in (0, 1)
        ]
        halves = jnp.concatenate(halves, axis=1).astype(jnp.bfloat16)
        z_out[:, 0] = halves[:16]
        z_out[:, 1] = halves[16:]
        lines = dot(ahead_h[...], edges, NT) + dot(ahead_l[...], edges, NT)
        real, imag = lines[:128], lines[128:]
        sides = real[:, :256] + pltpu.roll(imag[:, :256], 4, 1)
        ends = real[:, 256:384] + pltpu.roll(imag[:, 256:384], 64, 1)
        corners = real[:, 384:] + pltpu.roll(imag[:, 384:], 4, 1)
        pieces = [
            swap_groups(part.reshape(16, 8, 128))
            for part in (sides[:, :128], sides[:, 128:], ends, corners)
        ]
        z_out[:, 2] = tile(pieces[0], pieces[1])
        z_out[:, 3] = tile(pieces[2], pieces[3])
        make = column_copy(z_out, z_in, 2)
        exchange(make)

        @pl.when(py == 8)
        def _():
            green_copy().start()

        z_in[pl.ds(py, 1)] = z_out[pl.ds(py, 1)]
        arrive(make)

        cos_h, sin_h = wave_h[:256], wave_h[256:]
        cos_l, sin_l = wave_l[:256], wave_l[256:]
        ends = z_in[:, 3].astype(jnp.float32)
        adds = [*fold_edges(ends[:, :8]), fold_edges(ends[:, 8:])[0]]
        both = jnp.concatenate(
            [(z_in[:, i].astype(jnp.float32) + adds[i]).reshape(256, 128) for i in range(3)], axis=1
        )
        both = jnp.transpose(both).astype(jnp.bfloat16)
        c = dot(both, cos_h) + dot(both, cos_l)
        s = dot(both, sin_h) + dot(both, sin_l)
        apart = (lax.broadcasted_iota(jnp.int32, (128, 256), 0) < 16) & (py == 0)
        real = c[:128] + jnp.where(apart, 0.0, s[128:256])
        imag = jnp.where(apart, 0.0, c[128:256]) - s[:128]

        c_edge, s_edge = (v[256:].reshape(8, 16, 256)[:, :8] for v in (c, s))
        c_swap, s_swap = pltpu.roll(c_edge, 4, 1), pltpu.roll(s_edge, 4, 1)
        top = lax.broadcasted_iota(jnp.int32, (8, 8, 256), 1) < 4
        apart = (lax.broadcasted_iota(jnp.int32, (8, 8, 256), 0) == 0) & (py == 0)
        edge = jnp.where(
            top,
            c_edge + jnp.where(apart, 0.0, s_swap),
            jnp.where(apart, 0.0, c_edge) - s_swap,
        )

        def to_slots(values, layer):
            for half in (0, 1):
                lanes = slice(128 * half, 128 * half + 128)
                done = regroup([v[:, lanes] for v in values])
                for i in range(8):
                    whole = done[i].shape[0] == 16
                    y_out[8 * half + i, layer] = done[i].astype(jnp.bfloat16) if whole else tile(done[i])

        to_slots([real[16 * i : 16 * i + 16] for i in range(8)], 0)
        to_slots([imag[16 * i : 16 * i + 16] for i in range(8)], 1)
        to_slots([edge[i] for i in range(8)], 2)
        make = row_copy(y_out, y_in, 3, main)
        exchange(make)
        y_in[pl.ds(px, 1), 0:3] = y_out[pl.ds(px, 1), 0:3]

        @pl.when(py == 0)
        def _():
            blank = jnp.zeros((16, 256), jnp.float32)
            to_slots([c[128:144], -s[128:144]] + [blank] * 6, 3)
            to_slots([jnp.where(top[0], c_swap[0], -s_edge[0])] + [blank[:8]] * 7, 4)
            exchange(row_copy(y_out, y_in, 4, extra))
            y_in[pl.ds(px, 1), 3:5] = y_out[pl.ds(px, 1), 3:5]

        arrive(make)

        def forward_x(values):
            return dot(cos_h, values) + dot(cos_l, values), dot(sin_h, values) + dot(sin_l, values)

        def inverse_x(values):
            high, low = split(values)
            return (
                dot(cos_h, high) + dot(cos_l, high) + dot(cos_h, low),
                dot(sin_h, high) + dot(sin_l, high) + dot(sin_h, low),
            )

        adds = fold_edges(y_in[:, 2].astype(jnp.float32)[:, :8])
        c, s = forward_x(
            jnp.concatenate(
                [(y_in[:, i].astype(jnp.float32) + adds[i]).reshape(256, 128) for i in range(2)], axis=1
            ).astype(jnp.bfloat16)
        )
        real = (c[:, :128] + s[:, 128:]) * green[...]
        imag = (c[:, 128:] - s[:, :128]) * green[...]
        c, s = inverse_x(jnp.concatenate([real, imag], axis=1))
        real = (c[:, :128] - s[:, 128:]).reshape(16, 16, 128)
        imag = (c[:, 128:] + s[:, :128]).reshape(16, 16, 128)
        x_out[:, 0] = real.astype(jnp.bfloat16)
        x_out[:, 1] = imag.astype(jnp.bfloat16)
        x_out[:, 2] = tile(edges_of(real, imag))
        make = row_copy(x_out, x_in, 5, main)
        exchange(make)
        x_in[pl.ds(px, 1), 0:3] = x_out[pl.ds(px, 1), 0:3]

        @pl.when(py == 0)
        def _():
            arrive(row_copy(y_out, y_in, 4, extra))
            green_copy().wait_recv()
            first = lax.broadcasted_iota(jnp.int32, (256, 128), 1) < 16
            adds = fold_edges(y_in[:, 4].astype(jnp.float32)[:, :8])
            last = y_in[:, 3].astype(jnp.float32) + adds[0] + pltpu.roll(adds[1], 16, 2)
            c, s = forward_x(last.reshape(256, 128).astype(jnp.bfloat16))
            kernel = jnp.transpose(
                jnp.concatenate([green_in[...], jnp.zeros((112, 256), jnp.float32)], axis=0)
            )
            real = (c + pltpu.roll(s, 112, 1)) * kernel
            imag = (pltpu.roll(c, 112, 1) - s) * kernel
            c, s = inverse_x(real + pltpu.roll(imag, 16, 1))
            real = jnp.where(first, c - pltpu.roll(s, 112, 1), 0.0)
            imag = jnp.where(first, pltpu.roll(c, 112, 1) + s, 0.0)
            x_out[:, 3] = (real + pltpu.roll(imag, 16, 1)).astype(jnp.bfloat16).reshape(16, 16, 128)
            x_out[:, 4] = tile(edges_of(real.reshape(16, 16, 128), imag.reshape(16, 16, 128)))
            back_copy = row_copy(x_out, x_in, 6, extra)
            exchange(back_copy)
            x_in[pl.ds(px, 1), 3:5] = x_out[pl.ds(px, 1), 3:5]

        @pl.when(py == 8)
        def _():
            green_copy().wait_send()

        arrive(make)

        def to_rows(layer, count=16):
            halves = [
                regroup([x_in[8 * half + i, layer].astype(jnp.float32)[:count] for i in range(8)])
                for half in (0, 1)
            ]
            return [jnp.concatenate([halves[0][i], halves[1][i]], axis=1) for i in range(8)]

        real, imag, edge = to_rows(0), to_rows(1), to_rows(2, 8)
        shared[0] = real[0]
        shared[1] = imag[0]
        shared_edge[...] = edge[0]

        @pl.when(py == 0)
        def _():
            arrive(row_copy(x_out, x_in, 6, extra))
            last = to_rows(3)
            shared[0] = -last[1]
            shared[1] = last[0]
            last = pltpu.roll(to_rows(4, 8)[0], 4, 0)
            shared_edge[...] = jnp.where(top[0], -last, last)

        a = jnp.concatenate(real, axis=0).astype(jnp.bfloat16)
        b = jnp.concatenate(imag, axis=0).astype(jnp.bfloat16)
        a_too = jnp.concatenate([shared[0], *real[1:]], axis=0).astype(jnp.bfloat16)
        b_too = jnp.concatenate([shared[1], *imag[1:]], axis=0).astype(jnp.bfloat16)
        real = dot(cos_h, a, NT) + dot(cos_l, a, NT) - dot(sin_h, b, NT) - dot(sin_l, b, NT)
        imag = dot(cos_h, b_too, NT) + dot(cos_l, b_too, NT) + dot(sin_h, a_too, NT) + dot(sin_l, a_too, NT)
        sides = []
        for first in (edge[0], shared_edge[...]):
            rows = jnp.concatenate([tile(v) for v in [first, *edge[1:]]], axis=0)
            sides.append(
                (
                    dot(cos_h, rows, NT) + dot(cos_l, rows, NT),
                    dot(sin_h, rows, NT) + dot(sin_l, rows, NT),
                )
            )
        within = lax.broadcasted_iota(jnp.int32, (256, 128), 1) % 16
        sides = jnp.where(
            within < 4,
            sides[0][0] - pltpu.roll(sides[0][1], 124, 1),
            sides[1][0] + pltpu.roll(sides[1][1], 4, 1),
        )
        sides = jnp.where(within < 8, sides, 0.0).reshape(16, 16, 128)
        real, imag = real.reshape(16, 16, 128), imag.reshape(16, 16, 128)
        v_out[:, 0] = real.astype(jnp.bfloat16)
        v_out[:, 1] = imag.astype(jnp.bfloat16)
        v_out[:, 2] = sides.astype(jnp.bfloat16)
        v_out[:, 3] = tile(edges_of(real, imag), edges_of(sides, sides))
        make = column_copy(v_out, v_in, 7)
        exchange(make)
        v_in[pl.ds(py, 1)] = v_out[pl.ds(py, 1)]
        arrive(make)

        def to_lines(values):
            return swap_groups(values).reshape(-1, 128)

        got = jnp.concatenate([v_in[:, 0], v_in[:, 1]], axis=0).astype(jnp.float32)
        lines = jnp.concatenate([to_lines(got[:, :8]), to_lines(got[:, 8:])], axis=1).astype(jnp.bfloat16)
        grid = dot(lines, back_h[...], TN) + dot(lines, back_l[...], TN)
        for y in range(16):
            grid_ref[:, y, :] = grid[16 * y : 16 * y + 16]
        got = jnp.concatenate([v_in[:, 2], v_in[:, 3]], axis=0).astype(jnp.float32)
        sides = jnp.concatenate([to_lines(got[:16, :8]), to_lines(got[:16, 8:])], axis=1)
        ends, corners = to_lines(got[16:, :8]), to_lines(got[16:, 8:])
        lines = jnp.concatenate(
            [
                jnp.concatenate([sides, ends, corners], axis=1),
                jnp.concatenate(
                    [pltpu.roll(sides, 252, 1), pltpu.roll(ends, 64, 1), pltpu.roll(corners, 124, 1)],
                    axis=1,
                ),
            ],
            axis=0,
        ).astype(jnp.bfloat16)
        edges = dot(lines, back_h[...], TN) + dot(lines, back_l[...], TN)

        values = jnp.concatenate(
            [
                grid,
                edges[:256].reshape(16, 16, 256)[:, :8].reshape(128, 256),
                edges[256:320],
                edges[384:448].reshape(4, 16, 256)[:, :8].reshape(32, 256),
            ],
            axis=0,
        )
        high, low = split(values)
        sampled = dot(high, prof_h[...]) + dot(low, prof_h[...]) + dot(high, prof_l[...])
        total = jnp.sum(sampled * plane[...], axis=0, keepdims=True)
        inside = lax.broadcasted_iota(jnp.int32, (1, 1024), 1) < fill_ref[0]
        atom_ref[...] = jnp.where(inside, total, 0.0)

    return lines_of_atoms, planes_of_atoms, run


def step_kernel(*refs):
    far, fill_ref, outs = refs[:17], refs[17], refs[18:21]
    near, load_sem, refs = refs[21:38], refs[38], refs[39:]
    message_scratch, mesh_scratch = refs[:11], refs[11:]
    loads = [
        pltpu.make_async_copy(source, target, load_sem.at[i])
        for i, (source, target) in enumerate(zip(far, near, strict=True))
    ]
    for load in loads:
        load.start()
    feats_ref, nbr_ref, count_ref, radial_ref, *weights, charge_w_ref = near[:8]
    message_in = (feats_ref, radial_ref, nbr_ref, count_ref, fill_ref, *weights, charge_w_ref)
    count = 16
    px, py = lax.axis_index("gx"), lax.axis_index("gy")
    barrier = pltpu.get_barrier_semaphore()

    def greet(d, carry):
        for where in ((ring(px, d, count), py), (px, ring(py, d, count))):
            pl.semaphore_signal(barrier, inc=1, device_id=where, device_id_type=MESH)
        return carry

    lax.fori_loop(1, count, greet, 0)
    for dx in (-1, 1):
        for dy in (-1, 1):
            pl.semaphore_signal(
                barrier,
                inc=1,
                device_id=(ring(px, dx, count), ring(py, dy, count)),
                device_id_type=MESH,
            )
    lines_of_atoms, planes_of_atoms, run = mesh_stage(
        outs[0], fill_ref, *near[8:], *outs[1:], *mesh_scratch
    )

    def first_idle():
        for load in loads[8:]:
            load.wait()
        lines_of_atoms()

    for load in loads[:8]:
        load.wait()
    message_stage(
        lambda: pl.semaphore_wait(barrier, 34),
        (first_idle, planes_of_atoms),
        *message_in,
        outs[0],
        *message_scratch,
    )
    run()


def hand_on(*refs):
    for source, target in zip(refs[:3], refs[3:], strict=True):
        target[...] = source[...]


def shards(
    node_feats,
    radial,
    neighbours,
    nbr_count,
    domain_count,
    base_cells,
    spline_weights,
    w_proj,
    w_radial,
    w_mix,
    w_charge,
    green_kernel,
):
    vmem = pl.BlockSpec(memory_space=pltpu.VMEM)
    bf16, f32 = jnp.bfloat16, jnp.float32
    far = [
        node_feats,
        neighbours,
        nbr_count.reshape(1, 1024),
        radial.reshape(8 * K, 1024),
        w_proj,
        w_radial,
        w_mix,
        w_charge.reshape(1, 128),
        base_cells,
        spline_weights,
        jnp.transpose(green_kernel, (1, 2, 0)),
        *(jnp.asarray(table) for table in mesh_tables()),
    ]
    charges, atom_potential, potential = pl.pallas_call(
        step_kernel,
        out_shape=(
            jax.ShapeDtypeStruct((1, 1024), f32),
            jax.ShapeDtypeStruct((1, 1024), f32),
            jax.ShapeDtypeStruct((16, 16, 256), f32),
        ),
        in_specs=[pl.BlockSpec(memory_space=pltpu.HBM)] * 17
        + [pl.BlockSpec(memory_space=pltpu.SMEM)],
        out_specs=(vmem, vmem, vmem),
        scratch_shapes=[
            *(pltpu.VMEM(array.shape, array.dtype) for array in far),
            pltpu.SemaphoreType.DMA((17,)),
            pltpu.VMEM((128, 1024), f32),
            pltpu.VMEM((128, 1024), bf16),
            pltpu.VMEM((L, 256, 128), bf16),
            pltpu.VMEM((L, 512, 128), bf16),
            pltpu.VMEM((128, 640), bf16),
            pltpu.VMEM((128, 512), bf16),
            pltpu.VMEM((K, 8, 128), f32),
            pltpu.VMEM((K * 128, 8 * K), bf16),
            pltpu.VMEM((128, 256), f32),
            pltpu.SemaphoreType.DMA((L, 8)),
            pltpu.SemaphoreType.DMA((L, 8)),
            pltpu.VMEM((480, 1024), f32),
            pltpu.VMEM((256, 1024), bf16),
            pltpu.VMEM((256, 1024), bf16),
            *[pltpu.VMEM((16, 4, 16, 128), bf16)] * 2,
            *[pltpu.VMEM((16, 5, 16, 128), bf16)] * 4,
            *[pltpu.VMEM((16, 4, 16, 128), bf16)] * 2,
            pltpu.VMEM((2, 16, 256), f32),
            pltpu.VMEM((8, 256), f32),
            pltpu.VMEM((256, 128), f32),
            pltpu.VMEM((16, 256), f32),
            pltpu.VMEM((16, 256), f32),
            pltpu.SemaphoreType.DMA((9, 16)),
            pltpu.SemaphoreType.DMA((9, 16)),
        ],
        compiler_params=pltpu.CompilerParams(
            collective_id=0, has_side_effects=True, vmem_limit_bytes=56 * 1024 * 1024
        ),
        name="potential_step",
    )(
        *far,
        domain_count,
    )
    results = (charges, atom_potential, potential)
    charges, atom_potential, potential = pl.pallas_call(
        hand_on,
        out_shape=tuple(jax.ShapeDtypeStruct(array.shape, f32) for array in results),
        in_specs=[vmem] * 3,
        out_specs=[vmem] * 3,
        name="hand_on",
    )(*results)
    return (charges.reshape(1024), atom_potential.reshape(1024), potential)


def solution(mesh):
    return jax.shard_map(
        shards,
        mesh=mesh,
        in_specs=(
            P(("gx", "gy"), None),
            P(None, None, ("gx", "gy")),
            P(None, ("gx", "gy")),
            P(("gx", "gy")),
            P(("gx", "gy")),
            P(None, ("gx", "gy")),
            P(None, None, ("gx", "gy")),
            P(),
            P(),
            P(),
            P(),
            P(None, "gx", "gy"),
        ),
        out_specs=(P(("gx", "gy")), P(("gx", "gy")), P("gx", "gy", None)),
        check_vma=False,
    )
```

```python
import math

import jax
import jax.numpy as jnp
import ml_dtypes
import numpy as np
from jax import lax
from jax.experimental import pallas as pl
from jax.experimental.pallas import tpu as pltpu
from jax.sharding import PartitionSpec as P

K = 32
L = 2


MESH = pl.DeviceIdType.MESH
TN = (((0,), (0,)), ((), ()))
NT = (((1,), (1,)), ((), ()))
NN = (((1,), (0,)), ((), ()))


def dot(a, b, dims=NN):
    return lax.dot_general(a, b, dims, preferred_element_type=jnp.float32)


def ring(index, step, count):
    return lax.rem(index + step + count, count)


def message_stage(
    enter,
    idle,
    feats_ref,
    radial_ref,
    nbr_ref,
    count_ref,
    fill_ref,
    proj_ref,
    filt_ref,
    mix_ref,
    charge_w_ref,
    charges_ref,
    state,
    table,
    rows_out,
    rows_in,
    head_a,
    head_b,
    pick,
    filt_k,
    total,
    send_sem,
    recv_sem,
):
    px, py = lax.axis_index("gx"), lax.axis_index("gy")
    num_x = num_y = 16
    peers = [(dx, dy) for dx in (-1, 0, 1) for dy in (-1, 0, 1) if (dx, dy) != (0, 0)]
    code = nbr_ref[...]
    direction, slot = code // 1024, code % 1024
    lane = lax.broadcasted_iota(jnp.int32, (K, 1024), 1)
    live = lax.broadcasted_iota(jnp.int32, (K, 1024), 0) < count_ref[...]
    block = lane // 128
    near = slot - jnp.maximum(block - 1, 0) * 128
    far = jnp.where(
        direction < 3,
        192 + direction * 64 + slot,
        jnp.where(
            direction > 5,
            64 + direction * 64 + slot,
            jnp.where(direction == 3, 192 + slot, 320 + slot),
        ),
    )
    named = jnp.where(live, jnp.where(direction == 4, near, far), -8192).astype(jnp.float32)
    for b in range(8):
        pick[:, b, :] = named[:, b * 128 : (b + 1) * 128]

    state[...] = jnp.transpose(feats_ref[...].astype(jnp.float32))
    row_id = lax.broadcasted_iota(jnp.int32, (128, 128), 0).astype(jnp.bfloat16)
    one, zero = jnp.ones((128, 128), jnp.bfloat16), jnp.zeros((128, 128), jnp.bfloat16)
    basis_k = lax.broadcasted_iota(jnp.int32, (128, 8 * K), 1) % K

    def onehot(k, begin, groups):
        row = pick[k, begin // 128 : begin // 128 + 1, :]
        parts = [
            jnp.where(row_id == jnp.broadcast_to((row - 128.0 * g).astype(jnp.bfloat16), (128, 128)), one, zero)
            for g in range(groups)
        ]
        return jnp.concatenate(parts, axis=0)

    def messages(group, tables):
        begin = group * 256
        radial = radial_ref[:, begin : begin + 256]
        total[...] = jnp.zeros_like(total)

        for k in range(0, K, 2):
            filters = dot(filt_k[k * 128 : k * 128 + 256, :], radial)
            for half, (source, groups) in enumerate(tables):
                at = begin + 128 * half
                hot = jnp.concatenate([onehot(k, at, groups), onehot(k + 1, at, groups)], axis=1)
                got = dot(source(), hot)
                lanes = slice(128 * half, 128 * half + 128)
                total[:, lanes] += (
                    got[:, :128] * filters[:128, lanes] + got[:, 128:] * filters[128:, lanes]
                )
        return (total[...] * (1.0 / math.sqrt(K))).astype(jnp.bfloat16)

    for layer in range(L):
        spread = jnp.concatenate(
            [jnp.broadcast_to(filt_ref[layer, b : b + 1], (K, 128)) for b in range(8)], axis=0
        )
        spread = jnp.transpose(spread.astype(jnp.float32))
        for k in range(K):
            filt_k[k * 128 : (k + 1) * 128, :] = jnp.where(basis_k == k, spread, 0.0).astype(jnp.bfloat16)
        proj = proj_ref[layer]
        first = dot(proj, state[:, :256].astype(jnp.bfloat16), TN).astype(jnp.bfloat16)
        rows_out[layer] = jnp.transpose(first.astype(jnp.float32)).astype(jnp.bfloat16)
        if layer == 0:
            enter()
        copies = []
        for dx, dy in peers:
            if dx == 1:
                band, land = 1, 1 - dy
            elif dx == -1:
                band, land = 0, 4 - dy
            elif dy == 1:
                band, land = 3, 6
            else:
                band, land = 2, 7
            copies.append(
                pltpu.make_async_remote_copy(
                    src_ref=rows_out.at[layer, pl.ds(band * 64, 64)],
                    dst_ref=rows_in.at[layer, pl.ds(land * 64, 64)],
                    send_sem=send_sem.at[layer, land],
                    recv_sem=recv_sem.at[layer, land],
                    device_id=(ring(px, dx, num_x), ring(py, dy, num_y)),
                    device_id_type=MESH,
                )
            )
            copies[-1].start()
        table[:, :256] = first
        table[:, 256:] = dot(proj, state[:, 256:].astype(jnp.bfloat16), TN).astype(jnp.bfloat16)

        def update(group, tables):
            begin = group * 256
            u = messages(group, tables)
            mixed = dot(mix_ref[layer], u, TN)
            lanes = slice(begin, begin + 256)
            state[:, lanes] = (
                (state[:, lanes] + mixed / (1.0 + jnp.exp(-mixed))).astype(jnp.bfloat16).astype(jnp.float32)
            )

        def window(block):
            low = max(block - 1, 0) * 128
            high = min(block + 2, 8) * 128
            return (lambda: table[:, low:high]), (high - low) // 128

        for group in (1, 2, 3):
            update(group, [window(2 * group), window(2 * group + 1)])
        idle[layer]()
        for copy in copies:
            copy.wait()
        far_rows = jnp.transpose(rows_in[layer].astype(jnp.float32)).astype(jnp.bfloat16)
        head_a[:, :256] = table[:, :256]
        head_a[:, 256:] = far_rows[:, :384]
        head_b[:, :384] = table[:, :384]
        head_b[:, 384:] = far_rows[:, 384:]
        update(0, [((lambda: head_a[...]), 5), ((lambda: head_b[...]), 4)])
    charge = dot(jnp.broadcast_to(charge_w_ref[...], (8, 128)), state[...].astype(jnp.bfloat16))[0:1]
    inside = lax.broadcasted_iota(jnp.int32, (1, 1024), 1) < fill_ref[0]
    charges_ref[...] = jnp.where(inside, charge, 0.0)


def split(values):
    high = values.astype(jnp.bfloat16)
    return high, (values - high.astype(jnp.float32)).astype(jnp.bfloat16)


def np_split(values):
    high = values.astype(ml_dtypes.bfloat16)
    return high, (values - high.astype(np.float64)).astype(ml_dtypes.bfloat16)


def mesh_tables():
    ids = np.arange(256)
    angles = 2.0 * np.pi * (ids[:, None] * ids[None, :] % 256) / 256
    waves = np.concatenate([np.cos(angles), np.sin(angles)], axis=0)
    column, slot = np.arange(16)[:, None], np.arange(8)[None, :]
    kz = (16 * column + slot + (column >= 8)).reshape(128)
    turn = 2.0 * np.pi * (kz[:, None] * ids[None, :] % 256) / 256
    ahead = np.stack([np.cos(turn), -np.sin(turn)])
    back = 2.0 * ahead
    ahead[0, 0], ahead[1, 0] = 1.0, 1.0 - 2.0 * (ids % 2)
    back[0, 0], back[1, 0] = ahead[0, 0], ahead[1, 0]
    back = back / 256.0**3
    return (
        *np_split(waves),
        *np_split(ahead.reshape(256, 256)),
        *np_split(back.reshape(256, 256)),
    )


def regroup(parts):
    group = lax.broadcasted_iota(jnp.int32, parts[0].shape, 1) // 16
    parts = list(parts)
    for step in (1, 2, 4):
        low = (group & step) == 0
        for i in range(8):
            if i & step == 0:
                a, b = parts[i], parts[i | step]
                parts[i] = jnp.where(low, a, pltpu.roll(b, 16 * step, 1))
                parts[i | step] = jnp.where(low, pltpu.roll(a, 128 - 16 * step, 1), b)
    return parts


def swap_groups(values):
    row = lax.broadcasted_iota(jnp.int32, values.shape, 1)
    group = lax.broadcasted_iota(jnp.int32, values.shape, 2) // 16
    for step in (1, 2, 4):
        row_high, group_high = (row & step) != 0, (group & step) != 0
        if step == 4:
            moved = pltpu.roll(pltpu.roll(values, 4, 1), 64, 2)
        else:
            up = pltpu.roll(pltpu.roll(values, 8 - step, 1), 16 * step, 2)
            down = pltpu.roll(pltpu.roll(values, step, 1), 128 - 16 * step, 2)
            moved = jnp.where(row_high, down, up)
        values = jnp.where(row_high == group_high, values, moved)
    return values


def turned(values, step):
    return jnp.concatenate([values[step:], values[:step]], axis=0)


def fold_edges(edge):
    before, after = turned(edge, -1), turned(edge, 1)
    row = lax.broadcasted_iota(jnp.int32, edge.shape, 1)
    return [
        jnp.concatenate(
            [
                jnp.where(row < 2, pltpu.roll(before, step, 1), 0.0),
                jnp.where(row >= 6, pltpu.roll(after, step, 1), 0.0),
            ],
            axis=1,
        )
        for step in (6, 2)
    ]


def edges_of(real, imag):
    row = lax.broadcasted_iota(jnp.int32, (16, 8, 128), 1)
    ends = [
        pltpu.roll(part, step, 1)
        for values, step in ((real, 2), (imag, 6))
        for part in (turned(values, -1)[:, 8:], turned(values, 1)[:, :8])
    ]
    return jnp.where(
        row < 2, ends[0], jnp.where(row < 4, ends[1], jnp.where(row < 6, ends[2], ends[3]))
    )


def tile(low, high=None):
    high = jnp.zeros_like(low) if high is None else high
    return jnp.concatenate([low, high], axis=low.ndim - 2).astype(jnp.bfloat16)


def profile(cells, base, weights):
    total = jnp.zeros(cells.shape, jnp.float32)
    for offset in range(4):
        total = total + jnp.where(cells == base[offset], weights[offset], 0.0)
    return total


def mesh_stage(
    charges_ref,
    fill_ref,
    base_ref,
    spline_ref,
    green_ref,
    wave_h,
    wave_l,
    ahead_h,
    ahead_l,
    back_h,
    back_l,
    atom_ref,
    grid_ref,
    plane,
    prof_h,
    prof_l,
    z_out,
    z_in,
    y_out,
    y_in,
    x_out,
    x_in,
    v_out,
    v_in,
    shared,
    shared_edge,
    green,
    green_out,
    green_in,
    send_sem,
    recv_sem,
):
    count = 16
    px, py = lax.axis_index("gx"), lax.axis_index("gy")
    def remote(source, target, stage, index, where):
        return pltpu.make_async_remote_copy(
            src_ref=source,
            dst_ref=target,
            send_sem=send_sem.at[stage, index],
            recv_sem=recv_sem.at[stage, index],
            device_id=where,
            device_id_type=MESH,
        )

    def exchange(make):
        def start(d, carry):
            make(lax.rem(d + 3, count - 1) + 1).start()
            return carry

        lax.fori_loop(1, count, start, 0)

    def arrive(make):
        def wait(d, carry):
            make(d).wait()
            return carry

        lax.fori_loop(1, count, wait, 0)

    def column_copy(out, into, stage):
        def make(d):
            to = ring(py, d, count)
            return remote(out.at[to], into.at[py], stage, d, (px, to))

        return make

    def row_copy(out, into, stage, layers):
        def make(d):
            to = ring(px, d, count)
            return remote(out.at[to, layers], into.at[px, layers], stage, d, (to, py))

        return make

    main, extra = pl.ds(0, 3), pl.ds(3, 2)

    def green_copy():
        return remote(green_out, green_in, 8, 0, (px, 0))

    def rows(dim):
        base = base_ref[dim : dim + 1, :]
        cells = [base + offset for offset in range(4)]
        if dim == 2:
            cells = [jnp.where(c >= 256, c - 256, c) for c in cells]
        return cells, [spline_ref[dim, o : o + 1, :] for o in range(4)]

    def lines_of_atoms():
        z_cells = lax.broadcasted_iota(jnp.int32, (256, 1024), 0)
        high, low = split(profile(z_cells, *rows(2)))
        prof_h[...] = high
        prof_l[...] = low
        slots = [green_ref[:, i, :] for i in range(9)]
        green_out[...] = slots[0]
        picked = [jnp.where(py < 8, slots[i], slots[i + 1]) for i in range(8)]
        green[...] = jnp.transpose(jnp.concatenate(picked, axis=0))

    def planes_of_atoms():
        sixteen = lax.broadcasted_iota(jnp.int32, (16, 1024), 0)
        eight = lax.broadcasted_iota(jnp.int32, (8, 1024), 0)
        edge = jnp.where(eight < 2, eight, eight + 16)
        in_x, in_y = (profile(sixteen + 2, *rows(dim)) for dim in (0, 1))
        edge_x, edge_y = (profile(edge, *rows(dim)) for dim in (0, 1))
        for y in range(16):
            plane[16 * y : 16 * y + 16, :] = in_y[y : y + 1, :] * in_x
        for y in range(16):
            plane[256 + 8 * y : 264 + 8 * y, :] = in_y[y : y + 1, :] * edge_x
        for i in range(4):
            plane[384 + 16 * i : 400 + 16 * i, :] = edge_y[i : i + 1, :] * in_x
            plane[448 + 8 * i : 456 + 8 * i, :] = edge_y[i : i + 1, :] * edge_x

    def run():
        high, low = split(plane[...] * charges_ref[...])
        spread = dot(high, prof_h[...], NT) + dot(low, prof_h[...], NT) + dot(high, prof_l[...], NT)
        edges = spread[256:]
        edges = [
            tile(edges[:128].reshape(16, 8, 256)).reshape(256, 256),
            tile(edges[128:192]),
            tile(tile(edges[192:].reshape(4, 8, 256)).reshape(64, 256)),
        ]
        edges = jnp.concatenate(edges, axis=0)
        high, low = split(spread[:256])

        lines = dot(ahead_h[...], high, NT) + dot(ahead_l[...], high, NT) + dot(ahead_h[...], low, NT)
        halves = [
            swap_groups(lines[:, 128 * half : 128 * half + 128].reshape(32, 8, 128)) for half in (0, 1)
        ]
        halves = jnp.concatenate(halves, axis=1).astype(jnp.bfloat16)
        z_out[:, 0] = halves[:16]
        z_out[:, 1] = halves[16:]
        lines = dot(ahead_h[...], edges, NT) + dot(ahead_l[...], edges, NT)
        real, imag = lines[:128], lines[128:]
        sides = real[:, :256] + pltpu.roll(imag[:, :256], 4, 1)
        ends = real[:, 256:384] + pltpu.roll(imag[:, 256:384], 64, 1)
        corners = real[:, 384:] + pltpu.roll(imag[:, 384:], 4, 1)
        pieces = [
            swap_groups(part.reshape(16, 8, 128))
            for part in (sides[:, :128], sides[:, 128:], ends, corners)
        ]
        z_out[:, 2] = tile(pieces[0], pieces[1])
        z_out[:, 3] = tile(pieces[2], pieces[3])
        make = column_copy(z_out, z_in, 2)
        exchange(make)

        @pl.when(py == 8)
        def _():
            green_copy().start()

        z_in[pl.ds(py, 1)] = z_out[pl.ds(py, 1)]
        arrive(make)

        cos_h, sin_h = wave_h[:256], wave_h[256:]
        cos_l, sin_l = wave_l[:256], wave_l[256:]
        ends = z_in[:, 3].astype(jnp.float32)
        adds = [*fold_edges(ends[:, :8]), fold_edges(ends[:, 8:])[0]]
        both = jnp.concatenate(
            [(z_in[:, i].astype(jnp.float32) + adds[i]).reshape(256, 128) for i in range(3)], axis=1
        )
        both = jnp.transpose(both).astype(jnp.bfloat16)
        c = dot(both, cos_h) + dot(both, cos_l)
        s = dot(both, sin_h) + dot(both, sin_l)
        apart = (lax.broadcasted_iota(jnp.int32, (128, 256), 0) < 16) & (py == 0)
        real = c[:128] + jnp.where(apart, 0.0, s[128:256])
        imag = jnp.where(apart, 0.0, c[128:256]) - s[:128]

        c_edge, s_edge = (v[256:].reshape(8, 16, 256)[:, :8] for v in (c, s))
        c_swap, s_swap = pltpu.roll(c_edge, 4, 1), pltpu.roll(s_edge, 4, 1)
        top = lax.broadcasted_iota(jnp.int32, (8, 8, 256), 1) < 4
        apart = (lax.broadcasted_iota(jnp.int32, (8, 8, 256), 0) == 0) & (py == 0)
        edge = jnp.where(
            top,
            c_edge + jnp.where(apart, 0.0, s_swap),
            jnp.where(apart, 0.0, c_edge) - s_swap,
        )

        def to_slots(values, layer):
            for half in (0, 1):
                lanes = slice(128 * half, 128 * half + 128)
                done = regroup([v[:, lanes] for v in values])
                for i in range(8):
                    whole = done[i].shape[0] == 16
                    y_out[8 * half + i, layer] = done[i].astype(jnp.bfloat16) if whole else tile(done[i])

        to_slots([real[16 * i : 16 * i + 16] for i in range(8)], 0)
        to_slots([imag[16 * i : 16 * i + 16] for i in range(8)], 1)
        to_slots([edge[i] for i in range(8)], 2)
        make = row_copy(y_out, y_in, 3, main)
        exchange(make)
        y_in[pl.ds(px, 1), 0:3] = y_out[pl.ds(px, 1), 0:3]

        @pl.when(py == 0)
        def _():
            blank = jnp.zeros((16, 256), jnp.float32)
            to_slots([c[128:144], -s[128:144]] + [blank] * 6, 3)
            to_slots([jnp.where(top[0], c_swap[0], -s_edge[0])] + [blank[:8]] * 7, 4)
            exchange(row_copy(y_out, y_in, 4, extra))
            y_in[pl.ds(px, 1), 3:5] = y_out[pl.ds(px, 1), 3:5]

        arrive(make)

        def forward_x(values):
            return dot(cos_h, values) + dot(cos_l, values), dot(sin_h, values) + dot(sin_l, values)

        def inverse_x(values):
            high, low = split(values)
            return (
                dot(cos_h, high) + dot(cos_l, high) + dot(cos_h, low),
                dot(sin_h, high) + dot(sin_l, high) + dot(sin_h, low),
            )

        adds = fold_edges(y_in[:, 2].astype(jnp.float32)[:, :8])
        c, s = forward_x(
            jnp.concatenate(
                [(y_in[:, i].astype(jnp.float32) + adds[i]).reshape(256, 128) for i in range(2)], axis=1
            ).astype(jnp.bfloat16)
        )
        real = (c[:, :128] + s[:, 128:]) * green[...]
        imag = (c[:, 128:] - s[:, :128]) * green[...]
        c, s = inverse_x(jnp.concatenate([real, imag], axis=1))
        real = (c[:, :128] - s[:, 128:]).reshape(16, 16, 128)
        imag = (c[:, 128:] + s[:, :128]).reshape(16, 16, 128)
        x_out[:, 0] = real.astype(jnp.bfloat16)
        x_out[:, 1] = imag.astype(jnp.bfloat16)
        x_out[:, 2] = tile(edges_of(real, imag))
        make = row_copy(x_out, x_in, 5, main)
        exchange(make)
        x_in[pl.ds(px, 1), 0:3] = x_out[pl.ds(px, 1), 0:3]

        @pl.when(py == 0)
        def _():
            arrive(row_copy(y_out, y_in, 4, extra))
            green_copy().wait_recv()
            first = lax.broadcasted_iota(jnp.int32, (256, 128), 1) < 16
            adds = fold_edges(y_in[:, 4].astype(jnp.float32)[:, :8])
            last = y_in[:, 3].astype(jnp.float32) + adds[0] + pltpu.roll(adds[1], 16, 2)
            c, s = forward_x(last.reshape(256, 128).astype(jnp.bfloat16))
            kernel = jnp.transpose(
                jnp.concatenate([green_in[...], jnp.zeros((112, 256), jnp.float32)], axis=0)
            )
            real = (c + pltpu.roll(s, 112, 1)) * kernel
            imag = (pltpu.roll(c, 112, 1) - s) * kernel
            c, s = inverse_x(real + pltpu.roll(imag, 16, 1))
            real = jnp.where(first, c - pltpu.roll(s, 112, 1), 0.0)
            imag = jnp.where(first, pltpu.roll(c, 112, 1) + s, 0.0)
            x_out[:, 3] = (real + pltpu.roll(imag, 16, 1)).astype(jnp.bfloat16).reshape(16, 16, 128)
            x_out[:, 4] = tile(edges_of(real.reshape(16, 16, 128), imag.reshape(16, 16, 128)))
            back_copy = row_copy(x_out, x_in, 6, extra)
            exchange(back_copy)
            x_in[pl.ds(px, 1), 3:5] = x_out[pl.ds(px, 1), 3:5]

        @pl.when(py == 8)
        def _():
            green_copy().wait_send()

        arrive(make)

        def to_rows(layer, count=16):
            halves = [
                regroup([x_in[8 * half + i, layer].astype(jnp.float32)[:count] for i in range(8)])
                for half in (0, 1)
            ]
            return [jnp.concatenate([halves[0][i], halves[1][i]], axis=1) for i in range(8)]

        real, imag, edge = to_rows(0), to_rows(1), to_rows(2, 8)
        shared[0] = real[0]
        shared[1] = imag[0]
        shared_edge[...] = edge[0]

        @pl.when(py == 0)
        def _():
            arrive(row_copy(x_out, x_in, 6, extra))
            last = to_rows(3)
            shared[0] = -last[1]
            shared[1] = last[0]
            last = pltpu.roll(to_rows(4, 8)[0], 4, 0)
            shared_edge[...] = jnp.where(top[0], -last, last)

        a = jnp.concatenate(real, axis=0).astype(jnp.bfloat16)
        b = jnp.concatenate(imag, axis=0).astype(jnp.bfloat16)
        a_too = jnp.concatenate([shared[0], *real[1:]], axis=0).astype(jnp.bfloat16)
        b_too = jnp.concatenate([shared[1], *imag[1:]], axis=0).astype(jnp.bfloat16)
        real = dot(cos_h, a, NT) + dot(cos_l, a, NT) - dot(sin_h, b, NT) - dot(sin_l, b, NT)
        imag = dot(cos_h, b_too, NT) + dot(cos_l, b_too, NT) + dot(sin_h, a_too, NT) + dot(sin_l, a_too, NT)
        sides = []
        for first in (edge[0], shared_edge[...]):
            rows = jnp.concatenate([tile(v) for v in [first, *edge[1:]]], axis=0)
            sides.append(
                (
                    dot(cos_h, rows, NT) + dot(cos_l, rows, NT),
                    dot(sin_h, rows, NT) + dot(sin_l, rows, NT),
                )
            )
        within = lax.broadcasted_iota(jnp.int32, (256, 128), 1) % 16
        sides = jnp.where(
            within < 4,
            sides[0][0] - pltpu.roll(sides[0][1], 124, 1),
            sides[1][0] + pltpu.roll(sides[1][1], 4, 1),
        )
        sides = jnp.where(within < 8, sides, 0.0).reshape(16, 16, 128)
        real, imag = real.reshape(16, 16, 128), imag.reshape(16, 16, 128)
        v_out[:, 0] = real.astype(jnp.bfloat16)
        v_out[:, 1] = imag.astype(jnp.bfloat16)
        v_out[:, 2] = sides.astype(jnp.bfloat16)
        v_out[:, 3] = tile(edges_of(real, imag), edges_of(sides, sides))
        make = column_copy(v_out, v_in, 7)
        exchange(make)
        v_in[pl.ds(py, 1)] = v_out[pl.ds(py, 1)]
        arrive(make)

        def to_lines(values):
            return swap_groups(values).reshape(-1, 128)

        got = jnp.concatenate([v_in[:, 0], v_in[:, 1]], axis=0).astype(jnp.float32)
        lines = jnp.concatenate([to_lines(got[:, :8]), to_lines(got[:, 8:])], axis=1).astype(jnp.bfloat16)
        grid = dot(lines, back_h[...], TN) + dot(lines, back_l[...], TN)
        for y in range(16):
            grid_ref[:, y, :] = grid[16 * y : 16 * y + 16]
        got = jnp.concatenate([v_in[:, 2], v_in[:, 3]], axis=0).astype(jnp.float32)
        sides = jnp.concatenate([to_lines(got[:16, :8]), to_lines(got[:16, 8:])], axis=1)
        ends, corners = to_lines(got[16:, :8]), to_lines(got[16:, 8:])
        lines = jnp.concatenate(
            [
                jnp.concatenate([sides, ends, corners], axis=1),
                jnp.concatenate(
                    [pltpu.roll(sides, 252, 1), pltpu.roll(ends, 64, 1), pltpu.roll(corners, 124, 1)],
                    axis=1,
                ),
            ],
            axis=0,
        ).astype(jnp.bfloat16)
        edges = dot(lines, back_h[...], TN) + dot(lines, back_l[...], TN)

        values = jnp.concatenate(
            [
                grid,
                edges[:256].reshape(16, 16, 256)[:, :8].reshape(128, 256),
                edges[256:320],
                edges[384:448].reshape(4, 16, 256)[:, :8].reshape(32, 256),
            ],
            axis=0,
        )
        high, low = split(values)
        sampled = dot(high, prof_h[...]) + dot(low, prof_h[...]) + dot(high, prof_l[...])
        total = jnp.sum(sampled * plane[...], axis=0, keepdims=True)
        inside = lax.broadcasted_iota(jnp.int32, (1, 1024), 1) < fill_ref[0]
        atom_ref[...] = jnp.where(inside, total, 0.0)

    return lines_of_atoms, planes_of_atoms, run


def step_kernel(*refs):
    far, fill_ref, outs = refs[:17], refs[17], refs[18:21]
    near, load_sem, refs = refs[21:38], refs[38], refs[39:]
    message_scratch, mesh_scratch = refs[:11], refs[11:]
    loads = [
        pltpu.make_async_copy(source, target, load_sem.at[i])
        for i, (source, target) in enumerate(zip(far, near, strict=True))
    ]
    for load in loads:
        load.start()
    feats_ref, nbr_ref, count_ref, radial_ref, *weights, charge_w_ref = near[:8]
    message_in = (feats_ref, radial_ref, nbr_ref, count_ref, fill_ref, *weights, charge_w_ref)
    count = 16
    px, py = lax.axis_index("gx"), lax.axis_index("gy")
    barrier = pltpu.get_barrier_semaphore()

    def greet(d, carry):
        for where in ((ring(px, d, count), py), (px, ring(py, d, count))):
            pl.semaphore_signal(barrier, inc=1, device_id=where, device_id_type=MESH)
        return carry

    lax.fori_loop(1, count, greet, 0)
    for dx in (-1, 1):
        for dy in (-1, 1):
            pl.semaphore_signal(
                barrier,
                inc=1,
                device_id=(ring(px, dx, count), ring(py, dy, count)),
                device_id_type=MESH,
            )
    lines_of_atoms, planes_of_atoms, run = mesh_stage(
        outs[0], fill_ref, *near[8:], *outs[1:], *mesh_scratch
    )

    def first_idle():
        for load in loads[8:]:
            load.wait()
        lines_of_atoms()

    for load in loads[:8]:
        load.wait()
    message_stage(
        lambda: pl.semaphore_wait(barrier, 34),
        (first_idle, planes_of_atoms),
        *message_in,
        outs[0],
        *message_scratch,
    )
    run()


def hand_on(*refs):
    for source, target in zip(refs[:3], refs[3:], strict=True):
        target[...] = source[...]


def shards(
    node_feats,
    radial,
    neighbours,
    nbr_count,
    domain_count,
    base_cells,
    spline_weights,
    w_proj,
    w_radial,
    w_mix,
    w_charge,
    green_kernel,
):
    vmem = pl.BlockSpec(memory_space=pltpu.VMEM)
    bf16, f32 = jnp.bfloat16, jnp.float32
    far = [
        node_feats,
        neighbours,
        nbr_count.reshape(1, 1024),
        radial.reshape(8 * K, 1024),
        w_proj,
        w_radial,
        w_mix,
        w_charge.reshape(1, 128),
        base_cells,
        spline_weights,
        jnp.transpose(green_kernel, (1, 2, 0)),
        *(jnp.asarray(table) for table in mesh_tables()),
    ]
    charges, atom_potential, potential = pl.pallas_call(
        step_kernel,
        out_shape=(
            jax.ShapeDtypeStruct((1, 1024), f32),
            jax.ShapeDtypeStruct((1, 1024), f32),
            jax.ShapeDtypeStruct((16, 16, 256), f32),
        ),
        in_specs=[pl.BlockSpec(memory_space=pltpu.HBM)] * 17
        + [pl.BlockSpec(memory_space=pltpu.SMEM)],
        out_specs=(vmem, vmem, vmem),
        scratch_shapes=[
            *(pltpu.VMEM(array.shape, array.dtype) for array in far),
            pltpu.SemaphoreType.DMA((17,)),
            pltpu.VMEM((128, 1024), f32),
            pltpu.VMEM((128, 1024), bf16),
            pltpu.VMEM((L, 256, 128), bf16),
            pltpu.VMEM((L, 512, 128), bf16),
            pltpu.VMEM((128, 640), bf16),
            pltpu.VMEM((128, 512), bf16),
            pltpu.VMEM((K, 8, 128), f32),
            pltpu.VMEM((K * 128, 8 * K), bf16),
            pltpu.VMEM((128, 256), f32),
            pltpu.SemaphoreType.DMA((L, 8)),
            pltpu.SemaphoreType.DMA((L, 8)),
            pltpu.VMEM((480, 1024), f32),
            pltpu.VMEM((256, 1024), bf16),
            pltpu.VMEM((256, 1024), bf16),
            *[pltpu.VMEM((16, 4, 16, 128), bf16)] * 2,
            *[pltpu.VMEM((16, 5, 16, 128), bf16)] * 4,
            *[pltpu.VMEM((16, 4, 16, 128), bf16)] * 2,
            pltpu.VMEM((2, 16, 256), f32),
            pltpu.VMEM((8, 256), f32),
            pltpu.VMEM((256, 128), f32),
            pltpu.VMEM((16, 256), f32),
            pltpu.VMEM((16, 256), f32),
            pltpu.SemaphoreType.DMA((9, 16)),
            pltpu.SemaphoreType.DMA((9, 16)),
        ],
        compiler_params=pltpu.CompilerParams(
            collective_id=0, has_side_effects=True, vmem_limit_bytes=56 * 1024 * 1024
        ),
        name="potential_step",
    )(
        *far,
        domain_count,
    )
    results = (charges, atom_potential, potential)
    charges, atom_potential, potential = pl.pallas_call(
        hand_on,
        out_shape=tuple(jax.ShapeDtypeStruct(array.shape, f32) for array in results),
        in_specs=[vmem] * 3,
        out_specs=[vmem] * 3,
        name="hand_on",
    )(*results)
    return (charges.reshape(1024), atom_potential.reshape(1024), potential)


def solution(mesh):
    return jax.shard_map(
        shards,
        mesh=mesh,
        in_specs=(
            P(("gx", "gy"), None),
            P(None, None, ("gx", "gy")),
            P(None, ("gx", "gy")),
            P(("gx", "gy")),
            P(("gx", "gy")),
            P(None, ("gx", "gy")),
            P(None, None, ("gx", "gy")),
            P(),
            P(),
            P(),
            P(),
            P(None, "gx", "gy"),
        ),
        out_specs=(P(("gx", "gy")), P(("gx", "gy")), P("gx", "gy", None)),
        check_vma=False,
    )
```
